128 devices in a mesh: node: 4 (over y), wide: 32 (over x, z, core).
Axes of the slice: x: 4, y: 4, z: 4, core: 2. Of those that a mesh axis runs over, the one named last changes fastest.
Arguments:
- features: bfloat16 [128, 128, 9216], P(('node', 'wide')), may hold values from -6 to 6
- cotangent: bfloat16 [128, 128, 9216], P(('node', 'wide')), may hold values from -6 to 6
- wet_fraction: float32 [128, 9216], P(('node', 'wide')), may hold values from 0 to 1, as said below
- slot_tile: int32 [128], replicated, may hold values from -1 to 255, as said below
- neighbours: int32 [256, 8], replicated, may hold values from -1 to 511, as said below
- kernel: float32 [49, 128], replicated, may hold values from -0.875 to 0.875
- norm_gain: float32 [128], replicated, may hold values from 0.5 to 1.5
- weight_in: bfloat16 [128, 512], replicated, may hold values from -0.5 to 0.5
- bias_in: float32 [512], replicated, may hold values from -3 to 3
- weight_out: bfloat16 [512, 128], replicated, may hold values from -0.25 to 0.25
- layer_scale: float32 [128], replicated, may hold values from 0.5 to 1.5
Outputs:
- updated: bfloat16 [128, 128, 9216], P(('node', 'wide'))
- grad_features: bfloat16 [128, 128, 9216], P(('node', 'wide'))
- grad_weight_in: float32 [128, 512], replicated
- grad_weight_out: float32 [512, 128], replicated
- grad_kernel: float32 [49, 128], replicated
The draws below stay inside these ranges and needn't reach their ends.
Inputs may be any that keep to these rules, and one draw needn't show every extreme that they name: `slot_tile`: slot (n * 32 + w) + j is slot j of node index n and wide index w; -1 marks an empty slot. Tile id = grid row 32 + grid column; a tile of grid column w is held only by slots of wide index w; every ocean tile is held by exactly one slot and land tiles by none; in some grid column every slot holds a tile. Row t lists the neighbours of tile t in the order N, S, W, E, NW, NE, SW, SE as 2 id + flip, or -1 where there is no ocean tile (all -1 for land tiles). Columns wrap, so neighbours lie in grid columns c - 1, c, c + 1 mod 32; the N neighbour of a tile in the top grid row is the top-row tile of grid column 31 - c with flip 1, the only entries with flip 1. The table is symmetric: B is the S (W, E, NW, NE, SW, SE) neighbour of A exactly when A is the N (E, W, SE, SW, NE, NW) neighbour of B, and flipped N neighbours are mutual. `wet_fraction`: zero in every cell of an empty slot.
All inputs are finite; a program needn't handle non-finite values.
Results may differ from the reference program's by a relative error of at most 0.0077.
Values may be sent and summed in bfloat16 or wider, within the bound.
A program may use at most 192 MiB of HBM per device.

```python
import math
import jax
import jax.numpy as jnp
from jax import lax

C = 128
HID = 512
TS = 96
TPD = 1
CELLS = 9216
SLOTS = 128
TNX = 32
TNY = 8
TILES = 256


def grid_layout(key):
    column_slots = TNY - 4
    middle_rows = TNY - 2
    full_column = jax.random.randint(jax.random.fold_in(key, 21), (), 0, TNX)
    column_keys = jax.random.split(jax.random.fold_in(key, 22), TNX)
    columns = jnp.arange(TNX, dtype=jnp.int32)

    def column_draw(column_key, column):
        key_rows, key_slots, key_count = jax.random.split(column_key, 3)
        row_rank = jnp.argsort(jax.random.permutation(key_rows, middle_rows))
        dropped = jax.random.randint(key_count, (), 0, 3)
        ocean_count = jnp.where(column == full_column, column_slots, column_slots - dropped)
        middle_wet = row_rank < ocean_count - 1
        ocean_rows = jnp.concatenate([jnp.zeros((1,), bool), middle_wet, jnp.ones((1,), bool)])
        rank_order = jnp.cumsum(ocean_rows.astype(jnp.int32)) - 1
        slot_perm = jax.random.permutation(key_slots, column_slots)
        position = jnp.take(slot_perm, jnp.maximum(rank_order, 0))
        return (ocean_rows, position)
    ocean_map, position = jax.vmap(column_draw)(column_keys, columns)
    ocean_map = ocean_map.T
    position = position.T
    row_ids = jnp.arange(TNY, dtype=jnp.int32)[:, None]
    col_ids = columns[None, :]
    node_of = position // TPD
    place_in = position % TPD
    slot_index = (node_of * TNX + col_ids) * TPD + place_in
    tile_ids = row_ids * TNX + col_ids
    slot_tile = jnp.full((SLOTS,), -1, jnp.int32).at[jnp.where(ocean_map, slot_index, SLOTS).reshape(-1)].set(tile_ids.reshape(-1), mode='drop')

    def near_entry(row_step, col_step, fold):
        near_row = row_ids + row_step
        near_col = (col_ids + col_step) % TNX
        inside = (near_row >= 0) & (near_row < TNY)
        clipped = jnp.clip(near_row, 0, TNY - 1)
        near_wet = ocean_map[clipped, near_col] & inside & ocean_map
        near_code = jnp.where(near_wet, 2 * (clipped * TNX + near_col), -1)
        if fold:
            mirror_col = TNX - 1 - col_ids
            across = (near_row == TNY) & ocean_map & ocean_map[TNY - 1][mirror_col]
            near_code = jnp.where(across, 2 * ((TNY - 1) * TNX + mirror_col) + 1, near_code)
        return near_code
    near_table = jnp.stack([near_entry(1, 0, True), near_entry(-1, 0, False), near_entry(0, -1, False), near_entry(0, 1, False), near_entry(1, -1, False), near_entry(1, 1, False), near_entry(-1, -1, False), near_entry(-1, 1, False)], axis=-1)
    return (slot_tile, near_table.reshape(TILES, 8).astype(jnp.int32))


def draw_slot_tile(key, part):
    slot_tile, near_table = grid_layout(key)
    return slot_tile


def draw_neighbours(key, part):
    slot_tile, near_table = grid_layout(key)
    return near_table


def draw_wet_fraction(key, part):
    slot_tile, near_table = grid_layout(key)
    key = jax.random.fold_in(key, 3)
    raw_wet = jax.random.uniform(key, (SLOTS, CELLS), jnp.float32, -0.25, 1.75)
    return jnp.clip(raw_wet, 0.0, 1.0) * (slot_tile >= 0).astype(jnp.float32)[:, None]


def level_of(own_key, dims, cuts, smallest, high):
    gain, own = 1.0, jax.random.fold_in(own_key, 6)
    for dim, shards_of in cuts:
        heights = jnp.exp(jax.random.uniform(jax.random.fold_in(own, dim), (shards_of,), jnp.float32, smallest / len(cuts), high / len(cuts)))
        gain = gain * jnp.repeat(heights, dims[dim] // shards_of).reshape([-1 if axis == dim else 1 for axis in range(len(dims))])
    return gain


def noise(stream_key, extent, deviation, limit, pieces=(), kind=jnp.bfloat16):
    loudness = level_of(stream_key, extent, pieces, -0.22, 0.18) if pieces else 1.0
    values = jax.random.normal(stream_key, extent, jnp.float32) * deviation * loudness
    return jnp.minimum(jnp.maximum(values, -limit), limit).astype(kind)


def setup_inputs(seed: int = 0) -> dict:
    keys = jax.random.split(jax.random.key(seed), 12)
    return {
        "features": noise(keys[0], (SLOTS, C, CELLS), 1.0, 6.0, ((0, 128),)),
        "cotangent": noise(keys[1], (SLOTS, C, CELLS), 1.0, 6.0, ((0, 128),)),
        "wet_fraction": draw_wet_fraction(jax.random.fold_in(keys[11], 71), 0),
        "slot_tile": draw_slot_tile(jax.random.fold_in(keys[11], 71), 0),
        "neighbours": draw_neighbours(jax.random.fold_in(keys[11], 71), 0),
        "kernel": noise(keys[5], (49, C), 49 ** -0.5, 0.875, (), jnp.float32),
        "norm_gain": jnp.clip(1.0 + 0.1 * jax.random.normal(keys[6], (C,), jnp.float32), 0.5, 1.5),
        "weight_in": noise(keys[7], (C, HID), C ** -0.5, 0.5),
        "bias_in": noise(keys[8], (HID,), 0.5, 3.0, (), jnp.float32),
        "weight_out": noise(keys[9], (HID, C), HID ** -0.5, 0.25),
        "layer_scale": jnp.clip(jax.random.uniform(keys[10], (C,), jnp.float32, 0.5, 1.5), 0.5, 1.5),
    }


EPS = 1e-06
GELU_COEF = 0.7978845608028654

def gelu_tanh(values):
    return 0.5 * values * (1.0 + jnp.tanh(GELU_COEF * (values + 0.044715 * values * values * values)))

def cell_metric(tile_ids):
    grid_row = jnp.maximum(tile_ids, 0) // TNX
    cell_row = jnp.arange(CELLS, dtype=jnp.int32) // TS
    global_row = grid_row[:, None] * TS + cell_row[None, :]
    latitude = -80.0 + 160.0 * (global_row.astype(jnp.float32) + 0.5) / float(TNY * TS)
    return jnp.cos(latitude * (math.pi / 180.0))

def rim_pack(tile_data):
    channels, tile_side = (tile_data.shape[0], tile_data.shape[1])
    return jnp.concatenate([tile_data[:, tile_side - 3:, :].reshape(channels, 3 * tile_side), tile_data[:, :3, :].reshape(channels, 3 * tile_side), tile_data[:, :, :3].reshape(channels, 3 * tile_side), tile_data[:, :, tile_side - 3:].reshape(channels, 3 * tile_side)], axis=1)

def flip_both(strip):
    return strip[:, ::-1, ::-1]

def assemble(tile_data, packs, mirrored, flip_north):
    channels, tile_side = (tile_data.shape[0], tile_data.shape[1])
    strip_len = 3 * tile_side
    north_rims = packs[:, :, 0:strip_len].reshape(8, channels, 3, tile_side)
    south_rims = packs[:, :, strip_len:2 * strip_len].reshape(8, channels, 3, tile_side)
    west_rims = packs[:, :, 2 * strip_len:3 * strip_len].reshape(8, channels, tile_side, 3)
    east_rims = packs[:, :, 3 * strip_len:].reshape(8, channels, tile_side, 3)
    north_piece = jnp.where(flip_north > 0, flip_both(mirrored.reshape(channels, 3, tile_side)), south_rims[0])
    bottom = jnp.concatenate([north_rims[6][:, :, tile_side - 3:], north_rims[1], north_rims[7][:, :, :3]], axis=2)
    middle = jnp.concatenate([east_rims[2], tile_data, west_rims[3]], axis=2)
    upper_band = jnp.concatenate([south_rims[4][:, :, tile_side - 3:], north_piece, south_rims[5][:, :, :3]], axis=2)
    return jnp.concatenate([bottom, middle, upper_band], axis=1)

def frame_pack(spread):
    channels, wide_side = (spread.shape[0], spread.shape[1])
    tile_side = wide_side - 6
    return jnp.concatenate([spread[:, tile_side + 3:, :].reshape(channels, 3 * wide_side), spread[:, :3, :].reshape(channels, 3 * wide_side), spread[:, 3:tile_side + 3, :3].reshape(channels, 3 * tile_side), spread[:, 3:tile_side + 3, tile_side + 3:].reshape(channels, 3 * tile_side)], axis=1).astype(jnp.bfloat16)

def receive(interior, packs, mirrored, flip_north):
    channels, tile_side = (interior.shape[0], interior.shape[1])
    wide_side = tile_side + 6
    band_len = 3 * wide_side
    strip_len = 3 * tile_side
    rest = tile_side - 3
    upper_bands = packs[:, :, :band_len].reshape(8, channels, 3, wide_side).astype(jnp.float32)
    lower_bands = packs[:, :, band_len:2 * band_len].reshape(8, channels, 3, wide_side).astype(jnp.float32)
    left_bands = packs[:, :, 2 * band_len:2 * band_len + strip_len].reshape(8, channels, tile_side, 3).astype(jnp.float32)
    right_bands = packs[:, :, 2 * band_len + strip_len:].reshape(8, channels, tile_side, 3).astype(jnp.float32)
    from_north = jnp.where(flip_north > 0, flip_both(mirrored.reshape(channels, 3, tile_side).astype(jnp.float32)), lower_bands[0][:, :, 3:tile_side + 3])
    top_rows = from_north + jnp.pad(lower_bands[4][:, :, tile_side + 3:], ((0, 0), (0, 0), (0, rest))) + jnp.pad(lower_bands[5][:, :, :3], ((0, 0), (0, 0), (rest, 0)))
    bottom_rows = upper_bands[1][:, :, 3:tile_side + 3] + jnp.pad(upper_bands[6][:, :, tile_side + 3:], ((0, 0), (0, 0), (0, rest))) + jnp.pad(upper_bands[7][:, :, :3], ((0, 0), (0, 0), (rest, 0)))
    return interior + jnp.pad(bottom_rows, ((0, 0), (0, rest), (0, 0))) + jnp.pad(top_rows, ((0, 0), (rest, 0), (0, 0))) + jnp.pad(right_bands[2], ((0, 0), (0, 0), (0, rest))) + jnp.pad(left_bands[3], ((0, 0), (0, 0), (rest, 0)))

def conv_forward(padded, kernel):
    total = jnp.zeros((C, TS, TS), jnp.float32)
    for row_off in range(7):
        for col_off in range(7):
            window = padded[:, row_off:row_off + TS, col_off:col_off + TS].astype(jnp.float32)
            total = total + kernel[7 * row_off + col_off][:, None, None] * window
    return total.reshape(C, CELLS)

def kernel_grad(padded, grad_source):
    grad_grid = grad_source.reshape(C, TS, TS)
    rows_out = []
    for row_off in range(7):
        for col_off in range(7):
            window = padded[:, row_off:row_off + TS, col_off:col_off + TS].astype(jnp.float32)
            rows_out.append(lax.optimization_barrier(jnp.sum(grad_grid * window, axis=(1, 2))))
    return jnp.stack(rows_out, axis=0)

def spread_back(grad_bf, kernel):
    grad_vals = grad_bf.reshape(C, TS, TS).astype(jnp.float32)
    spread = jnp.zeros((C, TS + 6, TS + 6), jnp.float32)
    for row_off in range(7):
        for col_off in range(7):
            spread = spread.at[:, row_off:row_off + TS, col_off:col_off + TS].add(kernel[7 * row_off + col_off][:, None, None] * grad_vals)
    return spread

def block_tile(padded, tile_x, tile_grad, wet_row, metric_row, kernel, norm_gain, weight_in, bias_in, weight_out, layer_scale):
    conv_out = conv_forward(padded, kernel) / metric_row[None, :]
    centred = conv_out - lax.optimization_barrier(jnp.mean(conv_out, axis=0, keepdims=True))
    inv_std = lax.rsqrt(lax.optimization_barrier(jnp.mean(centred * centred, axis=0, keepdims=True)) + EPS)
    normed = centred * inv_std
    normed_bf = (normed * norm_gain[:, None]).astype(jnp.bfloat16)
    hidden = jnp.dot(weight_in.T, normed_bf, preferred_element_type=jnp.float32) + bias_in[:, None]
    active, gelu_back = jax.vjp(gelu_tanh, hidden)
    active_bf = active.astype(jnp.bfloat16)
    mixed = jnp.dot(weight_out.T, active_bf, preferred_element_type=jnp.float32)
    mask_scale = wet_row[None, :] * layer_scale[:, None]
    updated = (tile_x.astype(jnp.float32) + mask_scale * mixed).astype(jnp.bfloat16)
    grad_mixed = (mask_scale * tile_grad.astype(jnp.float32)).astype(jnp.bfloat16)
    grad_w_out = jnp.dot(active_bf, grad_mixed.T, preferred_element_type=jnp.float32)
    grad_active = jnp.dot(weight_out, grad_mixed, preferred_element_type=jnp.float32)
    grad_hidden = gelu_back(grad_active)[0].astype(jnp.bfloat16)
    grad_w_in = jnp.dot(normed_bf, grad_hidden.T, preferred_element_type=jnp.float32)
    grad_normed = jnp.dot(weight_in, grad_hidden, preferred_element_type=jnp.float32) * norm_gain[:, None]
    grad_conv = inv_std * (grad_normed - lax.optimization_barrier(jnp.mean(grad_normed, axis=0, keepdims=True)) - normed * lax.optimization_barrier(jnp.mean(grad_normed * normed, axis=0, keepdims=True)))
    grad_source = grad_conv / metric_row[None, :]
    grad_kern = kernel_grad(padded, grad_source)
    return (updated, grad_source.astype(jnp.bfloat16), grad_w_in, grad_w_out, grad_kern)

def reference(features, cotangent, wet_fraction, slot_tile, neighbours, kernel, norm_gain, weight_in, bias_in, weight_out, layer_scale):
    metric = cell_metric(slot_tile)
    weight_cells = wet_fraction * metric
    cell_field = (features.astype(jnp.float32) * weight_cells[:, None, :]).astype(jnp.bfloat16)
    tile_fields = cell_field.reshape(SLOTS, C, TS, TS)
    main_packs = jax.vmap(rim_pack)(tile_fields)
    north_strips = tile_fields[:, :, TS - 3:, :].reshape(SLOTS, C, 3 * TS)
    slot_ids = jnp.arange(SLOTS, dtype=jnp.int32)
    slot_of = jnp.zeros((TILES,), jnp.int32).at[jnp.where(slot_tile >= 0, slot_tile, TILES)].set(slot_ids, mode='drop')
    near_table = jnp.where(slot_tile[:, None] >= 0, neighbours[jnp.maximum(slot_tile, 0)], -1)
    present = near_table >= 0
    flipped = jnp.where(present, near_table % 2, 0)
    owner_slot = slot_of[jnp.maximum(near_table, 0) // 2]

    def forward_one(items):
        index, tile_x, tile_grad, wet_row, metric_row = items
        chosen = jnp.where(present[index][:, None, None], main_packs[owner_slot[index]], jnp.zeros((), jnp.bfloat16))
        padded = assemble(tile_fields[index], chosen, north_strips[owner_slot[index, 0]], flipped[index, 0])
        return block_tile(padded, tile_x, tile_grad, wet_row, metric_row, kernel, norm_gain, weight_in, bias_in, weight_out, layer_scale)
    updated, grad_source_bf, grad_w_in, grad_w_out, grad_kern = lax.map(forward_one, (slot_ids, features, cotangent, wet_fraction, metric))

    def border_one(grad_bf):
        spread = spread_back(grad_bf, kernel)
        return (frame_pack(spread), spread[:, TS + 3:, 3:TS + 3].reshape(C, 3 * TS).astype(jnp.bfloat16))
    frames, mirror_frames = lax.map(border_one, grad_source_bf)

    def back_one(items):
        index, grad_bf = items
        spread = spread_back(grad_bf, kernel)
        chosen = jnp.where(present[index][:, None, None], frames[owner_slot[index]], jnp.zeros((), jnp.bfloat16))
        return receive(spread[:, 3:TS + 3, 3:TS + 3], chosen, mirror_frames[owner_slot[index, 0]], flipped[index, 0])
    grad_field = lax.map(back_one, (slot_ids, grad_source_bf))
    grad_features = (cotangent.astype(jnp.float32) + weight_cells[:, None, :] * grad_field.reshape(SLOTS, C, CELLS)).astype(jnp.bfloat16)
    grad_scale = 1.0 / math.sqrt(SLOTS * CELLS)
    return (updated, grad_features, lax.optimization_barrier(jnp.sum(grad_w_in, axis=0)) * grad_scale, lax.optimization_barrier(jnp.sum(grad_w_out, axis=0)) * grad_scale, lax.optimization_barrier(jnp.sum(grad_kern, axis=0)) * grad_scale)
```

```python
import math

import jax
import jax.numpy as jnp
from jax import lax
from jax.experimental import pallas as pl
from jax.experimental.pallas import tpu as pltpu
from jax.sharding import PartitionSpec as P

C = 128
HID = 512
TS = 96
CELLS = TS * TS
NODE = 4
WIDE = 32
PITCH = 112
PADROWS = TS + 6
STRIP = 3 * TS
BAND = 3 * PITCH
BLOCK = 768
CHUNK = 256
EPS = 1e-06
GELU_COEF = 0.7978845608028654
CUBIC = 0.044715
GRAD_SCALE = 1.0 / math.sqrt(NODE * WIDE * CELLS)
MESH = pl.DeviceIdType.MESH
F32 = jnp.float32
BF16 = jnp.bfloat16
VMEM_LIMIT = 60 * 2**20


def border_peers(n, w):
    out = []
    for k in range(1, 4):
        out.append((k - 1, k - 1, (lax.rem(n + k, 4), w)))
    sides = ((3, 3, lax.rem(w + 31, 32)), (7, 4, lax.rem(w + 1, 32)), (11, 5, 31 - w))
    for base, source, column in sides:
        for k in range(4):
            out.append((base + k, source, (lax.rem(n + k, 4), column)))
    return out


def broadcast_taps(k49, kb):
    for t in range(49):
        kb[t] = jnp.broadcast_to(k49[t : t + 1, :], (8, C))


def taps_loop(src, kb, out, flip):
    def body(it, carry):
        i0 = (it // 6) * 4
        j0 = lax.rem(it, 6) * 16
        acc = [[None, None] for _ in range(4)]
        for b in range(7):
            for r in range(10):
                for h in range(2):
                    v = src[pl.ds((i0 + r) * PITCH + j0 + 5 + b + 8 * h, 8), :]
                    for a in range(7):
                        d = r - a
                        if 0 <= d < 4:
                            t = 48 - (7 * a + b) if flip else 7 * a + b
                            p = kb[t] * v
                            acc[d][h] = p if acc[d][h] is None else acc[d][h] + p
        for d in range(4):
            for h in range(2):
                o = pl.multiple_of((i0 + d) * TS + j0 + 8 * h, 8)
                out[pl.ds(o, 8), :] = acc[d][h]
        return carry

    lax.fori_loop(0, 144, body, 0)


def clear_margins(pad):
    zero8 = jnp.zeros((8, C), F32)
    zero_row = jnp.zeros((PITCH, C), F32)
    for r in (0, 1, 2, 99, 100, 101):
        pad[r * PITCH : (r + 1) * PITCH, :] = zero_row

    def body(i, carry):
        o = pl.multiple_of((i + 3) * PITCH, 8)
        pad[pl.ds(o, 8), :] = zero8
        pad[pl.ds(o + 104, 8), :] = zero8
        return carry

    lax.fori_loop(0, TS, body, 0)


def halo_kernel(feat, wc, k49, north_of, conv0, pad, got, strips, kb, send_sem, recv_sem):
    n = lax.axis_index("node")
    w = lax.axis_index("wide")
    peers = border_peers(n, w)
    barrier = pltpu.get_barrier_semaphore()
    for _, _, device in peers:
        pl.semaphore_signal(barrier, inc=1, device_id=device, device_id_type=MESH)

    broadcast_taps(k49, kb)
    clear_margins(pad)

    def prep(g, carry):
        o = pl.multiple_of(g * 384, 128)
        x = feat[:, pl.ds(o, 384)].astype(F32) * wc[:, pl.ds(o, 384)]
        t = x.astype(BF16).astype(F32).T
        for r in range(4):
            row = pl.multiple_of((g * 4 + r + 3) * PITCH + 8, 8)
            pad[pl.ds(row, TS), :] = t[r * TS : (r + 1) * TS]
        return carry

    lax.fori_loop(0, 24, prep, 0)
    for q in range(3):
        here = pl.ds(q * TS, TS)
        strips[3, here, :] = pad[pl.ds(3 * PITCH + 8 + q, TS, stride=PITCH), :].astype(BF16)
        strips[4, here, :] = pad[pl.ds(3 * PITCH + 101 + q, TS, stride=PITCH), :].astype(BF16)
        south = pad[pl.ds((3 + q) * PITCH + 8, TS), :]
        north = pad[pl.ds((96 + q) * PITCH + 8, TS), :]
        strips[5, here, :] = north.astype(BF16)
        for k in range(3):
            mine = jnp.where(north_of[k : k + 1, :] > 0.0, south, north)
            strips[k, here, :] = mine.astype(BF16)

    pl.semaphore_wait(barrier, len(peers))
    copies = []
    for slot, source, device in peers:
        copy = pltpu.make_async_remote_copy(
            src_ref=strips.at[source],
            dst_ref=got.at[slot],
            send_sem=send_sem.at[slot],
            recv_sem=recv_sem.at[slot],
            device_id=device,
            device_id_type=MESH,
        )
        copy.start()
        copies.append(copy)

    taps_loop(pad, kb, conv0, False)
    for copy in copies:
        copy.wait()


def halo_call(feat, wc, k49, north_of):
    vmem = pl.BlockSpec(memory_space=pltpu.VMEM)
    return pl.pallas_call(
        halo_kernel,
        out_shape=(
            jax.ShapeDtypeStruct((CELLS, C), F32),
            jax.ShapeDtypeStruct((PADROWS * PITCH, C), F32),
            jax.ShapeDtypeStruct((15, STRIP, C), BF16),
        ),
        in_specs=[vmem] * 4,
        out_specs=(vmem, vmem, vmem),
        scratch_shapes=[
            pltpu.VMEM((6, STRIP, C), BF16),
            pltpu.VMEM((49, 8, C), F32),
            pltpu.SemaphoreType.DMA((15,)),
            pltpu.SemaphoreType.DMA((15,)),
        ],
        compiler_params=pltpu.CompilerParams(
            collective_id=0, has_side_effects=True, vmem_limit_bytes=VMEM_LIMIT
        ),
        name="halo",
    )(feat, wc, k49, north_of)


def nt(a, b):
    return lax.dot_general(a, b, (((1,), (1,)), ((), ())), preferred_element_type=F32)


def mm(a, b):
    return jnp.dot(a, b, preferred_element_type=F32)


def wide2(column):
    return jnp.concatenate([column, column], axis=1)


def mlp_kernel(
    pick, got, conv0, feat, cot, wet, rmet, k49, gain, w_in_t, w_in, bias, w_out_t, w_out, scale,
    updated, gsrc, gwi, gwo, hw, he, hs, hn,
    cv, kb, strip,
):
    step = pl.program_id(0)

    @pl.when(step == 0)
    def _():
        broadcast_taps(k49, kb)
        gwi[...] = jnp.zeros_like(gwi)
        gwo[...] = jnp.zeros_like(gwo)
        hw[...] = jnp.zeros_like(hw)
        he[...] = jnp.zeros_like(he)

        def chosen(direction, q):
            v = got[pick[direction], pl.ds(q * TS, TS), :].astype(F32)
            return jnp.where(pick[8 + direction] > 0, v, 0.0)

        for side, (mid, top, low), col in ((hw, (2, 4, 6), 5), (he, (3, 5, 7), 8)):
            for q in range(3):
                strip[0:TS, :] = chosen(low, q)
                strip[0:3, :] = strip[TS - 3 : TS, :]
                strip[3 : TS + 3, :] = chosen(mid, q)
                strip[112 : 112 + TS, :] = chosen(top, q)
                strip[TS + 3 : TS + 6, :] = strip[112:115, :]
                side[pl.ds(col + q, PADROWS, stride=16), :] = strip[0:PADROWS, :]
        i0 = lax.broadcasted_iota(jnp.int32, (TS, TS), 0)
        i1 = lax.broadcasted_iota(jnp.int32, (TS, TS), 1)
        turn = (i0 + i1 == TS - 1).astype(BF16)
        for q in range(3):
            o = q * PITCH
            hs[o + 8 : o + 104, :] = chosen(1, q)
            hs[o : o + 8, :] = hw[q * 16 : q * 16 + 8, :]
            hs[o + 104 : o + 112, :] = he[q * 16 + 8 : q * 16 + 16, :]
            flipped = mm(turn, got[pick[16], (2 - q) * TS : (3 - q) * TS, :])
            north = jnp.where(pick[17] > 0, flipped, chosen(0, q))
            hn[o + 8 : o + 104, :] = jnp.where(pick[8] > 0, north, 0.0)
            r = (TS + 3 + q) * 16
            hn[o : o + 8, :] = hw[r : r + 8, :]
            hn[o + 104 : o + 112, :] = he[r + 8 : r + 16, :]

    cv[...] = conv0[...]

    for r in range(8):
        for side, taps, shift, col in ((hw, (0, 1, 2), 5, 0), (he, (4, 5, 6), -3, 88)):
            total = cv[r * TS + col : r * TS + col + 8, :]
            for a in range(7):
                row = step * 8 + r + a
                inside = jnp.logical_and(row >= 3, row < TS + 3).astype(F32)
                part = None
                for b in taps:
                    v = kb[7 * a + b] * side[pl.ds(row * 16 + b + shift, 8), :]
                    part = v if part is None else part + v
                total = total + part * inside
            cv[r * TS + col : r * TS + col + 8, :] = total

    def rim(rows, pairs):
        def body(jb, carry):
            j0 = pl.multiple_of(jb * 8, 8)
            for d, terms in pairs:
                o = pl.ds(pl.multiple_of(d * TS + j0, 8), 8)
                total = cv[o, :]
                for a, r in terms:
                    for b in range(7):
                        total = total + kb[7 * a + b] * rows[pl.ds(r * PITCH + j0 + 5 + b, 8), :]
                cv[o, :] = total
            return carry

        lax.fori_loop(0, 12, body, 0)

    @pl.when(step == 0)
    def _():
        rim(hs, [(i, [(a, i + a) for a in range(3 - i)]) for i in range(3)])

    @pl.when(step == 11)
    def _():
        rim(hn, [(5 + i, [(a, i + a - 6) for a in range(6 - i, 7)]) for i in range(3)])

    def chunk(c, carry):
        here = pl.ds(pl.multiple_of(c * CHUNK, CHUNK), CHUNK)
        rm = rmet[:, here]
        conv = cv[here, :].T * rm
        centred = conv - jnp.mean(conv, axis=0, keepdims=True)
        inv_std = lax.rsqrt(jnp.mean(centred * centred, axis=0, keepdims=True) + EPS)
        normed = centred * inv_std
        g2 = wide2(gain[...])
        normed_bf = (normed * g2).astype(BF16)
        hidden = mm(w_in_t[...], normed_bf) + wide2(bias[...])
        sq = hidden * hidden
        t = jnp.tanh(hidden * (GELU_COEF + (GELU_COEF * CUBIC) * sq))
        p = 0.5 + 0.5 * t
        active = hidden * p
        active_bf = active.astype(BF16)
        mixed = mm(w_out_t[...], active_bf)
        ms = wet[:, here] * wide2(scale[...])
        updated[:, here] = (feat[:, here].astype(F32) + ms * mixed).astype(BF16)
        gm = (ms * cot[:, here].astype(F32)).astype(BF16)
        slope = p + active * (1.0 - p) * (2.0 * GELU_COEF + (6.0 * GELU_COEF * CUBIC) * sq)
        gh = (mm(w_out[...], gm) * slope).astype(BF16)
        gn = mm(w_in[...], gh) * g2
        gwo[...] += nt(gm, active_bf)
        gwi[...] += nt(normed_bf, gh)
        gc = inv_std * (
            gn
            - jnp.mean(gn, axis=0, keepdims=True)
            - normed * jnp.mean(gn * normed, axis=0, keepdims=True)
        )
        gsrc[here, :] = (gc * rm).T.astype(BF16)
        return carry

    lax.fori_loop(0, BLOCK // CHUNK, chunk, 0)


def mlp_call(pick, got, conv0, feat, cot, wet, rmet, k49, gain, w_in, bias, w_out, scale):
    def whole(*shape):
        return pl.BlockSpec(shape, lambda i, p: (0,) * len(shape))

    rows = pl.BlockSpec((BLOCK, C), lambda i, p: (i, 0))
    cols = pl.BlockSpec((C, BLOCK), lambda i, p: (0, i))
    lane = pl.BlockSpec((1, BLOCK), lambda i, p: (0, i))
    return pl.pallas_call(
        mlp_kernel,
        out_shape=(
            jax.ShapeDtypeStruct((C, CELLS), BF16),
            jax.ShapeDtypeStruct((CELLS, C), BF16),
            jax.ShapeDtypeStruct((C, HID), F32),
            jax.ShapeDtypeStruct((C, HID), F32),
            jax.ShapeDtypeStruct((PADROWS * 16, C), F32),
            jax.ShapeDtypeStruct((PADROWS * 16, C), F32),
            jax.ShapeDtypeStruct((BAND, C), F32),
            jax.ShapeDtypeStruct((BAND, C), F32),
        ),
        grid_spec=pltpu.PrefetchScalarGridSpec(
            num_scalar_prefetch=1,
            grid=(CELLS // BLOCK,),
            in_specs=[
                whole(15, STRIP, C), rows, cols, cols, lane, lane, whole(49, C), whole(C, C),
                whole(HID, C), whole(C, HID), whole(HID, C), whole(C, HID), whole(HID, C),
                whole(C, C),
            ],
            out_specs=[
                cols, rows, whole(C, HID), whole(C, HID), whole(PADROWS * 16, C),
                whole(PADROWS * 16, C), whole(BAND, C), whole(BAND, C),
            ],
            scratch_shapes=[
                pltpu.VMEM((BLOCK, C), F32),
                pltpu.VMEM((49, 8, C), F32),
                pltpu.VMEM((208, C), F32),
            ],
        ),
        compiler_params=pltpu.CompilerParams(vmem_limit_bytes=VMEM_LIMIT),
        name="mlp",
    )(
        pick, got, conv0, feat, cot, wet, rmet, k49,
        jnp.broadcast_to(gain[:, None], (C, C)),
        w_in.T, w_in,
        jnp.broadcast_to(bias[:, None], (HID, C)),
        w_out.T, w_out,
        jnp.broadcast_to(scale[:, None], (C, C)),
    )


def back_kernel(
    gsrc, pad_hbm, hw, he, hs, hn, k49, north_of, gwi, gwo,
    inner, got, wsum, ksum,
    pad, gp, kb, frame, fw, fe, strips, wmine, wpart, wnode, wall, kacc, kmine, kpart, kwide, kall,
    pad_sem, bsend, brecv, s1, r1, s2, r2, s3, r3, s4, r4, s5, r5, s6, r6,
):
    n = lax.axis_index("node")
    w = lax.axis_index("wide")
    peers = border_peers(n, w)
    wide_peers = [(k, lax.rem(w + k, WIDE)) for k in range(1, WIDE)]
    node_peers = [(k, lax.rem(n + k, NODE)) for k in range(1, NODE)]
    greet = [(n, v) for _, v in wide_peers] + [(v, w) for _, v in node_peers]
    greet += [device for slot, _, device in peers if slot > 2 and slot not in (3, 7, 11)]
    barrier = pltpu.get_barrier_semaphore()
    for device in greet:
        pl.semaphore_signal(barrier, inc=1, device_id=device, device_id_type=MESH)
    fetch = pltpu.make_async_copy(pad_hbm, pad, pad_sem)
    fetch.start()

    def send(src, dst, send_sem, recv_sem, device):
        copy = pltpu.make_async_remote_copy(
            src_ref=src,
            dst_ref=dst,
            send_sem=send_sem,
            recv_sem=recv_sem,
            device_id=device,
            device_id_type=MESH,
        )
        copy.start()
        return copy

    for k in range(4):
        here = slice(k * C, (k + 1) * C)
        wmine[here, :] = (gwi[:, here] * GRAD_SCALE).astype(BF16)
        wmine[HID + k * C : HID + (k + 1) * C, :] = (gwo[:, here] * GRAD_SCALE).astype(BF16)
    pl.semaphore_wait(barrier, len(greet))
    first = []
    for k, v in wide_peers:
        src = wmine.at[pl.ds(pl.multiple_of(v * 32, 32), 32)]
        first.append(send(src, wpart.at[k], s1.at[k], r1.at[k], (n, v)))

    broadcast_taps(k49, kb)
    clear_margins(gp)

    def fill(i, carry):
        o = pl.multiple_of((i + 3) * PITCH + 8, 8)
        gp[pl.ds(o, TS), :] = gsrc[pl.ds(pl.multiple_of(i * TS, 32), TS), :].astype(F32)
        return carry

    lax.fori_loop(0, TS, fill, 0)

    def frame_rows(jb, carry):
        j0 = pl.multiple_of(jb * 8, 8)
        for f, p in enumerate((0, 1, 2, 99, 100, 101)):
            total = None
            for a in range(7):
                if 0 <= p - a < TS:
                    for b in range(7):
                        v = kb[7 * a + b] * gp[pl.ds((p - a + 3) * PITCH + j0 + 8 - b, 8), :]
                        total = v if total is None else total + v
            frame[f, pl.ds(j0, 8), :] = total
        return carry

    lax.fori_loop(0, 13, frame_rows, 0)

    def frame_cols(i, carry):
        p = i + 3
        for side, taps, q0 in ((fw, (0, 1, 2), 0), (fe, (4, 5, 6), 96)):
            total = None
            for a in range(7):
                for b in taps:
                    v = kb[7 * a + b] * gp[pl.ds((p - a + 3) * PITCH + q0 + 8 - b, 8), :]
                    total = v if total is None else total + v
            side[pl.ds(pl.multiple_of(p * 8, 8), 8), :] = total
        return carry

    lax.fori_loop(0, TS, frame_cols, 0)
    for f, p in enumerate((0, 1, 2, 99, 100, 101)):
        fw[p * 8 : p * 8 + 8, :] = frame[f, 0:8, :]
        fe[p * 8 : p * 8 + 8, :] = frame[f, 96:104, :]
    fw[PADROWS * 8 :, :] = jnp.zeros((80, C), F32)
    fe[PADROWS * 8 :, :] = jnp.zeros((80, C), F32)
    for q in range(3):
        here = pl.ds(q * PITCH, PITCH)
        strips[3, here, :] = fw[pl.ds(q, PITCH, stride=8), :].astype(BF16)
        strips[4, here, :] = fe[pl.ds(3 + q, PITCH, stride=8), :].astype(BF16)
        here = pl.ds(q * TS, TS)
        south = frame[q, 3 : 3 + TS, :]
        north = frame[3 + q, 3 : 3 + TS, :]
        strips[5, here, :] = north.astype(BF16)
        for k in range(3):
            mine = jnp.where(north_of[k : k + 1, :] > 0.0, south, north)
            strips[k, here, :] = mine.astype(BF16)
    borders = []
    for slot, source, device in peers:
        size = BAND if source in (3, 4) else STRIP
        borders.append(
            send(
                strips.at[source, pl.ds(0, size)],
                got.at[slot, pl.ds(0, size)],
                bsend.at[slot],
                brecv.at[slot],
                device,
            )
        )

    fetch.wait()
    pad[0:BAND, :] = hs[...]
    pad[99 * PITCH :, :] = hn[...]

    def sides(i, carry):
        o = pl.multiple_of((i + 3) * PITCH, 8)
        r = pl.multiple_of((i + 3) * 16, 8)
        pad[pl.ds(o, 8), :] = hw[pl.ds(r, 8), :]
        pad[pl.ds(o + 104, 8), :] = he[pl.ds(r + 8, 8), :]
        return carry

    lax.fori_loop(0, TS, sides, 0)
    kmine[48:64, :] = jnp.zeros((16, C), BF16)
    for b in range(7):

        def taps(it, acc, b=b):
            i0 = it * 4
            acc = list(acc)
            for jb in range(12):
                g = [gp[pl.ds((i0 + d + 3) * PITCH + 8 + 8 * jb, 8), :] for d in range(4)]
                for r in range(10):
                    v = pad[pl.ds((i0 + r) * PITCH + 8 * jb + 5 + b, 8), :]
                    for a in range(7):
                        if 0 <= r - a < 4:
                            acc[a] = acc[a] + g[r - a] * v
            return tuple(acc)

        zero = jnp.zeros((8, C), F32)
        acc = lax.fori_loop(0, 24, taps, (zero,) * 7)
        for a in range(7):
            kacc[7 * a + b : 7 * a + b + 1, :] = jnp.sum(acc[a], axis=0, keepdims=True)
    kacc[49:64, :] = jnp.zeros((15, C), F32)
    kmine[...] = (kacc[...] * GRAD_SCALE).astype(BF16)

    for copy in first:
        copy.wait()
    mine = pl.ds(pl.multiple_of(w * 32, 32), 32)
    total = wmine[mine, :].astype(F32)
    for k in range(1, WIDE):
        total = total + wpart[k].astype(F32)
    wnode[n] = total.astype(BF16)
    second = []
    for k, v in node_peers:
        second.append(send(wnode.at[n], wnode.at[n], s2.at[k], r2.at[k], (v, w)))
        src = kmine.at[pl.ds(pl.multiple_of(v * 16, 16), 16)]
        second.append(send(src, kpart.at[k], s4.at[k], r4.at[k], (v, w)))

    taps_loop(gp, kb, inner, True)

    for copy in second:
        copy.wait()
    total = wnode[0].astype(F32)
    for v in range(1, NODE):
        total = total + wnode[v].astype(F32)
    wall[w] = total.astype(BF16)
    total = kmine[pl.ds(pl.multiple_of(n * 16, 16), 16), :].astype(F32)
    for k in range(1, NODE):
        total = total + kpart[k].astype(F32)
    kwide[w] = total.astype(BF16)
    third = []
    for k, v in wide_peers:
        third.append(send(wall.at[w], wall.at[w], s3.at[k], r3.at[k], (n, v)))
        third.append(send(kwide.at[w], kwide.at[w], s5.at[k], r5.at[k], (n, v)))
    for copy in third:
        copy.wait()
    total = kwide[0].astype(F32)
    for v in range(1, WIDE):
        total = total + kwide[v].astype(F32)
    kall[n] = total.astype(BF16)
    fourth = []
    for k, v in node_peers:
        fourth.append(send(kall.at[n], kall.at[n], s6.at[k], r6.at[k], (v, w)))
    for v in range(WIDE):
        wsum[v * 32 : (v + 1) * 32, :] = wall[v].astype(F32)
    for copy in fourth:
        copy.wait()
    for v in range(NODE):
        ksum[v * 16 : (v + 1) * 16, :] = kall[v].astype(F32)
    for copy in borders:
        copy.wait()


def back_call(gsrc, pad, hw, he, hs, hn, k49, north_of, gwi, gwo):
    vmem = pl.BlockSpec(memory_space=pltpu.VMEM)
    dma = pltpu.SemaphoreType.DMA
    return pl.pallas_call(
        back_kernel,
        out_shape=(
            jax.ShapeDtypeStruct((CELLS, C), F32),
            jax.ShapeDtypeStruct((15, BAND, C), BF16),
            jax.ShapeDtypeStruct((8 * C, C), F32),
            jax.ShapeDtypeStruct((64, C), F32),
        ),
        in_specs=[vmem, pl.BlockSpec(memory_space=pl.ANY)] + [vmem] * 8,
        out_specs=(vmem,) * 4,
        scratch_shapes=[
            pltpu.VMEM((PADROWS * PITCH, C), F32),
            pltpu.VMEM((PADROWS * PITCH, C), F32),
            pltpu.VMEM((49, 8, C), F32),
            pltpu.VMEM((6, 104, C), F32),
            pltpu.VMEM((PITCH * 8, C), F32),
            pltpu.VMEM((PITCH * 8, C), F32),
            pltpu.VMEM((6, BAND, C), BF16),
            pltpu.VMEM((8 * C, C), BF16),
            pltpu.VMEM((WIDE, 32, C), BF16),
            pltpu.VMEM((NODE, 32, C), BF16),
            pltpu.VMEM((WIDE, 32, C), BF16),
            pltpu.VMEM((64, C), F32),
            pltpu.VMEM((64, C), BF16),
            pltpu.VMEM((NODE, 16, C), BF16),
            pltpu.VMEM((WIDE, 16, C), BF16),
            pltpu.VMEM((NODE, 16, C), BF16),
            dma,
            dma((15,)), dma((15,)),
            dma((WIDE,)), dma((WIDE,)),
            dma((NODE,)), dma((NODE,)),
            dma((WIDE,)), dma((WIDE,)),
            dma((NODE,)), dma((NODE,)),
            dma((WIDE,)), dma((WIDE,)),
            dma((NODE,)), dma((NODE,)),
        ],
        compiler_params=pltpu.CompilerParams(
            collective_id=1, has_side_effects=True, vmem_limit_bytes=VMEM_LIMIT
        ),
        name="back",
    )(gsrc, pad, hw, he, hs, hn, k49, north_of, gwi, gwo)


def final_kernel(pick, got, inner, cot, wc, out, cw, ce, low, top, strip, sb):
    step = pl.program_id(0)

    @pl.when(step == 0)
    def _():
        cw[...] = jnp.zeros_like(cw)
        ce[...] = jnp.zeros_like(ce)

        def chosen(direction, start, size):
            v = got[pick[direction], pl.ds(start, size), :].astype(F32)
            return jnp.where(pick[8 + direction] > 0, v, 0.0)

        for side, (mid, north, south), col in ((cw, (2, 4, 6), 0), (ce, (3, 5, 7), 5)):
            for q in range(3):
                strip[0] = chosen(mid, q * PITCH, PITCH)
                strip[1] = chosen(north, q * PITCH, PITCH)
                strip[2] = chosen(south, q * PITCH, PITCH)
                strip[0, TS : TS + 3, :] += strip[1, 0:3, :]
                strip[0, 3:6, :] += strip[2, TS + 3 : TS + 6, :]
                side[pl.ds(col + q, TS, stride=8), :] = strip[0, 3 : TS + 3, :]
        i0 = lax.broadcasted_iota(jnp.int32, (TS, TS), 0)
        i1 = lax.broadcasted_iota(jnp.int32, (TS, TS), 1)
        turn = (i0 + i1 == TS - 1).astype(BF16)
        for q in range(3):
            low[q * TS : (q + 1) * TS, :] = chosen(1, q * TS, TS)
            flipped = mm(turn, got[pick[16], (2 - q) * TS : (3 - q) * TS, :])
            north = jnp.where(pick[17] > 0, flipped, chosen(0, q * TS, TS))
            top[q * TS : (q + 1) * TS, :] = jnp.where(pick[8] > 0, north, 0.0)

    sb[...] = inner[...]
    for r in range(8):
        row = pl.multiple_of((step * 8 + r) * 8, 8)
        sb[r * TS : r * TS + 8, :] += cw[pl.ds(row, 8), :]
        sb[r * TS + 88 : r * TS + 96, :] += ce[pl.ds(row, 8), :]

    @pl.when(step == 0)
    def _():
        sb[0:STRIP, :] += low[...]

    @pl.when(step == 11)
    def _():
        sb[5 * TS :, :] += top[...]

    out[...] = (cot[...].astype(F32) + wc[...] * sb[...].T).astype(BF16)


def final_call(pick, got, inner, cot, wc):
    rows = pl.BlockSpec((BLOCK, C), lambda i, p: (i, 0))
    cols = pl.BlockSpec((C, BLOCK), lambda i, p: (0, i))
    lane = pl.BlockSpec((1, BLOCK), lambda i, p: (0, i))
    return pl.pallas_call(
        final_kernel,
        out_shape=jax.ShapeDtypeStruct((C, CELLS), BF16),
        grid_spec=pltpu.PrefetchScalarGridSpec(
            num_scalar_prefetch=1,
            grid=(CELLS // BLOCK,),
            in_specs=[pl.BlockSpec((15, BAND, C), lambda i, p: (0, 0, 0)), rows, cols, lane],
            out_specs=cols,
            scratch_shapes=[
                pltpu.VMEM((TS * 8, C), F32),
                pltpu.VMEM((TS * 8, C), F32),
                pltpu.VMEM((STRIP, C), F32),
                pltpu.VMEM((STRIP, C), F32),
                pltpu.VMEM((3, PITCH, C), F32),
                pltpu.VMEM((BLOCK, C), F32),
            ],
        ),
        compiler_params=pltpu.CompilerParams(vmem_limit_bytes=VMEM_LIMIT),
        name="final",
    )(pick, got, inner, cot, wc)


def local(
    features,
    cotangent,
    wet_fraction,
    slot_tile,
    neighbours,
    kernel,
    norm_gain,
    weight_in,
    bias_in,
    weight_out,
    layer_scale,
):
    n = lax.axis_index("node")
    w = lax.axis_index("wide")
    tile = slot_tile[n * WIDE + w]
    row = jnp.maximum(tile, 0) // WIDE
    cell_row = jnp.arange(CELLS, dtype=jnp.int32) // TS
    global_row = row * TS + cell_row
    latitude = -80.0 + 160.0 * (global_row.astype(F32) + 0.5) / float(8 * TS)
    metric = jnp.cos(latitude * (math.pi / 180.0))[None, :]
    near = jnp.where(tile >= 0, neighbours[jnp.maximum(tile, 0)], -1)
    present = near >= 0
    target = jnp.maximum(near, 0) // 2
    slot_ids = jnp.arange(NODE * WIDE, dtype=jnp.int32)
    owner = jnp.sum(
        jnp.where(slot_tile[None, :] == target[:, None], slot_ids[None, :], 0), axis=-1
    )
    turn = (n - owner // WIDE + NODE) % NODE
    base = jnp.array([-1, -1, 7, 3, 7, 3, 7, 3], jnp.int32)
    slot = jnp.where(present, jnp.maximum(base + turn, 0), 0)
    flip = jnp.where(present[0], near[0] % 2, 0)
    pick = jnp.concatenate(
        [
            slot.at[0].set(jnp.where(flip > 0, 0, slot[0])),
            present.astype(jnp.int32),
            jnp.stack([11 + turn[0], flip]),
        ]
    )
    column = slot_tile[((n + jnp.arange(1, 4)) % NODE) * WIDE + w]
    is_north = (column == target[1]) & present[1]
    north_of = jnp.broadcast_to(
        jnp.pad(is_north.astype(F32), (0, 5))[:, None], (8, C)
    )
    wc = wet_fraction * metric
    feat = features.reshape(C, CELLS)
    cot = cotangent.reshape(C, CELLS)
    conv0, pad, got = halo_call(feat, wc, kernel, north_of)
    updated, gsrc, gwi, gwo, hw, he, hs, hn = mlp_call(
        pick, got, conv0, feat, cot, wet_fraction, 1.0 / metric, kernel, norm_gain, weight_in,
        bias_in, weight_out, layer_scale,
    )
    inner, back_got, wsum, ksum = back_call(gsrc, pad, hw, he, hs, hn, kernel, north_of, gwi, gwo)
    grad_features = final_call(pick, back_got, inner, cot, wc)
    halves = wsum.reshape(2, 4, C, C)
    grad_in = jnp.transpose(halves[0], (1, 0, 2)).reshape(C, HID)
    grad_out = jnp.transpose(halves[1], (0, 2, 1)).reshape(HID, C)
    return (
        updated.reshape(1, C, CELLS),
        grad_features.reshape(1, C, CELLS),
        grad_in,
        grad_out,
        ksum[:49],
    )


def solution(mesh):
    shards = P(("node", "wide"), None, None)
    in_specs = (shards, shards, P(("node", "wide"), None)) + (P(),) * 8
    out_specs = (shards, shards, P(), P(), P())
    return jax.shard_map(local, mesh=mesh, in_specs=in_specs, out_specs=out_specs, check_vma=False)
```

```python
import math

import jax
import jax.numpy as jnp
from jax import lax
from jax.experimental import pallas as pl
from jax.experimental.pallas import tpu as pltpu
from jax.sharding import PartitionSpec as P

C = 128
HID = 512
TS = 96
CELLS = TS * TS
NODE = 4
WIDE = 32
PITCH = 112
PADROWS = TS + 6
STRIP = 3 * TS
BAND = 3 * PITCH
BLOCK = 768
CHUNK = 256
EPS = 1e-06
GELU_COEF = 0.7978845608028654
CUBIC = 0.044715
GRAD_SCALE = 1.0 / math.sqrt(NODE * WIDE * CELLS)
MESH = pl.DeviceIdType.MESH
F32 = jnp.float32
BF16 = jnp.bfloat16
VMEM_LIMIT = 60 * 2**20


def border_peers(n, w):
    out = []
    for k in range(1, 4):
        out.append((k - 1, k - 1, (lax.rem(n + k, 4), w)))
    sides = ((3, 3, lax.rem(w + 31, 32)), (7, 4, lax.rem(w + 1, 32)), (11, 5, 31 - w))
    for base, source, column in sides:
        for k in range(4):
            out.append((base + k, source, (lax.rem(n + k, 4), column)))
    return out


def broadcast_taps(k49, kb):
    for t in range(49):
        kb[t] = jnp.broadcast_to(k49[t : t + 1, :], (8, C))


def taps_loop(src, kb, out, flip):
    zero = jnp.zeros((TS, C), F32)

    def clear(i, carry):
        out[pl.ds(pl.multiple_of(i * TS, 8), TS), :] = zero
        return carry

    lax.fori_loop(0, TS, clear, 0)

    def body(it, carry):
        b = it // 12
        i0 = lax.rem(it, 12) * 8
        taps = [kb[48 - 7 * a - b] if flip else kb[7 * a + b] for a in range(7)]
        for jb in range(12):
            base = i0 * PITCH + 8 * jb + 5 + b
            v = [src[pl.ds(base + r * PITCH, 8), :] for r in range(14)]
            for d in range(8):
                total = taps[0] * v[d]
                for a in range(1, 7):
                    total = total + taps[a] * v[d + a]
                o = pl.ds(pl.multiple_of((i0 + d) * TS + 8 * jb, 8), 8)
                out[o, :] = out[o, :] + total
        return carry

    lax.fori_loop(0, 84, body, 0)


def clear_margins(pad):
    zero8 = jnp.zeros((8, C), F32)
    zero_row = jnp.zeros((PITCH, C), F32)
    for r in (0, 1, 2, 99, 100, 101):
        pad[r * PITCH : (r + 1) * PITCH, :] = zero_row

    def body(i, carry):
        o = pl.multiple_of((i + 3) * PITCH, 8)
        pad[pl.ds(o, 8), :] = zero8
        pad[pl.ds(o + 104, 8), :] = zero8
        return carry

    lax.fori_loop(0, TS, body, 0)


def cosine(x):
    x2 = x * x
    total = jnp.full_like(x, 1.0 / math.factorial(16))
    for k in range(7, -1, -1):
        total = total * x2 + (-1.0) ** k / math.factorial(2 * k)
    return total


def halo_kernel(
    feat, wet, k49, slot_tile, neighbours,
    conv0, field, got, wc, rmet, pick,
    pad, strips, kb, send_sem, recv_sem,
):
    n = lax.axis_index("node")
    w = lax.axis_index("wide")
    peers = border_peers(n, w)
    barrier = pltpu.get_barrier_semaphore()
    for _, _, device in peers:
        pl.semaphore_signal(barrier, inc=1, device_id=device, device_id_type=MESH)

    tile = slot_tile[n * WIDE + w]
    known = jnp.maximum(tile, 0)
    lane = lax.broadcasted_iota(jnp.int32, (1, 8), 1)
    near = jnp.where(tile >= 0, neighbours[pl.ds(known, 1), :], -1)
    present = near >= 0
    target = jnp.maximum(near, 0) >> 1
    flip = jnp.where(present, near & 1, 0)
    is_west = (lane == 2) | (lane == 4) | (lane == 6)
    is_east = (lane == 3) | (lane == 5) | (lane == 7)
    turn = jnp.zeros((1, 8), jnp.int32)
    mirror_turn = jnp.zeros((1, 8), jnp.int32)
    for k in range(4):
        m = lax.rem(n + 4 - k, 4) * WIDE
        held = jnp.where(
            is_west,
            slot_tile[m + lax.rem(w + 31, 32)],
            jnp.where(is_east, slot_tile[m + lax.rem(w + 1, 32)], slot_tile[m + w]),
        )
        turn = jnp.where(held == target, k, turn)
        mirror_turn = jnp.where(slot_tile[m + 31 - w] == target, k, mirror_turn)
    slot = jnp.where(is_west, 7 + turn, jnp.where(is_east, 3 + turn, turn - 1))
    slot = jnp.where(present & (flip == 0), jnp.maximum(slot, 0), 0)
    pick[...] = jnp.zeros((8, 128), jnp.int32)
    pick[0:1, 0:8] = slot
    pick[1:2, 0:8] = present.astype(jnp.int32)
    pick[2:3, 0:8] = 11 + mirror_turn
    pick[3:4, 0:8] = flip
    north_of = []
    for k in range(1, 4):
        held = slot_tile[lax.rem(n + k, 4) * WIDE + w]
        same = jnp.where((lane == 1) & present & (held == target), 1.0, 0.0)
        same = jnp.broadcast_to(jnp.sum(same, axis=1, keepdims=True), (1, C))
        north_of.append(same > 0.0)
        pick[3 + k : 4 + k, :] = same.astype(jnp.int32)

    broadcast_taps(k49, kb)
    clear_margins(pad)
    cell = lax.broadcasted_iota(jnp.int32, (1, 384), 1)
    sub_row = jnp.where(cell >= 96, 1.0, 0.0) + jnp.where(cell >= 192, 1.0, 0.0)
    sub_row = sub_row + jnp.where(cell >= 288, 1.0, 0.0)
    first_row = ((known >> 5) * TS).astype(F32) + 0.5

    def prep(g, carry):
        here = pl.ds(pl.multiple_of(g * 384, 128), 384)
        latitude = -80.0 + 160.0 * (sub_row + ((g * 4).astype(F32) + first_row)) / float(8 * TS)
        metric = cosine(latitude * (math.pi / 180.0))
        weight = wet[:, here] * metric
        wc[:, here] = weight
        rmet[:, here] = 1.0 / metric
        t = (feat[:, here].astype(F32) * weight).astype(BF16).astype(F32).T
        for r in range(4):
            row = pl.multiple_of((g * 4 + r + 3) * PITCH + 8, 8)
            pad[pl.ds(row, TS), :] = t[r * TS : (r + 1) * TS]
        field[pl.ds(pl.multiple_of(g * 384, 128), 384), :] = t.astype(BF16)
        return carry

    lax.fori_loop(0, 24, prep, 0)
    for q in range(3):
        here = pl.ds(q * TS, TS)
        strips[3, here, :] = pad[pl.ds(3 * PITCH + 8 + q, TS, stride=PITCH), :].astype(BF16)
        strips[4, here, :] = pad[pl.ds(3 * PITCH + 101 + q, TS, stride=PITCH), :].astype(BF16)
        south = pad[pl.ds((3 + q) * PITCH + 8, TS), :]
        north = pad[pl.ds((96 + q) * PITCH + 8, TS), :]
        strips[5, here, :] = north.astype(BF16)
        for k in range(3):
            strips[k, here, :] = jnp.where(north_of[k], south, north).astype(BF16)

    pl.semaphore_wait(barrier, len(peers))
    copies = []
    for slot, source, device in peers:
        copy = pltpu.make_async_remote_copy(
            src_ref=strips.at[source],
            dst_ref=got.at[slot],
            send_sem=send_sem.at[slot],
            recv_sem=recv_sem.at[slot],
            device_id=device,
            device_id_type=MESH,
        )
        copy.start()
        copies.append(copy)

    taps_loop(pad, kb, conv0, False)
    for copy in copies:
        copy.wait()


def halo_call(feat, wet, k49, slot_tile, neighbours):
    vmem = pl.BlockSpec(memory_space=pltpu.VMEM)
    smem = pl.BlockSpec(memory_space=pltpu.SMEM)
    return pl.pallas_call(
        halo_kernel,
        out_shape=(
            jax.ShapeDtypeStruct((CELLS, C), F32),
            jax.ShapeDtypeStruct((CELLS, C), BF16),
            jax.ShapeDtypeStruct((15, STRIP, C), BF16),
            jax.ShapeDtypeStruct((1, CELLS), F32),
            jax.ShapeDtypeStruct((1, CELLS), F32),
            jax.ShapeDtypeStruct((8, 128), jnp.int32),
        ),
        in_specs=[vmem, vmem, vmem, smem, vmem],
        out_specs=(vmem,) * 6,
        scratch_shapes=[
            pltpu.VMEM((PADROWS * PITCH, C), F32),
            pltpu.VMEM((6, STRIP, C), BF16),
            pltpu.VMEM((49, 8, C), F32),
            pltpu.SemaphoreType.DMA((15,)),
            pltpu.SemaphoreType.DMA((15,)),
        ],
        compiler_params=pltpu.CompilerParams(
            collective_id=0, has_side_effects=True, vmem_limit_bytes=VMEM_LIMIT
        ),
        name="halo",
    )(feat, wet, k49, slot_tile, neighbours)


def nt(a, b):
    return lax.dot_general(a, b, (((1,), (1,)), ((), ())), preferred_element_type=F32)


def mm(a, b):
    return jnp.dot(a, b, preferred_element_type=F32)


def wide2(column):
    return jnp.concatenate([column, column], axis=1)


def mlp_kernel(
    pick, got, conv0, feat, cot, wet, rmet, k49, gain_row, w_in, bias_row, w_out, scale_row,
    updated, gsrc, gwi, gwo, hw, he, hs, hn,
    cv, kb, strip, gain, scale, bias, w_in_t, w_out_t,
):
    step = pl.program_id(0)

    @pl.when(step == 0)
    def _():
        broadcast_taps(k49, kb)
        gain[...] = jnp.broadcast_to(gain_row[...], (C, C)).T
        scale[...] = jnp.broadcast_to(scale_row[...], (C, C)).T
        for k in range(4):
            here = slice(k * C, (k + 1) * C)
            bias[here, :] = jnp.broadcast_to(bias_row[:, here], (C, C)).T
            w_in_t[here, :] = w_in[:, here].astype(F32).T.astype(BF16)
            w_out_t[:, here] = w_out[here, :].astype(F32).T.astype(BF16)
        gwi[...] = jnp.zeros_like(gwi)
        gwo[...] = jnp.zeros_like(gwo)
        hw[...] = jnp.zeros_like(hw)
        he[...] = jnp.zeros_like(he)

        def chosen(direction, q):
            v = got[pick[0, direction], pl.ds(q * TS, TS), :].astype(F32)
            return jnp.where(pick[1, direction] > 0, v, 0.0)

        for side, (mid, top, low), col in ((hw, (2, 4, 6), 5), (he, (3, 5, 7), 8)):
            for q in range(3):
                strip[0:TS, :] = chosen(low, q)
                strip[0:3, :] = strip[TS - 3 : TS, :]
                strip[3 : TS + 3, :] = chosen(mid, q)
                strip[112 : 112 + TS, :] = chosen(top, q)
                strip[TS + 3 : TS + 6, :] = strip[112:115, :]
                side[pl.ds(col + q, PADROWS, stride=16), :] = strip[0:PADROWS, :]
        i0 = lax.broadcasted_iota(jnp.int32, (TS, TS), 0)
        i1 = lax.broadcasted_iota(jnp.int32, (TS, TS), 1)
        turn = (i0 + i1 == TS - 1).astype(BF16)
        for q in range(3):
            o = q * PITCH
            hs[o + 8 : o + 104, :] = chosen(1, q)
            hs[o : o + 8, :] = hw[q * 16 : q * 16 + 8, :]
            hs[o + 104 : o + 112, :] = he[q * 16 + 8 : q * 16 + 16, :]
            flipped = mm(turn, got[pick[2, 0], (2 - q) * TS : (3 - q) * TS, :])
            north = jnp.where(pick[3, 0] > 0, flipped, chosen(0, q))
            hn[o + 8 : o + 104, :] = jnp.where(pick[1, 0] > 0, north, 0.0)
            r = (TS + 3 + q) * 16
            hn[o : o + 8, :] = hw[r : r + 8, :]
            hn[o + 104 : o + 112, :] = he[r + 8 : r + 16, :]

    cv[...] = conv0[...]

    for r in range(8):
        for side, taps, shift, col in ((hw, (0, 1, 2), 5, 0), (he, (4, 5, 6), -3, 88)):
            total = cv[r * TS + col : r * TS + col + 8, :]
            for a in range(7):
                row = step * 8 + r + a
                inside = jnp.logical_and(row >= 3, row < TS + 3).astype(F32)
                part = None
                for b in taps:
                    v = kb[7 * a + b] * side[pl.ds(row * 16 + b + shift, 8), :]
                    part = v if part is None else part + v
                total = total + part * inside
            cv[r * TS + col : r * TS + col + 8, :] = total

    def rim(rows, pairs):
        def body(jb, carry):
            j0 = pl.multiple_of(jb * 8, 8)
            for d, terms in pairs:
                o = pl.ds(pl.multiple_of(d * TS + j0, 8), 8)
                total = cv[o, :]
                for a, r in terms:
                    for b in range(7):
                        total = total + kb[7 * a + b] * rows[pl.ds(r * PITCH + j0 + 5 + b, 8), :]
                cv[o, :] = total
            return carry

        lax.fori_loop(0, 12, body, 0)

    @pl.when(step == 0)
    def _():
        rim(hs, [(i, [(a, i + a) for a in range(3 - i)]) for i in range(3)])

    @pl.when(step == 11)
    def _():
        rim(hn, [(5 + i, [(a, i + a - 6) for a in range(6 - i, 7)]) for i in range(3)])

    for c in range(BLOCK // CHUNK):
        here = pl.ds(c * CHUNK, CHUNK)
        rm = rmet[:, here]
        conv = cv[here, :].T * rm
        centred = conv - jnp.mean(conv, axis=0, keepdims=True)
        inv_std = lax.rsqrt(jnp.mean(centred * centred, axis=0, keepdims=True) + EPS)
        normed = centred * inv_std
        g2 = wide2(gain[...])
        normed_bf = (normed * g2).astype(BF16)
        hidden = mm(w_in_t[...], normed_bf) + wide2(bias[...])
        sq = hidden * hidden
        t = jnp.tanh(hidden * (GELU_COEF + (GELU_COEF * CUBIC) * sq))
        p = 0.5 + 0.5 * t
        active = hidden * p
        active_bf = active.astype(BF16)
        mixed = mm(w_out_t[...], active_bf)
        ms = wet[:, here] * wide2(scale[...])
        updated[:, here] = (feat[:, here].astype(F32) + ms * mixed).astype(BF16)
        gm = (ms * cot[:, here].astype(F32)).astype(BF16)
        slope = p + active * (1.0 - p) * (2.0 * GELU_COEF + (6.0 * GELU_COEF * CUBIC) * sq)
        gh = (mm(w_out[...], gm) * slope).astype(BF16)
        gn = mm(w_in[...], gh) * g2
        gwo[...] += nt(gm, active_bf)
        gwi[...] += nt(normed_bf, gh)
        gc = inv_std * (
            gn
            - jnp.mean(gn, axis=0, keepdims=True)
            - normed * jnp.mean(gn * normed, axis=0, keepdims=True)
        )
        gsrc[here, :] = (gc * rm).T.astype(BF16)


def mlp_call(pick, got, conv0, feat, cot, wet, rmet, k49, gain, w_in, bias, w_out, scale):
    def whole(*shape):
        return pl.BlockSpec(shape, lambda i, p: (0,) * len(shape))

    rows = pl.BlockSpec((BLOCK, C), lambda i, p: (i, 0))
    cols = pl.BlockSpec((C, BLOCK), lambda i, p: (0, i))
    lane = pl.BlockSpec((1, BLOCK), lambda i, p: (0, i))
    return pl.pallas_call(
        mlp_kernel,
        out_shape=(
            jax.ShapeDtypeStruct((C, CELLS), BF16),
            jax.ShapeDtypeStruct((CELLS, C), BF16),
            jax.ShapeDtypeStruct((C, HID), F32),
            jax.ShapeDtypeStruct((C, HID), F32),
            jax.ShapeDtypeStruct((PADROWS * 16, C), F32),
            jax.ShapeDtypeStruct((PADROWS * 16, C), F32),
            jax.ShapeDtypeStruct((BAND, C), F32),
            jax.ShapeDtypeStruct((BAND, C), F32),
        ),
        grid_spec=pltpu.PrefetchScalarGridSpec(
            num_scalar_prefetch=1,
            grid=(CELLS // BLOCK,),
            in_specs=[
                whole(15, STRIP, C), rows, cols, cols, lane, lane, whole(49, C), whole(1, C),
                whole(C, HID), whole(1, HID), whole(HID, C), whole(1, C),
            ],
            out_specs=[
                cols, rows, whole(C, HID), whole(C, HID), whole(PADROWS * 16, C),
                whole(PADROWS * 16, C), whole(BAND, C), whole(BAND, C),
            ],
            scratch_shapes=[
                pltpu.VMEM((BLOCK, C), F32),
                pltpu.VMEM((49, 8, C), F32),
                pltpu.VMEM((208, C), F32),
                pltpu.VMEM((C, C), F32),
                pltpu.VMEM((C, C), F32),
                pltpu.VMEM((HID, C), F32),
                pltpu.VMEM((HID, C), BF16),
                pltpu.VMEM((C, HID), BF16),
            ],
        ),
        compiler_params=pltpu.CompilerParams(vmem_limit_bytes=VMEM_LIMIT),
        name="mlp",
    )(
        pick, got, conv0, feat, cot, wet, rmet, k49, gain[None, :], w_in, bias[None, :], w_out,
        scale[None, :],
    )


def back_kernel(
    gsrc, field, hw, he, hs, hn, k49, north_of, gwi, gwo,
    inner, got, g_in, g_out, ksum,
    pad, gp, kb, frame, fw, fe, strips, wmine, wpart, wnode, wall, kacc, kmine, kpart, kwide, kall,
    bsend, brecv, s1, r1, s2, r2, s3, r3, s4, r4, s5, r5, s6, r6,
):
    n = lax.axis_index("node")
    w = lax.axis_index("wide")
    peers = border_peers(n, w)
    wide_peers = [(k, lax.rem(w + k, WIDE)) for k in range(1, WIDE)]
    node_peers = [(k, lax.rem(n + k, NODE)) for k in range(1, NODE)]
    greet = [(n, v) for _, v in wide_peers] + [(v, w) for _, v in node_peers]
    greet += [device for slot, _, device in peers if slot > 2 and slot not in (3, 7, 11)]
    barrier = pltpu.get_barrier_semaphore()
    for device in greet:
        pl.semaphore_signal(barrier, inc=1, device_id=device, device_id_type=MESH)

    def send(src, dst, send_sem, recv_sem, device):
        copy = pltpu.make_async_remote_copy(
            src_ref=src,
            dst_ref=dst,
            send_sem=send_sem,
            recv_sem=recv_sem,
            device_id=device,
            device_id_type=MESH,
        )
        copy.start()
        return copy

    for k in range(4):
        here = slice(k * C, (k + 1) * C)
        wmine[here, :] = (gwi[:, here] * GRAD_SCALE).astype(BF16)
        wmine[HID + k * C : HID + (k + 1) * C, :] = (gwo[:, here] * GRAD_SCALE).astype(BF16)
    pl.semaphore_wait(barrier, len(greet))
    first = []
    for k, v in wide_peers:
        src = wmine.at[pl.ds(pl.multiple_of(v * 32, 32), 32)]
        first.append(send(src, wpart.at[k], s1.at[k], r1.at[k], (n, v)))

    broadcast_taps(k49, kb)
    clear_margins(gp)

    def fill(i, carry):
        o = pl.multiple_of((i + 3) * PITCH + 8, 8)
        here = pl.ds(pl.multiple_of(i * TS, 32), TS)
        gp[pl.ds(o, TS), :] = gsrc[here, :].astype(F32)
        pad[pl.ds(o, TS), :] = field[here, :].astype(F32)
        return carry

    lax.fori_loop(0, TS, fill, 0)

    def frame_rows(jb, carry):
        j0 = pl.multiple_of(jb * 8, 8)
        for f, p in enumerate((0, 1, 2, 99, 100, 101)):
            total = None
            for a in range(7):
                if 0 <= p - a < TS:
                    for b in range(7):
                        v = kb[7 * a + b] * gp[pl.ds((p - a + 3) * PITCH + j0 + 8 - b, 8), :]
                        total = v if total is None else total + v
            frame[f, pl.ds(j0, 8), :] = total
        return carry

    lax.fori_loop(0, 13, frame_rows, 0)

    def frame_cols(i, carry):
        p = i + 3
        for side, taps, q0 in ((fw, (0, 1, 2), 0), (fe, (4, 5, 6), 96)):
            total = None
            for a in range(7):
                for b in taps:
                    v = kb[7 * a + b] * gp[pl.ds((p - a + 3) * PITCH + q0 + 8 - b, 8), :]
                    total = v if total is None else total + v
            side[pl.ds(pl.multiple_of(p * 8, 8), 8), :] = total
        return carry

    lax.fori_loop(0, TS, frame_cols, 0)
    for f, p in enumerate((0, 1, 2, 99, 100, 101)):
        fw[p * 8 : p * 8 + 8, :] = frame[f, 0:8, :]
        fe[p * 8 : p * 8 + 8, :] = frame[f, 96:104, :]
    fw[PADROWS * 8 :, :] = jnp.zeros((80, C), F32)
    fe[PADROWS * 8 :, :] = jnp.zeros((80, C), F32)
    for q in range(3):
        here = pl.ds(q * PITCH, PITCH)
        strips[3, here, :] = fw[pl.ds(q, PITCH, stride=8), :].astype(BF16)
        strips[4, here, :] = fe[pl.ds(3 + q, PITCH, stride=8), :].astype(BF16)
        here = pl.ds(q * TS, TS)
        south = frame[q, 3 : 3 + TS, :]
        north = frame[3 + q, 3 : 3 + TS, :]
        strips[5, here, :] = north.astype(BF16)
        for k in range(3):
            strips[k, here, :] = jnp.where(north_of[4 + k : 5 + k, :] > 0, south, north).astype(BF16)
    borders = []
    for slot, source, device in peers:
        size = BAND if source in (3, 4) else STRIP
        borders.append(
            send(
                strips.at[source, pl.ds(0, size)],
                got.at[slot, pl.ds(0, size)],
                bsend.at[slot],
                brecv.at[slot],
                device,
            )
        )

    pad[0:BAND, :] = hs[...]
    pad[99 * PITCH :, :] = hn[...]

    def sides(i, carry):
        o = pl.multiple_of((i + 3) * PITCH, 8)
        r = pl.multiple_of((i + 3) * 16, 8)
        pad[pl.ds(o, 8), :] = hw[pl.ds(r, 8), :]
        pad[pl.ds(o + 104, 8), :] = he[pl.ds(r + 8, 8), :]
        return carry

    lax.fori_loop(0, TS, sides, 0)
    kmine[48:64, :] = jnp.zeros((16, C), BF16)
    zero = jnp.zeros((8, C), F32)

    def tap_column(b, carry):
        def taps(it, acc):
            i0 = it * 4
            acc = list(acc)
            for jb in range(12):
                g = [gp[pl.ds((i0 + d + 3) * PITCH + 8 + 8 * jb, 8), :] for d in range(4)]
                v = [pad[pl.ds((i0 + r) * PITCH + 8 * jb + 5 + b, 8), :] for r in range(10)]
                for a in range(7):
                    near = (g[0] * v[a] + g[1] * v[a + 1]) + (g[2] * v[a + 2] + g[3] * v[a + 3])
                    acc[a] = acc[a] + near
            return tuple(acc)

        acc = lax.fori_loop(0, 24, taps, (zero,) * 7)
        for a in range(7):
            kacc[pl.ds(7 * a + b, 1), :] = jnp.sum(acc[a], axis=0, keepdims=True)
        return carry

    lax.fori_loop(0, 7, tap_column, 0)
    kacc[49:64, :] = jnp.zeros((15, C), F32)
    kmine[...] = (kacc[...] * GRAD_SCALE).astype(BF16)

    for copy in first:
        copy.wait()
    mine = pl.ds(pl.multiple_of(w * 32, 32), 32)
    total = wmine[mine, :].astype(F32)
    for k in range(1, WIDE):
        total = total + wpart[k].astype(F32)
    wnode[n] = total.astype(BF16)
    second = []
    for k, v in node_peers:
        second.append(send(wnode.at[n], wnode.at[n], s2.at[k], r2.at[k], (v, w)))
        src = kmine.at[pl.ds(pl.multiple_of(v * 16, 16), 16)]
        second.append(send(src, kpart.at[k], s4.at[k], r4.at[k], (v, w)))

    taps_loop(gp, kb, inner, True)

    for copy in second:
        copy.wait()
    total = wnode[0].astype(F32)
    for v in range(1, NODE):
        total = total + wnode[v].astype(F32)
    wall[w] = total.astype(BF16)
    total = kmine[pl.ds(pl.multiple_of(n * 16, 16), 16), :].astype(F32)
    for k in range(1, NODE):
        total = total + kpart[k].astype(F32)
    kwide[w] = total.astype(BF16)
    third = []
    for k, v in wide_peers:
        third.append(send(wall.at[w], wall.at[w], s3.at[k], r3.at[k], (n, v)))
        third.append(send(kwide.at[w], kwide.at[w], s5.at[k], r5.at[k], (n, v)))
    for copy in third:
        copy.wait()
    total = kwide[0].astype(F32)
    for v in range(1, WIDE):
        total = total + kwide[v].astype(F32)
    kall[n] = total.astype(BF16)
    fourth = []
    for k, v in node_peers:
        fourth.append(send(kall.at[n], kall.at[n], s6.at[k], r6.at[k], (v, w)))
    for v in range(16):
        g_in[(v % 4) * 32 : (v % 4 + 1) * 32, (v // 4) * C : (v // 4 + 1) * C] = wall[v].astype(F32)
    for k in range(4):
        block = jnp.concatenate([wall[16 + 4 * k + v] for v in range(4)], axis=0)
        g_out[k * C : (k + 1) * C, :] = block.astype(F32).T
    for copy in fourth:
        copy.wait()
    for v in range(3):
        ksum[v * 16 : (v + 1) * 16, :] = kall[v].astype(F32)
    ksum[48:49, :] = kall[3].astype(F32)[0:1, :]
    for copy in borders:
        copy.wait()


def back_call(gsrc, field, hw, he, hs, hn, k49, north_of, gwi, gwo):
    vmem = pl.BlockSpec(memory_space=pltpu.VMEM)
    dma = pltpu.SemaphoreType.DMA
    return pl.pallas_call(
        back_kernel,
        out_shape=(
            jax.ShapeDtypeStruct((CELLS, C), F32),
            jax.ShapeDtypeStruct((15, BAND, C), BF16),
            jax.ShapeDtypeStruct((C, HID), F32),
            jax.ShapeDtypeStruct((HID, C), F32),
            jax.ShapeDtypeStruct((49, C), F32),
        ),
        in_specs=[vmem] * 10,
        out_specs=(vmem,) * 5,
        scratch_shapes=[
            pltpu.VMEM((PADROWS * PITCH, C), F32),
            pltpu.VMEM((PADROWS * PITCH, C), F32),
            pltpu.VMEM((49, 8, C), F32),
            pltpu.VMEM((6, 104, C), F32),
            pltpu.VMEM((PITCH * 8, C), F32),
            pltpu.VMEM((PITCH * 8, C), F32),
            pltpu.VMEM((6, BAND, C), BF16),
            pltpu.VMEM((8 * C, C), BF16),
            pltpu.VMEM((WIDE, 32, C), BF16),
            pltpu.VMEM((NODE, 32, C), BF16),
            pltpu.VMEM((WIDE, 32, C), BF16),
            pltpu.VMEM((64, C), F32),
            pltpu.VMEM((64, C), BF16),
            pltpu.VMEM((NODE, 16, C), BF16),
            pltpu.VMEM((WIDE, 16, C), BF16),
            pltpu.VMEM((NODE, 16, C), BF16),
            dma((15,)), dma((15,)),
            dma((WIDE,)), dma((WIDE,)),
            dma((NODE,)), dma((NODE,)),
            dma((WIDE,)), dma((WIDE,)),
            dma((NODE,)), dma((NODE,)),
            dma((WIDE,)), dma((WIDE,)),
            dma((NODE,)), dma((NODE,)),
        ],
        compiler_params=pltpu.CompilerParams(
            collective_id=1, has_side_effects=True, vmem_limit_bytes=VMEM_LIMIT
        ),
        name="back",
    )(gsrc, field, hw, he, hs, hn, k49, north_of, gwi, gwo)


def final_kernel(pick, got, inner, cot, wc, out, cw, ce, low, top, strip, sb):
    step = pl.program_id(0)

    @pl.when(step == 0)
    def _():
        cw[...] = jnp.zeros_like(cw)
        ce[...] = jnp.zeros_like(ce)

        def chosen(direction, start, size):
            v = got[pick[0, direction], pl.ds(start, size), :].astype(F32)
            return jnp.where(pick[1, direction] > 0, v, 0.0)

        for side, (mid, north, south), col in ((cw, (2, 4, 6), 0), (ce, (3, 5, 7), 5)):
            for q in range(3):
                strip[0] = chosen(mid, q * PITCH, PITCH)
                strip[1] = chosen(north, q * PITCH, PITCH)
                strip[2] = chosen(south, q * PITCH, PITCH)
                strip[0, TS : TS + 3, :] += strip[1, 0:3, :]
                strip[0, 3:6, :] += strip[2, TS + 3 : TS + 6, :]
                side[pl.ds(col + q, TS, stride=8), :] = strip[0, 3 : TS + 3, :]
        i0 = lax.broadcasted_iota(jnp.int32, (TS, TS), 0)
        i1 = lax.broadcasted_iota(jnp.int32, (TS, TS), 1)
        turn = (i0 + i1 == TS - 1).astype(BF16)
        for q in range(3):
            low[q * TS : (q + 1) * TS, :] = chosen(1, q * TS, TS)
            flipped = mm(turn, got[pick[2, 0], (2 - q) * TS : (3 - q) * TS, :])
            north = jnp.where(pick[3, 0] > 0, flipped, chosen(0, q * TS, TS))
            top[q * TS : (q + 1) * TS, :] = jnp.where(pick[1, 0] > 0, north, 0.0)

    sb[...] = inner[...]
    for r in range(8):
        row = pl.multiple_of((step * 8 + r) * 8, 8)
        sb[r * TS : r * TS + 8, :] += cw[pl.ds(row, 8), :]
        sb[r * TS + 88 : r * TS + 96, :] += ce[pl.ds(row, 8), :]

    @pl.when(step == 0)
    def _():
        sb[0:STRIP, :] += low[...]

    @pl.when(step == 11)
    def _():
        sb[5 * TS :, :] += top[...]

    out[...] = (cot[...].astype(F32) + wc[...] * sb[...].T).astype(BF16)


def final_call(pick, got, inner, cot, wc):
    rows = pl.BlockSpec((BLOCK, C), lambda i, p: (i, 0))
    cols = pl.BlockSpec((C, BLOCK), lambda i, p: (0, i))
    lane = pl.BlockSpec((1, BLOCK), lambda i, p: (0, i))
    return pl.pallas_call(
        final_kernel,
        out_shape=jax.ShapeDtypeStruct((C, CELLS), BF16),
        grid_spec=pltpu.PrefetchScalarGridSpec(
            num_scalar_prefetch=1,
            grid=(CELLS // BLOCK,),
            in_specs=[pl.BlockSpec((15, BAND, C), lambda i, p: (0, 0, 0)), rows, cols, lane],
            out_specs=cols,
            scratch_shapes=[
                pltpu.VMEM((TS * 8, C), F32),
                pltpu.VMEM((TS * 8, C), F32),
                pltpu.VMEM((STRIP, C), F32),
                pltpu.VMEM((STRIP, C), F32),
                pltpu.VMEM((3, PITCH, C), F32),
                pltpu.VMEM((BLOCK, C), F32),
            ],
        ),
        compiler_params=pltpu.CompilerParams(vmem_limit_bytes=VMEM_LIMIT),
        name="final",
    )(pick, got, inner, cot, wc)


def local(
    features,
    cotangent,
    wet_fraction,
    slot_tile,
    neighbours,
    kernel,
    norm_gain,
    weight_in,
    bias_in,
    weight_out,
    layer_scale,
):
    feat = features.reshape(C, CELLS)
    cot = cotangent.reshape(C, CELLS)
    conv0, field, got, wc, rmet, pick = halo_call(
        feat, wet_fraction, kernel, slot_tile, neighbours
    )
    updated, gsrc, gwi, gwo, hw, he, hs, hn = mlp_call(
        pick, got, conv0, feat, cot, wet_fraction, rmet, kernel, norm_gain, weight_in, bias_in,
        weight_out, layer_scale,
    )
    inner, back_got, grad_in, grad_out, ksum = back_call(
        gsrc, field, hw, he, hs, hn, kernel, pick, gwi, gwo
    )
    grad_features = final_call(pick, back_got, inner, cot, wc)
    return (
        updated.reshape(1, C, CELLS),
        grad_features.reshape(1, C, CELLS),
        grad_in,
        grad_out,
        ksum,
    )


def solution(mesh):
    shards = P(("node", "wide"), None, None)
    in_specs = (shards, shards, P(("node", "wide"), None)) + (P(),) * 8
    out_specs = (shards, shards, P(), P(), P())
    return jax.shard_map(local, mesh=mesh, in_specs=in_specs, out_specs=out_specs, check_vma=False)
```

```python
import math

import jax
import jax.numpy as jnp
from jax import lax
from jax.experimental import pallas as pl
from jax.experimental.pallas import tpu as pltpu
from jax.sharding import PartitionSpec as P

C = 128
HID = 512
TS = 96
CELLS = TS * TS
NODE = 4
WIDE = 32
PITCH = 112
PADROWS = TS + 6
STRIP = 3 * TS
BAND = 3 * PITCH
BLOCK = 768
CHUNK = 256
EPS = 1e-06
GELU_COEF = 0.7978845608028654
CUBIC = 0.044715
GRAD_SCALE = 1.0 / math.sqrt(NODE * WIDE * CELLS)
MESH = pl.DeviceIdType.MESH
F32 = jnp.float32
BF16 = jnp.bfloat16
VMEM_LIMIT = 60 * 2**20


def border_peers(n, w):
    out = []
    for k in range(1, 4):
        out.append((k - 1, k - 1, (lax.rem(n + k, 4), w)))
    sides = ((3, 3, lax.rem(w + 31, 32)), (7, 4, lax.rem(w + 1, 32)), (11, 5, 31 - w))
    for base, source, column in sides:
        for k in range(4):
            out.append((base + k, source, (lax.rem(n + k, 4), column)))
    return out


def broadcast_taps(k49, kb):
    for t in range(49):
        kb[t] = jnp.broadcast_to(k49[t : t + 1, :], (8, C))


def taps_columns(src, kb, out, flip, low, high):
    def body(it, carry):
        b = it // 12
        i0 = lax.rem(it, 12) * 8
        taps = [kb[48 - 7 * a - b] if flip else kb[7 * a + b] for a in range(7)]
        for jb in range(12):
            base = i0 * PITCH + 8 * jb + 5 + b
            v = [src[pl.ds(base + r * PITCH, 8), :] for r in range(14)]
            for d in range(8):
                total = taps[0] * v[d]
                for a in range(1, 7):
                    total = total + taps[a] * v[d + a]
                o = pl.ds(pl.multiple_of((i0 + d) * TS + 8 * jb, 8), 8)
                out[o, :] = out[o, :] + total
        return carry

    lax.fori_loop(low * 12, high * 12, body, 0)


def clear_rows(out):
    zero = jnp.zeros((TS, C), F32)

    def body(i, carry):
        out[pl.ds(pl.multiple_of(i * TS, 8), TS), :] = zero
        return carry

    lax.fori_loop(0, TS, body, 0)


def clear_margins(pad):
    zero8 = jnp.zeros((8, C), F32)
    zero_row = jnp.zeros((PITCH, C), F32)
    for r in (0, 1, 2, 99, 100, 101):
        pad[r * PITCH : (r + 1) * PITCH, :] = zero_row

    def body(i, carry):
        o = pl.multiple_of((i + 3) * PITCH, 8)
        pad[pl.ds(o, 8), :] = zero8
        pad[pl.ds(o + 104, 8), :] = zero8
        return carry

    lax.fori_loop(0, TS, body, 0)


def cosine(x):
    x2 = x * x
    total = jnp.full_like(x, 1.0 / math.factorial(16))
    for k in range(7, -1, -1):
        total = total * x2 + (-1.0) ** k / math.factorial(2 * k)
    return total


def nt(a, b):
    return lax.dot_general(a, b, (((1,), (1,)), ((), ())), preferred_element_type=F32)


def mm(a, b):
    return jnp.dot(a, b, preferred_element_type=F32)


def wide2(column):
    return jnp.concatenate([column, column], axis=1)


def find_neighbours(n, w, slot_tile, neighbours):
    tile = slot_tile[n * WIDE + w]
    known = jnp.maximum(tile, 0)
    columns = {0: w, 3: lax.rem(w + 1, 32), 7: lax.rem(w + 31, 32), 11: 31 - w}
    held = {key: [slot_tile[k * WIDE + col] for k in range(4)] for key, col in columns.items()}
    bases = (0, 0, 7, 3, 7, 3, 7, 3)
    slots, present, targets = [], [], []

    def find(base, target):
        slot = jnp.int32(0)
        for k in range(4):
            away = lax.rem(n + 4 - k, 4)
            here = jnp.maximum(away - 1, 0) if base == 0 else base + away
            slot = jnp.where(held[base][k] == target, here, slot)
        return slot

    for d in range(8):
        near = jnp.where(tile >= 0, neighbours[known * 8 + d], -1)
        present.append(near >= 0)
        targets.append(jnp.maximum(near, 0) >> 1)
        slots.append(find(bases[d], targets[d]))
        if d == 0:
            flip = near & 1
    mirror = find(11, targets[0])
    north_of = []
    for k in range(1, 4):
        other = slot_tile[lax.rem(n + k, 4) * WIDE + w]
        north_of.append(present[1] & (other == targets[1]))
    return known, slots, present, mirror, present[0] & (flip == 1), north_of


def block_kernel(
    feat_hbm, cot_hbm, wet, k49, slot_tile, neighbours, gain_row, w_in, bias_row, w_out, scale_row,
    updated_hbm, grad_hbm, g_in, g_out, ksum,
    feat, cot, updated, grad, wc, rmet, pad, gp, cells, kb, strips, got, hw, he, hs, hn, strip,
    gain, scale, bias, w_in_t, w_out_t, gwi, gwo, frame, fw, fe, back_strips, back_got, cw, ce,
    kx, wmine, part8, mine4, part4, nodes, all4, wall,
    in_sem, up_sem, gr_sem, fsend, frecv, bsend, brecv, s1, r1, s2, r2, s3, r3, s4, r4, s5, r5,
):
    n = lax.axis_index("node")
    w = lax.axis_index("wide")
    x = w // 8
    z = lax.rem(w, 8)
    peers = border_peers(n, w)
    z_peers = [(k, lax.rem(z + k, 8)) for k in range(1, 8)]
    x_peers = [(k, lax.rem(x + k, 4)) for k in range(1, 4)]
    n_peers = [(k, lax.rem(n + k, 4)) for k in range(1, 4)]
    greet = [device for _, _, device in peers]
    greet += [(n, x * 8 + v) for _, v in z_peers] + [(n, v * 8 + z) for _, v in x_peers]
    barrier = pltpu.get_barrier_semaphore()
    for device in greet:
        pl.semaphore_signal(barrier, inc=1, device_id=device, device_id_type=MESH)
    fetch = [
        pltpu.make_async_copy(feat_hbm, feat, in_sem.at[0]),
        pltpu.make_async_copy(cot_hbm, cot, in_sem.at[1]),
    ]
    for copy in fetch:
        copy.start()

    def send(src, dst, send_sem, recv_sem, device):
        copy = pltpu.make_async_remote_copy(
            src_ref=src,
            dst_ref=dst,
            send_sem=send_sem,
            recv_sem=recv_sem,
            device_id=device,
            device_id_type=MESH,
        )
        copy.start()
        return copy

    known, slots, present, mirror, folded, north_of = find_neighbours(n, w, slot_tile, neighbours)
    broadcast_taps(k49, kb)
    clear_margins(pad)
    clear_margins(gp)
    clear_rows(cells)
    cell = lax.broadcasted_iota(jnp.int32, (1, 384), 1)
    sub_row = jnp.where(cell >= 96, 1.0, 0.0) + jnp.where(cell >= 192, 1.0, 0.0)
    sub_row = sub_row + jnp.where(cell >= 288, 1.0, 0.0)
    first_row = ((known >> 5) * TS).astype(F32) + 0.5
    fetch[0].wait()

    def prep(g, carry):
        here = pl.ds(pl.multiple_of(g * 384, 128), 384)
        latitude = -80.0 + 160.0 * (sub_row + ((g * 4).astype(F32) + first_row)) / float(8 * TS)
        metric = cosine(latitude * (math.pi / 180.0))
        weight = wet[:, here] * metric
        wc[:, here] = weight
        rmet[:, here] = 1.0 / metric
        t = (feat[:, here].astype(F32) * weight).astype(BF16).astype(F32).T
        for r in range(4):
            row = pl.multiple_of((g * 4 + r + 3) * PITCH + 8, 8)
            pad[pl.ds(row, TS), :] = t[r * TS : (r + 1) * TS]
        return carry

    lax.fori_loop(0, 2, lambda g, carry: prep(g * 23, carry), 0)
    for q in range(3):
        here = pl.ds(q * TS, TS)
        south = pad[pl.ds((3 + q) * PITCH + 8, TS), :]
        north = pad[pl.ds((96 + q) * PITCH + 8, TS), :]
        strips[5, here, :] = north.astype(BF16)
        for k in range(3):
            strips[k, here, :] = jnp.where(north_of[k], south, north).astype(BF16)
    pl.semaphore_wait(barrier, len(greet))
    copies = []

    def send_strips(sources):
        for slot, source, device in peers:
            if source in sources:
                copies.append(
                    send(strips.at[source], got.at[slot], fsend.at[slot], frecv.at[slot], device)
                )

    send_strips((0, 1, 2, 5))
    lax.fori_loop(1, 23, prep, 0)
    for q in range(3):
        here = pl.ds(q * TS, TS)
        strips[3, here, :] = pad[pl.ds(3 * PITCH + 8 + q, TS, stride=PITCH), :].astype(BF16)
        strips[4, here, :] = pad[pl.ds(3 * PITCH + 101 + q, TS, stride=PITCH), :].astype(BF16)
    send_strips((3, 4))

    taps_columns(pad, kb, cells, False, 0, 7)
    gain[...] = jnp.broadcast_to(gain_row[...], (C, C)).T
    scale[...] = jnp.broadcast_to(scale_row[...], (C, C)).T
    for k in range(4):
        here = slice(k * C, (k + 1) * C)
        bias[here, :] = jnp.broadcast_to(bias_row[:, here], (C, C)).T
        w_in_t[here, :] = w_in[:, here].astype(F32).T.astype(BF16)
        w_out_t[:, here] = w_out[here, :].astype(F32).T.astype(BF16)
    gwi[...] = jnp.zeros_like(gwi)
    gwo[...] = jnp.zeros_like(gwo)
    hw[...] = jnp.zeros_like(hw)
    he[...] = jnp.zeros_like(he)
    i0 = lax.broadcasted_iota(jnp.int32, (TS, TS), 0)
    i1 = lax.broadcasted_iota(jnp.int32, (TS, TS), 1)
    turn = (i0 + i1 == TS - 1).astype(BF16)
    for copy in copies:
        copy.wait()

    def chosen(direction, q):
        v = got[slots[direction], pl.ds(q * TS, TS), :].astype(F32)
        return jnp.where(present[direction], v, 0.0)

    for side, (mid, top, low), col in ((hw, (2, 4, 6), 5), (he, (3, 5, 7), 8)):
        for q in range(3):
            strip[0:TS, :] = chosen(low, q)
            strip[0:3, :] = strip[TS - 3 : TS, :]
            strip[3 : TS + 3, :] = chosen(mid, q)
            strip[112 : 112 + TS, :] = chosen(top, q)
            strip[TS + 3 : TS + 6, :] = strip[112:115, :]
            side[pl.ds(col + q, PADROWS, stride=16), :] = strip[0:PADROWS, :]
    for q in range(3):
        o = q * PITCH
        hs[o + 8 : o + 104, :] = chosen(1, q)
        hs[o : o + 8, :] = hw[q * 16 : q * 16 + 8, :]
        hs[o + 104 : o + 112, :] = he[q * 16 + 8 : q * 16 + 16, :]
        flipped = mm(turn, got[mirror, pl.ds((2 - q) * TS, TS), :])
        north = jnp.where(folded, flipped, chosen(0, q))
        hn[o + 8 : o + 104, :] = jnp.where(present[0], north, 0.0)
        r = (TS + 3 + q) * 16
        hn[o : o + 8, :] = hw[r : r + 8, :]
        hn[o + 104 : o + 112, :] = he[r + 8 : r + 16, :]
    pad[0:BAND, :] = hs[...]
    pad[99 * PITCH :, :] = hn[...]

    def rim(rows, pairs):
        def body(jb, carry):
            j0 = pl.multiple_of(jb * 8, 8)
            for d, terms in pairs:
                o = pl.ds(pl.multiple_of(d * TS + j0, 8), 8)
                total = cells[o, :]
                for a, r in terms:
                    part = None
                    for b in range(7):
                        v = kb[7 * a + b] * rows[pl.ds(r * PITCH + j0 + 5 + b, 8), :]
                        part = v if part is None else part + v
                    total = total + part
                cells[o, :] = total
            return carry

        lax.fori_loop(0, 12, body, 0)

    rim(hs, [(i, [(a, i + a) for a in range(3 - i)]) for i in range(3)])
    rim(hn, [(93 + i, [(a, i + a - 6) for a in range(6 - i, 7)]) for i in range(3)])

    def sides(i, carry):
        p = pl.multiple_of((i + 3) * PITCH, 8)
        r = pl.multiple_of((i + 3) * 16, 8)
        pad[pl.ds(p, 8), :] = hw[pl.ds(r, 8), :]
        pad[pl.ds(p + 104, 8), :] = he[pl.ds(r + 8, 8), :]
        for side, taps, shift, col in ((hw, (0, 1, 2), 5, 0), (he, (4, 5, 6), -3, 88)):
            o = pl.ds(pl.multiple_of(i * TS + col, 8), 8)
            total = cells[o, :]
            for a in range(7):
                row = i + a
                inside = jnp.logical_and(row >= 3, row < TS + 3).astype(F32)
                part = None
                for b in taps:
                    v = kb[7 * a + b] * side[pl.ds(row * 16 + b + shift, 8), :]
                    part = v if part is None else part + v
                total = total + part * inside
            cells[o, :] = total
        return carry

    lax.fori_loop(0, TS, sides, 0)
    fetch[1].wait()

    def mlp_block(step, carry):
        for c in range(BLOCK // CHUNK):
            here = pl.ds(pl.multiple_of(step * BLOCK + c * CHUNK, CHUNK), CHUNK)
            rm = rmet[:, here]
            conv = cells[here, :].T * rm
            centred = conv - jnp.mean(conv, axis=0, keepdims=True)
            inv_std = lax.rsqrt(jnp.mean(centred * centred, axis=0, keepdims=True) + EPS)
            normed = centred * inv_std
            g2 = wide2(gain[...])
            normed_bf = (normed * g2).astype(BF16)
            hidden = mm(w_in_t[...], normed_bf) + wide2(bias[...])
            sq = hidden * hidden
            t = jnp.tanh(hidden * (GELU_COEF + (GELU_COEF * CUBIC) * sq))
            p = 0.5 + 0.5 * t
            active = hidden * p
            active_bf = active.astype(BF16)
            mixed = mm(w_out_t[...], active_bf)
            ms = wet[:, here] * wide2(scale[...])
            updated[:, here] = (feat[:, here].astype(F32) + ms * mixed).astype(BF16)
            gm = (ms * cot[:, here].astype(F32)).astype(BF16)
            slope = p + active * (1.0 - p) * (2.0 * GELU_COEF + (6.0 * GELU_COEF * CUBIC) * sq)
            gh = (mm(w_out[...], gm) * slope).astype(BF16)
            gn = mm(w_in[...], gh) * g2
            gwo[...] += nt(gm, active_bf)
            gwi[...] += nt(normed_bf, gh)
            gc = inv_std * (
                gn
                - jnp.mean(gn, axis=0, keepdims=True)
                - normed * jnp.mean(gn * normed, axis=0, keepdims=True)
            )
            gs = (gc * rm).T.astype(BF16).astype(F32)
            for r in range(8):
                low, high = max(c * CHUNK, r * TS), min((c + 1) * CHUNK, (r + 1) * TS)
                if low < high:
                    o = pl.multiple_of((step * 8 + r + 3) * PITCH + 8 + low - r * TS, 8)
                    gp[pl.ds(o, high - low), :] = gs[low - c * CHUNK : high - c * CHUNK]
        return carry

    lax.fori_loop(0, CELLS // BLOCK, mlp_block, 0)
    out_updated = pltpu.make_async_copy(updated, updated_hbm, up_sem)
    out_updated.start()

    def frame_rows(jb, carry):
        j0 = pl.multiple_of(jb * 8, 8)
        for f, p in enumerate((0, 1, 2, 99, 100, 101)):
            total = None
            for a in range(7):
                if 0 <= p - a < TS:
                    for b in range(7):
                        v = kb[7 * a + b] * gp[pl.ds((p - a + 3) * PITCH + j0 + 8 - b, 8), :]
                        total = v if total is None else total + v
            frame[f, pl.ds(j0, 8), :] = total
        return carry

    lax.fori_loop(0, 13, frame_rows, 0)

    def frame_cols(i, carry):
        p = i + 3
        for side, taps, q0 in ((fw, (0, 1, 2), 0), (fe, (4, 5, 6), 96)):
            total = None
            for a in range(7):
                for b in taps:
                    v = kb[7 * a + b] * gp[pl.ds((p - a + 3) * PITCH + q0 + 8 - b, 8), :]
                    total = v if total is None else total + v
            side[pl.ds(pl.multiple_of(p * 8, 8), 8), :] = total
        return carry

    lax.fori_loop(0, TS, frame_cols, 0)
    for f, p in enumerate((0, 1, 2, 99, 100, 101)):
        fw[p * 8 : p * 8 + 8, :] = frame[f, 0:8, :]
        fe[p * 8 : p * 8 + 8, :] = frame[f, 96:104, :]
    fw[PADROWS * 8 :, :] = jnp.zeros((80, C), F32)
    fe[PADROWS * 8 :, :] = jnp.zeros((80, C), F32)
    for q in range(3):
        here = pl.ds(q * PITCH, PITCH)
        back_strips[3, here, :] = fw[pl.ds(q, PITCH, stride=8), :].astype(BF16)
        back_strips[4, here, :] = fe[pl.ds(3 + q, PITCH, stride=8), :].astype(BF16)
        here = pl.ds(q * TS, TS)
        south = frame[q, 3 : 3 + TS, :]
        north = frame[3 + q, 3 : 3 + TS, :]
        back_strips[5, here, :] = north.astype(BF16)
        for k in range(3):
            back_strips[k, here, :] = jnp.where(north_of[k], south, north).astype(BF16)
    borders = []
    for slot, source, device in peers:
        size = BAND if source in (3, 4) else STRIP
        borders.append(
            send(
                back_strips.at[source, pl.ds(0, size)],
                back_got.at[slot, pl.ds(0, size)],
                bsend.at[slot],
                brecv.at[slot],
                device,
            )
        )

    kx[...] = jnp.zeros_like(kx)
    zero = jnp.zeros((8, C), F32)

    def tap_column(b, carry):
        def taps(it, acc):
            i0 = it * 4
            acc = list(acc)
            for jb in range(12):
                g = [gp[pl.ds((i0 + d + 3) * PITCH + 8 + 8 * jb, 8), :] for d in range(4)]
                v = [pad[pl.ds((i0 + r) * PITCH + 8 * jb + 5 + b, 8), :] for r in range(10)]
                for a in range(7):
                    near = (g[0] * v[a] + g[1] * v[a + 1]) + (g[2] * v[a + 2] + g[3] * v[a + 3])
                    acc[a] = acc[a] + near
            return tuple(acc)

        acc = lax.fori_loop(0, 24, taps, (zero,) * 7)
        for a in range(7):
            t = 7 * a + b
            row = (t // 2) * 16 + lax.rem(t, 2)
            kx[pl.ds(row, 1), :] = jnp.sum(acc[a], axis=0, keepdims=True)
        return carry

    lax.fori_loop(0, 7, tap_column, 0)

    for c in range(32):
        acc = gwi if c < 16 else gwo
        part = acc[(c % 4) * 32 : (c % 4 + 1) * 32, (c // 4 % 4) * C : (c // 4 % 4 + 1) * C]
        wmine[c * 48 : c * 48 + 32, :] = (part * GRAD_SCALE).astype(BF16)
        wmine[c * 48 + 32 : c * 48 + 48, :] = (kx[c * 16 : c * 16 + 16, :] * GRAD_SCALE).astype(BF16)
    stage = []
    for k, v in z_peers:
        src = wmine.at[pl.ds(pl.multiple_of(v * 192, 64), 192)]
        stage.append(send(src, part8.at[k], s1.at[k], r1.at[k], (n, x * 8 + v)))
    clear_rows(cells)
    taps_columns(gp, kb, cells, True, 0, 2)
    for copy in stage:
        copy.wait()
    total = wmine[pl.ds(pl.multiple_of(z * 192, 64), 192), :].astype(F32)
    for k in range(1, 8):
        total = total + part8[k].astype(F32)
    mine4[...] = total
    stage = []
    for k, v in x_peers:
        src = mine4.at[pl.ds(pl.multiple_of(v * 48, 16), 48)]
        stage.append(send(src, part4.at[k], s2.at[k], r2.at[k], (n, v * 8 + z)))
    taps_columns(gp, kb, cells, True, 2, 3)
    for copy in stage:
        copy.wait()
    total = mine4[pl.ds(pl.multiple_of(x * 48, 16), 48), :]
    for k in range(1, 4):
        total = total + part4[k]
    nodes[n] = total
    stage = []
    for k, v in n_peers:
        stage.append(send(nodes.at[n], nodes.at[n], s3.at[k], r3.at[k], (v, w)))
    taps_columns(gp, kb, cells, True, 3, 4)
    for copy in stage:
        copy.wait()
    all4[x] = ((nodes[0] + nodes[1]) + (nodes[2] + nodes[3])).astype(BF16)
    stage = []
    for k, v in x_peers:
        stage.append(send(all4.at[x], all4.at[x], s4.at[k], r4.at[k], (n, v * 8 + z)))
    taps_columns(gp, kb, cells, True, 4, 5)
    for copy in stage:
        copy.wait()
    for v in range(4):
        wall[z, v * 48 : (v + 1) * 48, :] = all4[v]
    stage = []
    for k, v in z_peers:
        stage.append(send(wall.at[z], wall.at[z], s5.at[k], r5.at[k], (n, x * 8 + v)))
    taps_columns(gp, kb, cells, True, 5, 7)
    for copy in borders:
        copy.wait()

    cw[...] = jnp.zeros_like(cw)
    ce[...] = jnp.zeros_like(ce)

    def received(direction, start, size):
        v = back_got[slots[direction], pl.ds(start, size), :].astype(F32)
        return jnp.where(present[direction], v, 0.0)

    for side, (mid, north, south), col in ((cw, (2, 4, 6), 0), (ce, (3, 5, 7), 5)):
        for q in range(3):
            strip[0:PITCH, :] = received(mid, q * PITCH, PITCH)
            strip[PITCH : 2 * PITCH, :] = received(north, q * PITCH, PITCH)
            strip[2 * PITCH :, :] = received(south, q * PITCH, PITCH)
            strip[TS : TS + 3, :] += strip[PITCH : PITCH + 3, :]
            strip[3:6, :] += strip[2 * PITCH + TS + 3 : 2 * PITCH + TS + 6, :]
            side[pl.ds(col + q, TS, stride=8), :] = strip[3 : TS + 3, :]
    for q in range(3):
        cells[q * TS : (q + 1) * TS, :] += received(1, q * TS, TS)
        flipped = mm(turn, back_got[mirror, pl.ds((2 - q) * TS, TS), :])
        north = jnp.where(folded, flipped, received(0, q * TS, TS))
        cells[(93 + q) * TS : (94 + q) * TS, :] += jnp.where(present[0], north, 0.0)

    def finish(step, carry):
        for r in range(8):
            i = step * 8 + r
            o = pl.multiple_of(i * TS, 8)
            row = pl.multiple_of(i * 8, 8)
            cells[pl.ds(o, 8), :] += cw[pl.ds(row, 8), :]
            cells[pl.ds(o + 88, 8), :] += ce[pl.ds(row, 8), :]
        here = pl.ds(pl.multiple_of(step * BLOCK, BLOCK), BLOCK)
        whole = cot[:, here].astype(F32) + wc[:, here] * cells[here, :].T
        grad[:, here] = whole.astype(BF16)
        return carry

    lax.fori_loop(0, CELLS // BLOCK, finish, 0)
    out_grad = pltpu.make_async_copy(grad, grad_hbm, gr_sem)
    out_grad.start()
    for copy in stage:
        copy.wait()
    for c in range(32):
        rows = slice((c % 4) * 48, (c % 4) * 48 + 32)
        if c < 16:
            g_in[(c % 4) * 32 : (c % 4 + 1) * 32, (c // 4) * C : (c // 4 + 1) * C] = wall[
                c // 4, rows, :
            ].astype(F32)
        elif c % 4 == 0:
            block = jnp.concatenate(
                [wall[c // 4, v * 48 : v * 48 + 32, :] for v in range(4)], axis=0
            )
            g_out[(c // 4 - 4) * C : (c // 4 - 3) * C, :] = block.astype(F32).T
        if c < 25:
            size = min(2, 49 - 2 * c)
            pair = wall[c // 4, (c % 4) * 48 + 32 : (c % 4) * 48 + 48, :].astype(F32)
            ksum[2 * c : 2 * c + size, :] = pair[0:size]
    out_updated.wait()
    out_grad.wait()


def block_call(*args):
    vmem = pl.BlockSpec(memory_space=pltpu.VMEM)
    smem = pl.BlockSpec(memory_space=pltpu.SMEM)
    hbm = pl.BlockSpec(memory_space=pl.ANY)
    dma = pltpu.SemaphoreType.DMA
    shapes = [
        ((C, CELLS), BF16), ((C, CELLS), BF16), ((C, CELLS), BF16), ((C, CELLS), BF16),
        ((1, CELLS), F32), ((1, CELLS), F32),
        ((PADROWS * PITCH, C), F32), ((PADROWS * PITCH, C), F32), ((CELLS, C), F32),
        ((49, 8, C), F32), ((6, STRIP, C), BF16), ((15, STRIP, C), BF16),
        ((PADROWS * 16, C), F32), ((PADROWS * 16, C), F32), ((BAND, C), F32), ((BAND, C), F32),
        ((3 * PITCH, C), F32),
        ((C, C), F32), ((C, C), F32), ((HID, C), F32), ((HID, C), BF16), ((C, HID), BF16),
        ((C, HID), F32), ((C, HID), F32),
        ((6, 104, C), F32), ((PITCH * 8, C), F32), ((PITCH * 8, C), F32),
        ((6, BAND, C), BF16), ((15, BAND, C), BF16), ((TS * 8, C), F32), ((TS * 8, C), F32),
        ((512, C), F32), ((1536, C), BF16), ((8, 192, C), BF16), ((192, C), F32),
        ((4, 48, C), F32), ((4, 48, C), F32), ((4, 48, C), BF16), ((8, 192, C), BF16),
    ]
    sems = [dma((2,)), dma, dma, dma((15,)), dma((15,)), dma((15,)), dma((15,))]
    sems += [dma((8,)), dma((8,))] + [dma((4,))] * 6 + [dma((8,)), dma((8,))]
    return pl.pallas_call(
        block_kernel,
        out_shape=(
            jax.ShapeDtypeStruct((C, CELLS), BF16),
            jax.ShapeDtypeStruct((C, CELLS), BF16),
            jax.ShapeDtypeStruct((C, HID), F32),
            jax.ShapeDtypeStruct((HID, C), F32),
            jax.ShapeDtypeStruct((49, C), F32),
        ),
        in_specs=[hbm, hbm, vmem, vmem, smem, smem] + [vmem] * 5,
        out_specs=(hbm, hbm, vmem, vmem, vmem),
        scratch_shapes=[pltpu.VMEM(shape, dtype) for shape, dtype in shapes] + sems,
        compiler_params=pltpu.CompilerParams(
            collective_id=0, has_side_effects=True, vmem_limit_bytes=VMEM_LIMIT
        ),
        name="block",
    )(*args)


def local(
    features,
    cotangent,
    wet_fraction,
    slot_tile,
    neighbours,
    kernel,
    norm_gain,
    weight_in,
    bias_in,
    weight_out,
    layer_scale,
):
    updated, grad_features, grad_in, grad_out, grad_kernel = block_call(
        features.reshape(C, CELLS),
        cotangent.reshape(C, CELLS),
        wet_fraction,
        kernel,
        slot_tile,
        neighbours.reshape(-1),
        norm_gain[None, :],
        weight_in,
        bias_in[None, :],
        weight_out,
        layer_scale[None, :],
    )
    return (
        updated.reshape(1, C, CELLS),
        grad_features.reshape(1, C, CELLS),
        grad_in,
        grad_out,
        grad_kernel,
    )


def solution(mesh):
    shards = P(("node", "wide"), None, None)
    in_specs = (shards, shards, P(("node", "wide"), None)) + (P(),) * 8
    out_specs = (shards, shards, P(), P(), P())
    return jax.shard_map(local, mesh=mesh, in_specs=in_specs, out_specs=out_specs, check_vma=False)
```

```python
import math

import jax
import jax.numpy as jnp
from jax import lax
from jax.experimental import pallas as pl
from jax.experimental.pallas import tpu as pltpu
from jax.sharding import PartitionSpec as P

C = 128
HID = 512
TS = 96
CELLS = TS * TS
NODE = 4
WIDE = 32
PITCH = 112
PADROWS = TS + 6
STRIP = 3 * TS
BAND = 3 * PITCH
BLOCK = 1536
CHUNK = 256
EPS = 1e-06
GELU_COEF = 0.7978845608028654
CUBIC = 0.044715
GRAD_SCALE = 1.0 / math.sqrt(NODE * WIDE * CELLS)
MESH = pl.DeviceIdType.MESH
F32 = jnp.float32
BF16 = jnp.bfloat16
VMEM_LIMIT = 60 * 2**20


def border_peers(n, w):
    out = []
    for k in range(1, 4):
        out.append((k - 1, k - 1, (lax.rem(n + k, 4), w)))
    sides = ((3, 3, lax.rem(w + 31, 32)), (7, 4, lax.rem(w + 1, 32)), (11, 5, 31 - w))
    for base, source, column in sides:
        for k in range(4):
            out.append((base + k, source, (lax.rem(n + k, 4), column)))
    return out


def broadcast_taps(k49, kb):
    for t in range(49):
        kb[t] = jnp.broadcast_to(k49[t : t + 1, :], (8, C))


def taps_columns(src, kb, out, flip, low, high):
    def body(it, carry):
        b = it // 12
        i0 = lax.rem(it, 12) * 8
        taps = [kb[48 - 7 * a - b] if flip else kb[7 * a + b] for a in range(7)]
        for jb in range(12):
            base = i0 * PITCH + 8 * jb + 5 + b
            v = [src[pl.ds(base + r * PITCH, 8), :] for r in range(14)]
            for d in range(8):
                total = taps[0] * v[d]
                for a in range(1, 7):
                    total = total + taps[a] * v[d + a]
                o = pl.ds(pl.multiple_of((i0 + d) * TS + 8 * jb, 8), 8)
                out[o, :] = out[o, :] + total
        return carry

    lax.fori_loop(low * 12, high * 12, body, 0)


def clear_rows(out):
    zero = jnp.zeros((TS, C), F32)

    def body(i, carry):
        out[pl.ds(pl.multiple_of(i * TS, 8), TS), :] = zero
        return carry

    lax.fori_loop(0, TS, body, 0)


def clear_margins(pad):
    zero8 = jnp.zeros((8, C), F32)
    zero_row = jnp.zeros((PITCH, C), F32)
    for r in (0, 1, 2, 99, 100, 101):
        pad[r * PITCH : (r + 1) * PITCH, :] = zero_row

    def body(i, carry):
        o = pl.multiple_of((i + 3) * PITCH, 8)
        pad[pl.ds(o, 8), :] = zero8
        pad[pl.ds(o + 104, 8), :] = zero8
        return carry

    lax.fori_loop(0, TS, body, 0)


def cosine(x):
    x2 = x * x
    total = jnp.full_like(x, 1.0 / math.factorial(16))
    for k in range(7, -1, -1):
        total = total * x2 + (-1.0) ** k / math.factorial(2 * k)
    return total


def nt(a, b):
    return lax.dot_general(a, b, (((1,), (1,)), ((), ())), preferred_element_type=F32)


def mm(a, b):
    return jnp.dot(a, b, preferred_element_type=F32)


def tree(parts):
    while len(parts) > 1:
        pairs = [parts[k] + parts[k + 1] for k in range(0, len(parts) - 1, 2)]
        parts = pairs + parts[len(pairs) * 2 :]
    return parts[0]


def wide2(column):
    return jnp.concatenate([column, column], axis=1)


def find_neighbours(n, w, slot_tile, neighbours):
    tile = slot_tile[n * WIDE + w]
    known = jnp.maximum(tile, 0)
    columns = {0: w, 3: lax.rem(w + 1, 32), 7: lax.rem(w + 31, 32), 11: 31 - w}
    held = {key: [slot_tile[k * WIDE + col] for k in range(4)] for key, col in columns.items()}
    bases = (0, 0, 7, 3, 7, 3, 7, 3)
    slots, present, targets = [], [], []

    def find(base, target):
        slot = jnp.int32(0)
        for k in range(4):
            away = lax.rem(n + 4 - k, 4)
            here = jnp.maximum(away - 1, 0) if base == 0 else base + away
            slot = jnp.where(held[base][k] == target, here, slot)
        return slot

    for d in range(8):
        near = jnp.where(tile >= 0, neighbours[known * 8 + d], -1)
        present.append(near >= 0)
        targets.append(jnp.maximum(near, 0) >> 1)
        slots.append(find(bases[d], targets[d]))
        if d == 0:
            flip = near & 1
    mirror = find(11, targets[0])
    north_of = []
    for k in range(1, 4):
        other = slot_tile[lax.rem(n + k, 4) * WIDE + w]
        north_of.append(present[1] & (other == targets[1]))
    return known, slots, present, mirror, present[0] & (flip == 1), north_of


def block_kernel(
    feat_hbm, cot_hbm, wet, k49, slot_tile, neighbours, gain_row, w_in, bias_row, w_out, scale_row,
    updated_hbm, grad_hbm, g_in, g_out, ksum,
    feat, cot, updated, grad, wc, rmet, pad, gp, cells, kb, strips, got, hw, he, hs, hn, strip,
    gain, scale, bias, w_in_t, w_out_t, gwi, gwo, frame, fw, fe, back_strips, back_got, cw, ce,
    wmine, part8, mine4, part4, nodes, all4, wall, kx, kmine, kz, kq, kn,
    in_sem, up_sem, gr_sem, fsend, frecv, bsend, brecv, s1, r1, s2, r2, s3, r3, s4, r4, s5, r5,
    s6, r6, s7, r7, s8, r8,
):
    n = lax.axis_index("node")
    w = lax.axis_index("wide")
    x = w // 8
    z = lax.rem(w, 8)
    peers = border_peers(n, w)
    z_peers = [(k, lax.rem(z + k, 8)) for k in range(1, 8)]
    x_peers = [(k, lax.rem(x + k, 4)) for k in range(1, 4)]
    n_peers = [(k, lax.rem(n + k, 4)) for k in range(1, 4)]
    greet = [device for _, _, device in peers]
    greet += [(n, x * 8 + v) for _, v in z_peers] + [(n, v * 8 + z) for _, v in x_peers]
    barrier = pltpu.get_barrier_semaphore()
    for device in greet:
        pl.semaphore_signal(barrier, inc=1, device_id=device, device_id_type=MESH)
    fetch = [
        pltpu.make_async_copy(feat_hbm.at[0], feat, in_sem.at[0]),
        pltpu.make_async_copy(cot_hbm.at[0], cot, in_sem.at[1]),
    ]
    for copy in fetch:
        copy.start()

    def send(src, dst, send_sem, recv_sem, device):
        copy = pltpu.make_async_remote_copy(
            src_ref=src,
            dst_ref=dst,
            send_sem=send_sem,
            recv_sem=recv_sem,
            device_id=device,
            device_id_type=MESH,
        )
        copy.start()
        return copy

    known, slots, present, mirror, folded, north_of = find_neighbours(n, w, slot_tile, neighbours)
    broadcast_taps(k49, kb)
    clear_margins(pad)
    clear_margins(gp)
    clear_rows(cells)
    cell = lax.broadcasted_iota(jnp.int32, (1, 384), 1)
    sub_row = jnp.where(cell >= 96, 1.0, 0.0) + jnp.where(cell >= 192, 1.0, 0.0)
    sub_row = sub_row + jnp.where(cell >= 288, 1.0, 0.0)
    first_row = ((known >> 5) * TS).astype(F32) + 0.5
    fetch[0].wait()

    def prep(g, carry):
        here = pl.ds(pl.multiple_of(g * 384, 128), 384)
        latitude = -80.0 + 160.0 * (sub_row + ((g * 4).astype(F32) + first_row)) / float(8 * TS)
        metric = cosine(latitude * (math.pi / 180.0))
        weight = wet[:, here] * metric
        wc[:, here] = weight
        rmet[:, here] = 1.0 / metric
        t = (feat[:, here].astype(F32) * weight).astype(BF16).astype(F32).T
        for r in range(4):
            row = pl.multiple_of((g * 4 + r + 3) * PITCH + 8, 8)
            pad[pl.ds(row, TS), :] = t[r * TS : (r + 1) * TS]
        return carry

    def prep_pair(g, carry):
        prep(2 * g - 1, carry)
        return prep(2 * g, carry)

    prep(jnp.int32(0), 0)
    prep(jnp.int32(23), 0)
    for q in range(3):
        here = pl.ds(q * TS, TS)
        south = pad[pl.ds((3 + q) * PITCH + 8, TS), :]
        north = pad[pl.ds((96 + q) * PITCH + 8, TS), :]
        strips[5, here, :] = north.astype(BF16)
        for k in range(3):
            strips[k, here, :] = jnp.where(north_of[k], south, north).astype(BF16)
    pl.semaphore_wait(barrier, len(greet))
    copies = []

    def send_strips(sources):
        for slot, source, device in peers:
            if source in sources:
                copies.append(
                    send(strips.at[source], got.at[slot], fsend.at[slot], frecv.at[slot], device)
                )

    send_strips((0, 1, 2, 5))
    lax.fori_loop(1, 12, prep_pair, 0)
    for q in range(3):
        here = pl.ds(q * TS, TS)
        strips[3, here, :] = pad[pl.ds(3 * PITCH + 8 + q, TS, stride=PITCH), :].astype(BF16)
        strips[4, here, :] = pad[pl.ds(3 * PITCH + 101 + q, TS, stride=PITCH), :].astype(BF16)
    send_strips((3, 4))

    taps_columns(pad, kb, cells, False, 0, 7)
    gain[...] = jnp.broadcast_to(gain_row[...], (C, C)).T
    scale[...] = jnp.broadcast_to(scale_row[...], (C, C)).T
    for k in range(4):
        here = slice(k * C, (k + 1) * C)
        bias[here, :] = jnp.broadcast_to(bias_row[:, here], (C, C)).T
        w_in_t[here, :] = w_in[:, here].astype(F32).T.astype(BF16)
        w_out_t[:, here] = w_out[here, :].astype(F32).T.astype(BF16)
    gwi[...] = jnp.zeros_like(gwi)
    gwo[...] = jnp.zeros_like(gwo)
    hw[...] = jnp.zeros_like(hw)
    he[...] = jnp.zeros_like(he)
    i0 = lax.broadcasted_iota(jnp.int32, (TS, TS), 0)
    i1 = lax.broadcasted_iota(jnp.int32, (TS, TS), 1)
    turn = (i0 + i1 == TS - 1).astype(BF16)
    for copy in copies:
        copy.wait()

    def chosen(direction, q):
        v = got[slots[direction], pl.ds(q * TS, TS), :].astype(F32)
        return jnp.where(present[direction], v, 0.0)

    for side, (mid, top, low), col in ((hw, (2, 4, 6), 5), (he, (3, 5, 7), 8)):
        for q in range(3):
            strip[0:TS, :] = chosen(low, q)
            strip[0:3, :] = strip[TS - 3 : TS, :]
            strip[3 : TS + 3, :] = chosen(mid, q)
            strip[112 : 112 + TS, :] = chosen(top, q)
            strip[TS + 3 : TS + 6, :] = strip[112:115, :]
            side[pl.ds(col + q, PADROWS, stride=16), :] = strip[0:PADROWS, :]
    for q in range(3):
        o = q * PITCH
        hs[o + 8 : o + 104, :] = chosen(1, q)
        hs[o : o + 8, :] = hw[q * 16 : q * 16 + 8, :]
        hs[o + 104 : o + 112, :] = he[q * 16 + 8 : q * 16 + 16, :]
        flipped = mm(turn, got[mirror, pl.ds((2 - q) * TS, TS), :])
        north = jnp.where(folded, flipped, chosen(0, q))
        hn[o + 8 : o + 104, :] = jnp.where(present[0], north, 0.0)
        r = (TS + 3 + q) * 16
        hn[o : o + 8, :] = hw[r : r + 8, :]
        hn[o + 104 : o + 112, :] = he[r + 8 : r + 16, :]
    pad[0:BAND, :] = hs[...]
    pad[99 * PITCH :, :] = hn[...]

    def rim(rows, pairs):
        def body(jb, carry):
            j0 = pl.multiple_of(jb * 8, 8)
            for d, terms in pairs:
                o = pl.ds(pl.multiple_of(d * TS + j0, 8), 8)
                total = cells[o, :]
                for a, r in terms:
                    part = None
                    for b in range(7):
                        v = kb[7 * a + b] * rows[pl.ds(r * PITCH + j0 + 5 + b, 8), :]
                        part = v if part is None else part + v
                    total = total + part
                cells[o, :] = total
            return carry

        lax.fori_loop(0, 12, body, 0)

    rim(hs, [(i, [(a, i + a) for a in range(3 - i)]) for i in range(3)])
    rim(hn, [(93 + i, [(a, i + a - 6) for a in range(6 - i, 7)]) for i in range(3)])

    def sides(g, carry):
        for e in range(4):
            i = g * 4 + e
            p = pl.multiple_of((i + 3) * PITCH, 8)
            r = pl.multiple_of((i + 3) * 16, 8)
            pad[pl.ds(p, 8), :] = hw[pl.ds(r, 8), :]
            pad[pl.ds(p + 104, 8), :] = he[pl.ds(r + 8, 8), :]
            for side, taps, shift, col in ((hw, (0, 1, 2), 5, 0), (he, (4, 5, 6), -3, 88)):
                parts = []
                for a in range(7):
                    row = i + a
                    inside = jnp.logical_and(row >= 3, row < TS + 3).astype(F32)
                    v = [
                        kb[7 * a + b] * side[pl.ds(row * 16 + b + shift, 8), :] for b in taps
                    ]
                    parts.append(((v[0] + v[1]) + v[2]) * inside)
                o = pl.ds(pl.multiple_of(i * TS + col, 8), 8)
                cells[o, :] = cells[o, :] + tree(parts)
        return carry

    lax.fori_loop(0, TS // 4, sides, 0)
    fetch[1].wait()

    def first_half(here):
        rm = rmet[:, here]
        conv = cells[here, :].T * rm
        centred = conv - jnp.mean(conv, axis=0, keepdims=True)
        inv_std = lax.rsqrt(jnp.mean(centred * centred, axis=0, keepdims=True) + EPS)
        normed = centred * inv_std
        normed_bf = (normed * wide2(gain[...])).astype(BF16)
        ms = wet[:, here] * wide2(scale[...])
        gm = (ms * cot[:, here].astype(F32)).astype(BF16)
        hidden = mm(w_in_t[...], normed_bf) + wide2(bias[...])
        grad_active = mm(w_out[...], gm)
        return rm, inv_std, normed, normed_bf, ms, gm, hidden, grad_active

    def second_half(here, rm, inv_std, normed, normed_bf, ms, gm, hidden, grad_active):
        sq = hidden * hidden
        t = jnp.tanh(hidden * (GELU_COEF + (GELU_COEF * CUBIC) * sq))
        p = 0.5 + 0.5 * t
        active = hidden * p
        slope = p + active * (1.0 - p) * (2.0 * GELU_COEF + (6.0 * GELU_COEF * CUBIC) * sq)
        active_bf = active.astype(BF16)
        gh = (grad_active * slope).astype(BF16)
        mixed = mm(w_out_t[...], active_bf)
        updated[:, here] = (feat[:, here].astype(F32) + ms * mixed).astype(BF16)
        gn = mm(w_in[...], gh) * wide2(gain[...])
        gc = inv_std * (
            gn
            - jnp.mean(gn, axis=0, keepdims=True)
            - normed * jnp.mean(gn * normed, axis=0, keepdims=True)
        )
        gwo[...] += nt(gm, active_bf)
        gwi[...] += nt(normed_bf, gh)
        return (gc * rm).T.astype(BF16).astype(F32)

    def mlp_block(step, carry):
        at = [
            pl.ds(pl.multiple_of(step * BLOCK + c * CHUNK, CHUNK), CHUNK)
            for c in range(BLOCK // CHUNK)
        ]
        ahead = first_half(at[0])
        for c in range(BLOCK // CHUNK):
            now = ahead
            if c + 1 < BLOCK // CHUNK:
                ahead = first_half(at[c + 1])
            gs = second_half(at[c], *now)
            for r in range(BLOCK // TS):
                low, high = max(c * CHUNK, r * TS), min((c + 1) * CHUNK, (r + 1) * TS)
                if low < high:
                    row = step * (BLOCK // TS) + r + 3
                    o = pl.multiple_of(row * PITCH + 8 + low - r * TS, 8)
                    gp[pl.ds(o, high - low), :] = gs[low - c * CHUNK : high - c * CHUNK]
        return carry

    lax.fori_loop(0, CELLS // BLOCK, mlp_block, 0)
    out_updated = pltpu.make_async_copy(updated, updated_hbm.at[0], up_sem)
    out_updated.start()

    for k in range(4):
        here = slice(k * C, (k + 1) * C)
        wmine[here, :] = (gwi[:, here] * GRAD_SCALE).astype(BF16)
        wmine[HID + k * C : HID + (k + 1) * C, :] = (gwo[:, here] * GRAD_SCALE).astype(BF16)
    stage1 = []
    for k, v in z_peers:
        src = wmine.at[pl.ds(pl.multiple_of(v * C, C), C)]
        stage1.append(send(src, part8.at[k], s1.at[k], r1.at[k], (n, x * 8 + v)))

    def frame_rows(jb, carry):
        j0 = pl.multiple_of(jb * 8, 8)
        for f, p in enumerate((0, 1, 2, 99, 100, 101)):
            parts = []
            for a in range(7):
                if 0 <= p - a < TS:
                    parts += [
                        kb[7 * a + b] * gp[pl.ds((p - a + 3) * PITCH + j0 + 8 - b, 8), :]
                        for b in range(7)
                    ]
            frame[f, pl.ds(j0, 8), :] = tree(parts)
        return carry

    lax.fori_loop(0, 13, frame_rows, 0)

    def frame_cols(g, carry):
        for e in range(4):
            p = g * 4 + e + 3
            for side, taps, q0 in ((fw, (0, 1, 2), 0), (fe, (4, 5, 6), 96)):
                parts = [
                    kb[7 * a + b] * gp[pl.ds((p - a + 3) * PITCH + q0 + 8 - b, 8), :]
                    for a in range(7)
                    for b in taps
                ]
                side[pl.ds(pl.multiple_of(p * 8, 8), 8), :] = tree(parts)
        return carry

    lax.fori_loop(0, TS // 4, frame_cols, 0)
    for f, p in enumerate((0, 1, 2, 99, 100, 101)):
        fw[p * 8 : p * 8 + 8, :] = frame[f, 0:8, :]
        fe[p * 8 : p * 8 + 8, :] = frame[f, 96:104, :]
    fw[PADROWS * 8 :, :] = jnp.zeros((80, C), F32)
    fe[PADROWS * 8 :, :] = jnp.zeros((80, C), F32)
    for q in range(3):
        here = pl.ds(q * PITCH, PITCH)
        back_strips[3, here, :] = fw[pl.ds(q, PITCH, stride=8), :].astype(BF16)
        back_strips[4, here, :] = fe[pl.ds(3 + q, PITCH, stride=8), :].astype(BF16)
        here = pl.ds(q * TS, TS)
        south = frame[q, 3 : 3 + TS, :]
        north = frame[3 + q, 3 : 3 + TS, :]
        back_strips[5, here, :] = north.astype(BF16)
        for k in range(3):
            back_strips[k, here, :] = jnp.where(north_of[k], south, north).astype(BF16)
    borders = []
    for slot, source, device in peers:
        size = BAND if source in (3, 4) else STRIP
        borders.append(
            send(
                back_strips.at[source, pl.ds(0, size)],
                back_got.at[slot, pl.ds(0, size)],
                bsend.at[slot],
                brecv.at[slot],
                device,
            )
        )

    kx[...] = jnp.zeros_like(kx)
    zero = jnp.zeros((8, C), F32)

    def tap_column(b, carry):
        def taps(it, acc):
            i0 = it * 4
            acc = list(acc)
            for jb in range(12):
                g = [gp[pl.ds((i0 + d + 3) * PITCH + 8 + 8 * jb, 8), :] for d in range(4)]
                v = [pad[pl.ds((i0 + r) * PITCH + 8 * jb + 5 + b, 8), :] for r in range(10)]
                for a in range(7):
                    near = (g[0] * v[a] + g[1] * v[a + 1]) + (g[2] * v[a + 2] + g[3] * v[a + 3])
                    acc[a] = acc[a] + near
            return tuple(acc)

        acc = lax.fori_loop(0, 24, taps, (zero,) * 7)
        for a in range(7):
            t = 7 * a + b
            kx[pl.ds(t, 1), :] = jnp.sum(acc[a], axis=0, keepdims=True)
        return carry

    lax.fori_loop(0, 7, tap_column, 0)

    kmine[...] = (kx[...] * GRAD_SCALE).astype(BF16)
    kz[z] = kmine[...]
    kstage = []
    for k, v in z_peers:
        kstage.append(send(kmine, kz.at[z], s6.at[k], r6.at[k], (n, x * 8 + v)))
    for copy in stage1:
        copy.wait()
    total = wmine[pl.ds(pl.multiple_of(z * C, C), C), :].astype(F32)
    for k in range(1, 8):
        total = total + part8[k].astype(F32)
    mine4[...] = total
    stage2 = []
    for k, v in x_peers:
        src = mine4.at[pl.ds(pl.multiple_of(v * 32, 32), 32)]
        stage2.append(send(src, part4.at[k], s2.at[k], r2.at[k], (n, v * 8 + z)))
    clear_rows(cells)
    taps_columns(gp, kb, cells, True, 0, 2)
    for copy in stage2 + kstage:
        copy.wait()
    total = mine4[pl.ds(pl.multiple_of(x * 32, 32), 32), :]
    for k in range(1, 4):
        total = total + part4[k]
    nodes[n] = total
    stage3 = []
    for k, v in n_peers:
        stage3.append(send(nodes.at[n], nodes.at[n], s3.at[k], r3.at[k], (v, w)))
    total = kz[0].astype(F32)
    for v in range(1, 8):
        total = total + kz[v].astype(F32)
    kq[x] = total
    kstage = []
    for k, v in x_peers:
        kstage.append(send(kq.at[x], kq.at[x], s7.at[k], r7.at[k], (n, v * 8 + z)))
    taps_columns(gp, kb, cells, True, 2, 4)
    for copy in stage3 + kstage:
        copy.wait()
    all4[x] = ((nodes[0] + nodes[1]) + (nodes[2] + nodes[3])).astype(BF16)
    stage4 = []
    for k, v in x_peers:
        stage4.append(send(all4.at[x], all4.at[x], s4.at[k], r4.at[k], (n, v * 8 + z)))
    kn[n] = (kq[0] + kq[1]) + (kq[2] + kq[3])
    kstage = []
    for k, v in n_peers:
        kstage.append(send(kn.at[n], kn.at[n], s8.at[k], r8.at[k], (v, w)))
    taps_columns(gp, kb, cells, True, 4, 6)
    for copy in stage4:
        copy.wait()
    for v in range(4):
        wall[z, v * 32 : (v + 1) * 32, :] = all4[v]
    stage5 = []
    for k, v in z_peers:
        stage5.append(send(wall.at[z], wall.at[z], s5.at[k], r5.at[k], (n, x * 8 + v)))
    taps_columns(gp, kb, cells, True, 6, 7)
    for copy in borders:
        copy.wait()

    cw[...] = jnp.zeros_like(cw)
    ce[...] = jnp.zeros_like(ce)

    def received(direction, start, size):
        v = back_got[slots[direction], pl.ds(start, size), :].astype(F32)
        return jnp.where(present[direction], v, 0.0)

    for side, (mid, north, south), col in ((cw, (2, 4, 6), 0), (ce, (3, 5, 7), 5)):
        for q in range(3):
            strip[0:PITCH, :] = received(mid, q * PITCH, PITCH)
            strip[PITCH : 2 * PITCH, :] = received(north, q * PITCH, PITCH)
            strip[2 * PITCH :, :] = received(south, q * PITCH, PITCH)
            strip[TS : TS + 3, :] += strip[PITCH : PITCH + 3, :]
            strip[3:6, :] += strip[2 * PITCH + TS + 3 : 2 * PITCH + TS + 6, :]
            side[pl.ds(col + q, TS, stride=8), :] = strip[3 : TS + 3, :]
    for q in range(3):
        cells[q * TS : (q + 1) * TS, :] += received(1, q * TS, TS)
        flipped = mm(turn, back_got[mirror, pl.ds((2 - q) * TS, TS), :])
        north = jnp.where(folded, flipped, received(0, q * TS, TS))
        cells[(93 + q) * TS : (94 + q) * TS, :] += jnp.where(present[0], north, 0.0)

    def finish(step, carry):
        for r in range(BLOCK // TS):
            i = step * (BLOCK // TS) + r
            o = pl.multiple_of(i * TS, 8)
            row = pl.multiple_of(i * 8, 8)
            cells[pl.ds(o, 8), :] += cw[pl.ds(row, 8), :]
            cells[pl.ds(o + 88, 8), :] += ce[pl.ds(row, 8), :]
        here = pl.ds(pl.multiple_of(step * BLOCK, BLOCK), BLOCK)
        whole = cot[:, here].astype(F32) + wc[:, here] * cells[here, :].T
        grad[:, here] = whole.astype(BF16)
        return carry

    lax.fori_loop(0, CELLS // BLOCK, finish, 0)
    out_grad = pltpu.make_async_copy(grad, grad_hbm.at[0], gr_sem)
    out_grad.start()
    for copy in kstage:
        copy.wait()
    ksum[...] = ((kn[0] + kn[1]) + (kn[2] + kn[3]))[0:49, :]
    for copy in stage5:
        copy.wait()
    for k in range(4):
        here = slice(k * C, (k + 1) * C)
        g_in[:, here] = wall[k].astype(F32)
        g_out[here, :] = wall[4 + k].astype(F32).T
    out_updated.wait()
    out_grad.wait()


def block_call(*args):
    vmem = pl.BlockSpec(memory_space=pltpu.VMEM)
    smem = pl.BlockSpec(memory_space=pltpu.SMEM)
    hbm = pl.BlockSpec(memory_space=pl.ANY)
    dma = pltpu.SemaphoreType.DMA
    shapes = [
        ((C, CELLS), BF16), ((C, CELLS), BF16), ((C, CELLS), BF16), ((C, CELLS), BF16),
        ((1, CELLS), F32), ((1, CELLS), F32),
        ((PADROWS * PITCH, C), F32), ((PADROWS * PITCH, C), F32), ((CELLS, C), F32),
        ((49, 8, C), F32), ((6, STRIP, C), BF16), ((15, STRIP, C), BF16),
        ((PADROWS * 16, C), F32), ((PADROWS * 16, C), F32), ((BAND, C), F32), ((BAND, C), F32),
        ((3 * PITCH, C), F32),
        ((C, C), F32), ((C, C), F32), ((HID, C), F32), ((HID, C), BF16), ((C, HID), BF16),
        ((C, HID), F32), ((C, HID), F32),
        ((6, 104, C), F32), ((PITCH * 8, C), F32), ((PITCH * 8, C), F32),
        ((6, BAND, C), BF16), ((15, BAND, C), BF16), ((TS * 8, C), F32), ((TS * 8, C), F32),
        ((8 * C, C), BF16), ((8, C, C), BF16), ((C, C), F32), ((4, 32, C), F32),
        ((4, 32, C), F32), ((4, 32, C), BF16), ((8, C, C), BF16),
        ((64, C), F32), ((64, C), BF16), ((8, 64, C), BF16), ((4, 64, C), F32), ((4, 64, C), F32),
    ]
    sems = [dma((2,)), dma, dma, dma((15,)), dma((15,)), dma((15,)), dma((15,))]
    sems += [dma((8,)), dma((8,))] + [dma((4,))] * 6 + [dma((8,))] * 4 + [dma((4,))] * 4
    return pl.pallas_call(
        block_kernel,
        out_shape=(
            jax.ShapeDtypeStruct((1, C, CELLS), BF16),
            jax.ShapeDtypeStruct((1, C, CELLS), BF16),
            jax.ShapeDtypeStruct((C, HID), F32),
            jax.ShapeDtypeStruct((HID, C), F32),
            jax.ShapeDtypeStruct((49, C), F32),
        ),
        in_specs=[hbm, hbm, vmem, vmem, smem, smem] + [vmem] * 5,
        out_specs=(hbm, hbm, vmem, vmem, vmem),
        scratch_shapes=[pltpu.VMEM(shape, dtype) for shape, dtype in shapes] + sems,
        compiler_params=pltpu.CompilerParams(
            collective_id=0, has_side_effects=True, vmem_limit_bytes=VMEM_LIMIT
        ),
        name="block",
    )(*args)


def local(
    features,
    cotangent,
    wet_fraction,
    slot_tile,
    neighbours,
    kernel,
    norm_gain,
    weight_in,
    bias_in,
    weight_out,
    layer_scale,
):
    return block_call(
        features,
        cotangent,
        wet_fraction,
        kernel,
        slot_tile,
        neighbours.reshape(-1),
        norm_gain[None, :],
        weight_in,
        bias_in[None, :],
        weight_out,
        layer_scale[None, :],
    )


def solution(mesh):
    shards = P(("node", "wide"), None, None)
    in_specs = (shards, shards, P(("node", "wide"), None)) + (P(),) * 8
    out_specs = (shards, shards, P(), P(), P())
    return jax.shard_map(local, mesh=mesh, in_specs=in_specs, out_specs=out_specs, check_vma=False)
```

```python
import math

import jax
import jax.numpy as jnp
from jax import lax
from jax.experimental import pallas as pl
from jax.experimental.pallas import tpu as pltpu
from jax.sharding import PartitionSpec as P

C = 128
HID = 512
TS = 96
CELLS = TS * TS
NODE = 4
WIDE = 32
PITCH = 112
PADROWS = TS + 6
STRIP = 3 * TS
BAND = 3 * PITCH
BLOCK = 1536
CHUNK = 256
EPS = 1e-06
GELU_COEF = 0.7978845608028654
CUBIC = 0.044715
GRAD_SCALE = 1.0 / math.sqrt(NODE * WIDE * CELLS)
MESH = pl.DeviceIdType.MESH
F32 = jnp.float32
BF16 = jnp.bfloat16
VMEM_LIMIT = 60 * 2**20


def border_peers(n, w):
    out = []
    for k in range(1, 4):
        out.append((k - 1, k - 1, (lax.rem(n + k, 4), w)))
    sides = ((3, 3, lax.rem(w + 31, 32)), (7, 4, lax.rem(w + 1, 32)), (11, 5, 31 - w))
    for base, source, column in sides:
        for k in range(4):
            out.append((base + k, source, (lax.rem(n + k, 4), column)))
    return out


def broadcast_taps(k49, kb):
    for t in range(49):
        kb[t] = jnp.broadcast_to(k49[t : t + 1, :], (8, C))


def taps_columns(src, kb, out, flip, low, high):
    def body(it, carry):
        b = it // 12
        i0 = lax.rem(it, 12) * 8
        taps = [kb[48 - 7 * a - b] if flip else kb[7 * a + b] for a in range(7)]
        for jb in range(12):
            base = i0 * PITCH + 8 * jb + 5 + b
            v = [src[pl.ds(base + r * PITCH, 8), :] for r in range(14)]
            for d in range(8):
                total = taps[0] * v[d]
                for a in range(1, 7):
                    total = total + taps[a] * v[d + a]
                o = pl.ds(pl.multiple_of((i0 + d) * TS + 8 * jb, 8), 8)
                out[o, :] = out[o, :] + total
        return carry

    lax.fori_loop(low * 12, high * 12, body, 0)


def clear_rows(out):
    zero = jnp.zeros((TS, C), F32)

    def body(i, carry):
        out[pl.ds(pl.multiple_of(i * TS, 8), TS), :] = zero
        return carry

    lax.fori_loop(0, TS, body, 0)


def clear_margins(pad):
    zero8 = jnp.zeros((8, C), F32)
    zero_row = jnp.zeros((PITCH, C), F32)
    for r in (0, 1, 2, 99, 100, 101):
        pad[r * PITCH : (r + 1) * PITCH, :] = zero_row

    def body(i, carry):
        o = pl.multiple_of((i + 3) * PITCH, 8)
        pad[pl.ds(o, 8), :] = zero8
        pad[pl.ds(o + 104, 8), :] = zero8
        return carry

    lax.fori_loop(0, TS, body, 0)


def cosine(x):
    x2 = x * x
    total = jnp.full_like(x, 1.0 / math.factorial(16))
    for k in range(7, -1, -1):
        total = total * x2 + (-1.0) ** k / math.factorial(2 * k)
    return total


def nt(a, b):
    return lax.dot_general(a, b, (((1,), (1,)), ((), ())), preferred_element_type=F32)


def mm(a, b):
    return jnp.dot(a, b, preferred_element_type=F32)


def tree(parts):
    while len(parts) > 1:
        pairs = [parts[k] + parts[k + 1] for k in range(0, len(parts) - 1, 2)]
        parts = pairs + parts[len(pairs) * 2 :]
    return parts[0]


def wide2(column):
    return jnp.concatenate([column, column], axis=1)


def find_neighbours(n, w, slot_tile, neighbours):
    tile = slot_tile[n * WIDE + w]
    known = jnp.maximum(tile, 0)
    columns = {0: w, 3: lax.rem(w + 1, 32), 7: lax.rem(w + 31, 32), 11: 31 - w}
    held = {key: [slot_tile[k * WIDE + col] for k in range(4)] for key, col in columns.items()}
    bases = (0, 0, 7, 3, 7, 3, 7, 3)
    slots, present, targets = [], [], []

    def find(base, target):
        slot = jnp.int32(0)
        for k in range(4):
            away = lax.rem(n + 4 - k, 4)
            here = jnp.maximum(away - 1, 0) if base == 0 else base + away
            slot = jnp.where(held[base][k] == target, here, slot)
        return slot

    for d in range(8):
        near = jnp.where(tile >= 0, neighbours[d, known], -1)
        present.append(near >= 0)
        targets.append(jnp.maximum(near, 0) >> 1)
        slots.append(find(bases[d], targets[d]))
        if d == 0:
            flip = near & 1
    mirror = find(11, targets[0])
    north_of = []
    for k in range(1, 4):
        other = slot_tile[lax.rem(n + k, 4) * WIDE + w]
        north_of.append(present[1] & (other == targets[1]))
    return known, slots, present, mirror, present[0] & (flip == 1), north_of


def block_kernel(
    feat_hbm, cot_hbm, wet, k49, slot_tile, neighbours, gain_row, w_in, bias_row, w_out, scale_row,
    updated_hbm, grad_hbm, g_in, g_out, ksum,
    feat, cot, updated, grad, wc, rmet, pad, gp, cells, kb, strips, got, hw, he, hs, hn, strip,
    gain, scale, bias, w_in_t, w_out_t, gwi, gwo, frame, fw, fe, back_strips, back_got, cw, ce,
    wmine, part8, mine4, part4, nodes, all4, wall, kx, kmine, kz, kq, kn,
    in_sem, up_sem, gr_sem, fsend, frecv, bsend, brecv, s1, r1, s2, r2, s3, r3, s4, r4, s5, r5,
    s6, r6, s7, r7, s8, r8,
):
    n = lax.axis_index("node")
    w = lax.axis_index("wide")
    x = w // 8
    z = lax.rem(w, 8)
    peers = border_peers(n, w)
    z_peers = [(k, lax.rem(z + k, 8)) for k in range(1, 8)]
    x_peers = [(k, lax.rem(x + k, 4)) for k in range(1, 4)]
    n_peers = [(k, lax.rem(n + k, 4)) for k in range(1, 4)]
    greet = [device for _, _, device in peers]
    greet += [(n, x * 8 + v) for _, v in z_peers] + [(n, v * 8 + z) for _, v in x_peers]
    barrier = pltpu.get_barrier_semaphore()
    for device in greet:
        pl.semaphore_signal(barrier, inc=1, device_id=device, device_id_type=MESH)
    fetch = [
        pltpu.make_async_copy(feat_hbm.at[0], feat, in_sem.at[0]),
        pltpu.make_async_copy(cot_hbm.at[0], cot, in_sem.at[1]),
    ]
    for copy in fetch:
        copy.start()

    def send(src, dst, send_sem, recv_sem, device):
        copy = pltpu.make_async_remote_copy(
            src_ref=src,
            dst_ref=dst,
            send_sem=send_sem,
            recv_sem=recv_sem,
            device_id=device,
            device_id_type=MESH,
        )
        copy.start()
        return copy

    known, slots, present, mirror, folded, north_of = find_neighbours(n, w, slot_tile, neighbours)
    broadcast_taps(k49, kb)
    clear_margins(pad)
    clear_margins(gp)
    clear_rows(cells)
    cell = lax.broadcasted_iota(jnp.int32, (1, 384), 1)
    sub_row = jnp.where(cell >= 96, 1.0, 0.0) + jnp.where(cell >= 192, 1.0, 0.0)
    sub_row = sub_row + jnp.where(cell >= 288, 1.0, 0.0)
    first_row = ((known >> 5) * TS).astype(F32) + 0.5
    fetch[0].wait()

    def prep(g, carry):
        here = pl.ds(pl.multiple_of(g * 384, 128), 384)
        latitude = -80.0 + 160.0 * (sub_row + ((g * 4).astype(F32) + first_row)) / float(8 * TS)
        metric = cosine(latitude * (math.pi / 180.0))
        weight = wet[:, here] * metric
        wc[:, here] = weight
        rmet[:, here] = 1.0 / metric
        t = (feat[:, here].astype(F32) * weight).astype(BF16).astype(F32).T
        for r in range(4):
            row = pl.multiple_of((g * 4 + r + 3) * PITCH + 8, 8)
            pad[pl.ds(row, TS), :] = t[r * TS : (r + 1) * TS]
        return carry

    def prep_pair(g, carry):
        prep(2 * g - 1, carry)
        return prep(2 * g, carry)

    prep(jnp.int32(0), 0)
    prep(jnp.int32(23), 0)
    for q in range(3):
        here = pl.ds(q * TS, TS)
        south = pad[pl.ds((3 + q) * PITCH + 8, TS), :]
        north = pad[pl.ds((96 + q) * PITCH + 8, TS), :]
        strips[5, here, :] = north.astype(BF16)
        for k in range(3):
            strips[k, here, :] = jnp.where(north_of[k], south, north).astype(BF16)
    pl.semaphore_wait(barrier, len(greet))
    copies = []

    def send_strips(sources):
        for slot, source, device in peers:
            if source in sources:
                copies.append(
                    send(strips.at[source], got.at[slot], fsend.at[slot], frecv.at[slot], device)
                )

    send_strips((0, 1, 2, 5))
    lax.fori_loop(1, 12, prep_pair, 0)
    for q in range(3):
        here = pl.ds(q * TS, TS)
        strips[3, here, :] = pad[pl.ds(3 * PITCH + 8 + q, TS, stride=PITCH), :].astype(BF16)
        strips[4, here, :] = pad[pl.ds(3 * PITCH + 101 + q, TS, stride=PITCH), :].astype(BF16)
    send_strips((3, 4))

    taps_columns(pad, kb, cells, False, 0, 7)
    gain[...] = jnp.broadcast_to(gain_row[...], (C, C)).T
    scale[...] = jnp.broadcast_to(scale_row[...], (C, C)).T
    for k in range(4):
        here = slice(k * C, (k + 1) * C)
        bias[here, :] = jnp.broadcast_to(bias_row[:, here], (C, C)).T
        w_in_t[here, :] = w_in[:, here].astype(F32).T.astype(BF16)
        w_out_t[:, here] = w_out[here, :].astype(F32).T.astype(BF16)
    gwi[...] = jnp.zeros_like(gwi)
    gwo[...] = jnp.zeros_like(gwo)
    hw[...] = jnp.zeros_like(hw)
    he[...] = jnp.zeros_like(he)
    i0 = lax.broadcasted_iota(jnp.int32, (TS, TS), 0)
    i1 = lax.broadcasted_iota(jnp.int32, (TS, TS), 1)
    turn = (i0 + i1 == TS - 1).astype(BF16)
    for copy in copies:
        copy.wait()

    def chosen(direction, q):
        v = got[slots[direction], pl.ds(q * TS, TS), :].astype(F32)
        return jnp.where(present[direction], v, 0.0)

    for side, (mid, top, low), col in ((hw, (2, 4, 6), 5), (he, (3, 5, 7), 8)):
        for q in range(3):
            strip[0:TS, :] = chosen(low, q)
            strip[0:3, :] = strip[TS - 3 : TS, :]
            strip[3 : TS + 3, :] = chosen(mid, q)
            strip[112 : 112 + TS, :] = chosen(top, q)
            strip[TS + 3 : TS + 6, :] = strip[112:115, :]
            side[pl.ds(col + q, PADROWS, stride=16), :] = strip[0:PADROWS, :]
    for q in range(3):
        o = q * PITCH
        hs[o + 8 : o + 104, :] = chosen(1, q)
        hs[o : o + 8, :] = hw[q * 16 : q * 16 + 8, :]
        hs[o + 104 : o + 112, :] = he[q * 16 + 8 : q * 16 + 16, :]
        flipped = mm(turn, got[mirror, pl.ds((2 - q) * TS, TS), :])
        north = jnp.where(folded, flipped, chosen(0, q))
        hn[o + 8 : o + 104, :] = jnp.where(present[0], north, 0.0)
        r = (TS + 3 + q) * 16
        hn[o : o + 8, :] = hw[r : r + 8, :]
        hn[o + 104 : o + 112, :] = he[r + 8 : r + 16, :]
    pad[0:BAND, :] = hs[...]
    pad[99 * PITCH :, :] = hn[...]

    def rim(rows, pairs):
        def body(jb, carry):
            j0 = pl.multiple_of(jb * 8, 8)
            for d, terms in pairs:
                o = pl.ds(pl.multiple_of(d * TS + j0, 8), 8)
                total = cells[o, :]
                for a, r in terms:
                    part = None
                    for b in range(7):
                        v = kb[7 * a + b] * rows[pl.ds(r * PITCH + j0 + 5 + b, 8), :]
                        part = v if part is None else part + v
                    total = total + part
                cells[o, :] = total
            return carry

        lax.fori_loop(0, 12, body, 0)

    rim(hs, [(i, [(a, i + a) for a in range(3 - i)]) for i in range(3)])
    rim(hn, [(93 + i, [(a, i + a - 6) for a in range(6 - i, 7)]) for i in range(3)])

    def sides(g, carry):
        for e in range(4):
            i = g * 4 + e
            p = pl.multiple_of((i + 3) * PITCH, 8)
            r = pl.multiple_of((i + 3) * 16, 8)
            pad[pl.ds(p, 8), :] = hw[pl.ds(r, 8), :]
            pad[pl.ds(p + 104, 8), :] = he[pl.ds(r + 8, 8), :]
            for side, taps, shift, col in ((hw, (0, 1, 2), 5, 0), (he, (4, 5, 6), -3, 88)):
                parts = []
                for a in range(7):
                    row = i + a
                    inside = jnp.logical_and(row >= 3, row < TS + 3).astype(F32)
                    v = [
                        kb[7 * a + b] * side[pl.ds(row * 16 + b + shift, 8), :] for b in taps
                    ]
                    parts.append(((v[0] + v[1]) + v[2]) * inside)
                o = pl.ds(pl.multiple_of(i * TS + col, 8), 8)
                cells[o, :] = cells[o, :] + tree(parts)
        return carry

    lax.fori_loop(0, TS // 4, sides, 0)
    fetch[1].wait()

    def first_half(here):
        rm = rmet[:, here]
        conv = cells[here, :].T * rm
        centred = conv - jnp.mean(conv, axis=0, keepdims=True)
        inv_std = lax.rsqrt(jnp.mean(centred * centred, axis=0, keepdims=True) + EPS)
        normed = centred * inv_std
        normed_bf = (normed * wide2(gain[...])).astype(BF16)
        ms = wet[:, here] * wide2(scale[...])
        gm = (ms * cot[:, here].astype(F32)).astype(BF16)
        hidden = mm(w_in_t[...], normed_bf) + wide2(bias[...])
        grad_active = mm(w_out[...], gm)
        return rm, inv_std, normed, normed_bf, ms, gm, hidden, grad_active

    def second_half(here, rm, inv_std, normed, normed_bf, ms, gm, hidden, grad_active):
        sq = hidden * hidden
        t = jnp.tanh(hidden * (GELU_COEF + (GELU_COEF * CUBIC) * sq))
        p = 0.5 + 0.5 * t
        active = hidden * p
        slope = p + active * (1.0 - p) * (2.0 * GELU_COEF + (6.0 * GELU_COEF * CUBIC) * sq)
        active_bf = active.astype(BF16)
        gh = (grad_active * slope).astype(BF16)
        mixed = mm(w_out_t[...], active_bf)
        updated[:, here] = (feat[:, here].astype(F32) + ms * mixed).astype(BF16)
        gn = mm(w_in[...], gh) * wide2(gain[...])
        gc = inv_std * (
            gn
            - jnp.mean(gn, axis=0, keepdims=True)
            - normed * jnp.mean(gn * normed, axis=0, keepdims=True)
        )
        gwo[...] += nt(gm, active_bf)
        gwi[...] += nt(normed_bf, gh)
        return (gc * rm).T.astype(BF16).astype(F32)

    def mlp_block(step, carry):
        at = [
            pl.ds(pl.multiple_of(step * BLOCK + c * CHUNK, CHUNK), CHUNK)
            for c in range(BLOCK // CHUNK)
        ]
        ahead = first_half(at[0])
        for c in range(BLOCK // CHUNK):
            now = ahead
            if c + 1 < BLOCK // CHUNK:
                ahead = first_half(at[c + 1])
            gs = second_half(at[c], *now)
            for r in range(BLOCK // TS):
                low, high = max(c * CHUNK, r * TS), min((c + 1) * CHUNK, (r + 1) * TS)
                if low < high:
                    row = step * (BLOCK // TS) + r + 3
                    o = pl.multiple_of(row * PITCH + 8 + low - r * TS, 8)
                    gp[pl.ds(o, high - low), :] = gs[low - c * CHUNK : high - c * CHUNK]
        return carry

    lax.fori_loop(0, CELLS // BLOCK, mlp_block, 0)
    out_updated = pltpu.make_async_copy(updated, updated_hbm.at[0], up_sem)
    out_updated.start()

    for k in range(4):
        here = slice(k * C, (k + 1) * C)
        wmine[here, :] = (gwi[:, here] * GRAD_SCALE).astype(BF16)
        wmine[HID + k * C : HID + (k + 1) * C, :] = (gwo[:, here] * GRAD_SCALE).astype(BF16)
    stage1 = []
    for k, v in z_peers:
        src = wmine.at[pl.ds(pl.multiple_of(v * C, C), C)]
        stage1.append(send(src, part8.at[k], s1.at[k], r1.at[k], (n, x * 8 + v)))

    def frame_rows(jb, carry):
        j0 = pl.multiple_of(jb * 8, 8)
        for f, p in enumerate((0, 1, 2, 99, 100, 101)):
            parts = []
            for a in range(7):
                if 0 <= p - a < TS:
                    parts += [
                        kb[7 * a + b] * gp[pl.ds((p - a + 3) * PITCH + j0 + 8 - b, 8), :]
                        for b in range(7)
                    ]
            frame[f, pl.ds(j0, 8), :] = tree(parts)
        return carry

    lax.fori_loop(0, 13, frame_rows, 0)

    def frame_cols(g, carry):
        for e in range(4):
            p = g * 4 + e + 3
            for side, taps, q0 in ((fw, (0, 1, 2), 0), (fe, (4, 5, 6), 96)):
                parts = [
                    kb[7 * a + b] * gp[pl.ds((p - a + 3) * PITCH + q0 + 8 - b, 8), :]
                    for a in range(7)
                    for b in taps
                ]
                side[pl.ds(pl.multiple_of(p * 8, 8), 8), :] = tree(parts)
        return carry

    lax.fori_loop(0, TS // 4, frame_cols, 0)
    for f, p in enumerate((0, 1, 2, 99, 100, 101)):
        fw[p * 8 : p * 8 + 8, :] = frame[f, 0:8, :]
        fe[p * 8 : p * 8 + 8, :] = frame[f, 96:104, :]
    fw[PADROWS * 8 :, :] = jnp.zeros((80, C), F32)
    fe[PADROWS * 8 :, :] = jnp.zeros((80, C), F32)
    for q in range(3):
        here = pl.ds(q * PITCH, PITCH)
        back_strips[3, here, :] = fw[pl.ds(q, PITCH, stride=8), :].astype(BF16)
        back_strips[4, here, :] = fe[pl.ds(3 + q, PITCH, stride=8), :].astype(BF16)
        here = pl.ds(q * TS, TS)
        south = frame[q, 3 : 3 + TS, :]
        north = frame[3 + q, 3 : 3 + TS, :]
        back_strips[5, here, :] = north.astype(BF16)
        for k in range(3):
            back_strips[k, here, :] = jnp.where(north_of[k], south, north).astype(BF16)
    borders = []
    for slot, source, device in peers:
        size = BAND if source in (3, 4) else STRIP
        borders.append(
            send(
                back_strips.at[source, pl.ds(0, size)],
                back_got.at[slot, pl.ds(0, size)],
                bsend.at[slot],
                brecv.at[slot],
                device,
            )
        )

    kx[...] = jnp.zeros_like(kx)
    zero = jnp.zeros((8, C), F32)

    def tap_column(b, carry):
        def taps(it, acc):
            i0 = it * 4
            acc = list(acc)
            for jb in range(12):
                g = [gp[pl.ds((i0 + d + 3) * PITCH + 8 + 8 * jb, 8), :] for d in range(4)]
                v = [pad[pl.ds((i0 + r) * PITCH + 8 * jb + 5 + b, 8), :] for r in range(10)]
                for a in range(7):
                    near = (g[0] * v[a] + g[1] * v[a + 1]) + (g[2] * v[a + 2] + g[3] * v[a + 3])
                    acc[a] = acc[a] + near
            return tuple(acc)

        acc = lax.fori_loop(0, 24, taps, (zero,) * 7)
        for a in range(7):
            t = 7 * a + b
            kx[pl.ds(t, 1), :] = jnp.sum(acc[a], axis=0, keepdims=True)
        return carry

    lax.fori_loop(0, 7, tap_column, 0)

    kmine[...] = (kx[...] * GRAD_SCALE).astype(BF16)
    kz[z] = kmine[...]
    kstage = []
    for k, v in z_peers:
        kstage.append(send(kmine, kz.at[z], s6.at[k], r6.at[k], (n, x * 8 + v)))
    for copy in stage1:
        copy.wait()
    total = wmine[pl.ds(pl.multiple_of(z * C, C), C), :].astype(F32)
    for k in range(1, 8):
        total = total + part8[k].astype(F32)
    mine4[...] = total
    stage2 = []
    for k, v in x_peers:
        src = mine4.at[pl.ds(pl.multiple_of(v * 32, 32), 32)]
        stage2.append(send(src, part4.at[k], s2.at[k], r2.at[k], (n, v * 8 + z)))
    clear_rows(cells)
    taps_columns(gp, kb, cells, True, 0, 2)
    for copy in stage2 + kstage:
        copy.wait()
    total = mine4[pl.ds(pl.multiple_of(x * 32, 32), 32), :]
    for k in range(1, 4):
        total = total + part4[k]
    nodes[n] = total
    stage3 = []
    for k, v in n_peers:
        stage3.append(send(nodes.at[n], nodes.at[n], s3.at[k], r3.at[k], (v, w)))
    total = kz[0].astype(F32)
    for v in range(1, 8):
        total = total + kz[v].astype(F32)
    kq[x] = total
    kstage = []
    for k, v in x_peers:
        kstage.append(send(kq.at[x], kq.at[x], s7.at[k], r7.at[k], (n, v * 8 + z)))
    taps_columns(gp, kb, cells, True, 2, 4)
    for copy in stage3 + kstage:
        copy.wait()
    all4[x] = ((nodes[0] + nodes[1]) + (nodes[2] + nodes[3])).astype(BF16)
    stage4 = []
    for k, v in x_peers:
        stage4.append(send(all4.at[x], all4.at[x], s4.at[k], r4.at[k], (n, v * 8 + z)))
    kn[n] = (kq[0] + kq[1]) + (kq[2] + kq[3])
    kstage = []
    for k, v in n_peers:
        kstage.append(send(kn.at[n], kn.at[n], s8.at[k], r8.at[k], (v, w)))
    taps_columns(gp, kb, cells, True, 4, 6)
    for copy in stage4:
        copy.wait()
    for v in range(4):
        wall[z, v * 32 : (v + 1) * 32, :] = all4[v]
    stage5 = []
    for k, v in z_peers:
        stage5.append(send(wall.at[z], wall.at[z], s5.at[k], r5.at[k], (n, x * 8 + v)))
    taps_columns(gp, kb, cells, True, 6, 7)
    for copy in borders:
        copy.wait()

    cw[...] = jnp.zeros_like(cw)
    ce[...] = jnp.zeros_like(ce)

    def received(direction, start, size):
        v = back_got[slots[direction], pl.ds(start, size), :].astype(F32)
        return jnp.where(present[direction], v, 0.0)

    for side, (mid, north, south), col in ((cw, (2, 4, 6), 0), (ce, (3, 5, 7), 5)):
        for q in range(3):
            strip[0:PITCH, :] = received(mid, q * PITCH, PITCH)
            strip[PITCH : 2 * PITCH, :] = received(north, q * PITCH, PITCH)
            strip[2 * PITCH :, :] = received(south, q * PITCH, PITCH)
            strip[TS : TS + 3, :] += strip[PITCH : PITCH + 3, :]
            strip[3:6, :] += strip[2 * PITCH + TS + 3 : 2 * PITCH + TS + 6, :]
            side[pl.ds(col + q, TS, stride=8), :] = strip[3 : TS + 3, :]
    for q in range(3):
        cells[q * TS : (q + 1) * TS, :] += received(1, q * TS, TS)
        flipped = mm(turn, back_got[mirror, pl.ds((2 - q) * TS, TS), :])
        north = jnp.where(folded, flipped, received(0, q * TS, TS))
        cells[(93 + q) * TS : (94 + q) * TS, :] += jnp.where(present[0], north, 0.0)

    def finish(step, carry):
        for r in range(BLOCK // TS):
            i = step * (BLOCK // TS) + r
            o = pl.multiple_of(i * TS, 8)
            row = pl.multiple_of(i * 8, 8)
            cells[pl.ds(o, 8), :] += cw[pl.ds(row, 8), :]
            cells[pl.ds(o + 88, 8), :] += ce[pl.ds(row, 8), :]
        here = pl.ds(pl.multiple_of(step * BLOCK, BLOCK), BLOCK)
        whole = cot[:, here].astype(F32) + wc[:, here] * cells[here, :].T
        grad[:, here] = whole.astype(BF16)
        return carry

    lax.fori_loop(0, CELLS // BLOCK, finish, 0)
    out_grad = pltpu.make_async_copy(grad, grad_hbm.at[0], gr_sem)
    out_grad.start()
    for copy in kstage:
        copy.wait()
    ksum[...] = ((kn[0] + kn[1]) + (kn[2] + kn[3]))[0:49, :]
    for copy in stage5:
        copy.wait()
    for k in range(4):
        here = slice(k * C, (k + 1) * C)
        g_in[:, here] = wall[k].astype(F32)
        g_out[here, :] = wall[4 + k].astype(F32).T
    out_updated.wait()
    out_grad.wait()


def block_call(*args):
    vmem = pl.BlockSpec(memory_space=pltpu.VMEM)
    smem = pl.BlockSpec(memory_space=pltpu.SMEM)
    hbm = pl.BlockSpec(memory_space=pl.ANY)
    dma = pltpu.SemaphoreType.DMA
    shapes = [
        ((C, CELLS), BF16), ((C, CELLS), BF16), ((C, CELLS), BF16), ((C, CELLS), BF16),
        ((1, CELLS), F32), ((1, CELLS), F32),
        ((PADROWS * PITCH, C), F32), ((PADROWS * PITCH, C), F32), ((CELLS, C), F32),
        ((49, 8, C), F32), ((6, STRIP, C), BF16), ((15, STRIP, C), BF16),
        ((PADROWS * 16, C), F32), ((PADROWS * 16, C), F32), ((BAND, C), F32), ((BAND, C), F32),
        ((3 * PITCH, C), F32),
        ((C, C), F32), ((C, C), F32), ((HID, C), F32), ((HID, C), BF16), ((C, HID), BF16),
        ((C, HID), F32), ((C, HID), F32),
        ((6, 104, C), F32), ((PITCH * 8, C), F32), ((PITCH * 8, C), F32),
        ((6, BAND, C), BF16), ((15, BAND, C), BF16), ((TS * 8, C), F32), ((TS * 8, C), F32),
        ((8 * C, C), BF16), ((8, C, C), BF16), ((C, C), F32), ((4, 32, C), F32),
        ((4, 32, C), F32), ((4, 32, C), BF16), ((8, C, C), BF16),
        ((64, C), F32), ((64, C), BF16), ((8, 64, C), BF16), ((4, 64, C), F32), ((4, 64, C), F32),
    ]
    sems = [dma((2,)), dma, dma, dma((15,)), dma((15,)), dma((15,)), dma((15,))]
    sems += [dma((8,)), dma((8,))] + [dma((4,))] * 6 + [dma((8,))] * 4 + [dma((4,))] * 4
    return pl.pallas_call(
        block_kernel,
        out_shape=(
            jax.ShapeDtypeStruct((1, C, CELLS), BF16),
            jax.ShapeDtypeStruct((1, C, CELLS), BF16),
            jax.ShapeDtypeStruct((C, HID), F32),
            jax.ShapeDtypeStruct((HID, C), F32),
            jax.ShapeDtypeStruct((49, C), F32),
        ),
        in_specs=[hbm, hbm, vmem, vmem, smem, smem] + [vmem] * 5,
        out_specs=(hbm, hbm, vmem, vmem, vmem),
        scratch_shapes=[pltpu.VMEM(shape, dtype) for shape, dtype in shapes] + sems,
        compiler_params=pltpu.CompilerParams(
            collective_id=0, has_side_effects=True, vmem_limit_bytes=VMEM_LIMIT
        ),
        name="block",
    )(*args)


def hand_over_kernel(*refs):
    sources, results, held = refs[:5], refs[5:10], refs[10:15]
    in_sem, out_sem = refs[15:]
    pieces = []
    for source, result, stage in zip(sources[:2], results[:2], held[:2]):
        for k in range(4):
            here = pl.ds(k * 32, 32)
            pieces.append((source.at[0, here], stage.at[here], result.at[0, here]))
    pieces += [(a, b, c) for a, b, c in zip(sources[2:], held[2:], results[2:])]
    loads = [pltpu.make_async_copy(a, b, in_sem.at[k]) for k, (a, b, _) in enumerate(pieces)]
    stores = [pltpu.make_async_copy(b, c, out_sem.at[k]) for k, (_, b, c) in enumerate(pieces)]
    for copy in loads:
        copy.start()
    for load, store in zip(loads, stores):
        load.wait()
        store.start()
    for copy in stores:
        copy.wait()


def hand_over(*arrays):
    hbm = pl.BlockSpec(memory_space=pl.ANY)
    held = [pltpu.VMEM((C, CELLS), BF16)] * 2
    held += [pltpu.VMEM(a.shape, a.dtype) for a in arrays[2:]]
    return pl.pallas_call(
        hand_over_kernel,
        out_shape=tuple(jax.ShapeDtypeStruct(a.shape, a.dtype) for a in arrays),
        in_specs=[hbm] * 5,
        out_specs=(hbm,) * 5,
        scratch_shapes=held + [pltpu.SemaphoreType.DMA((11,))] * 2,
        compiler_params=pltpu.CompilerParams(vmem_limit_bytes=VMEM_LIMIT),
        name="hand_over",
    )(*arrays)


def local(
    features,
    cotangent,
    wet_fraction,
    slot_tile,
    neighbours,
    kernel,
    norm_gain,
    weight_in,
    bias_in,
    weight_out,
    layer_scale,
):
    results = block_call(
        features,
        cotangent,
        wet_fraction,
        kernel,
        slot_tile,
        neighbours.T,
        norm_gain[None, :],
        weight_in,
        bias_in[None, :],
        weight_out,
        layer_scale[None, :],
    )
    return hand_over(*results)


def solution(mesh):
    shards = P(("node", "wide"), None, None)
    in_specs = (shards, shards, P(("node", "wide"), None)) + (P(),) * 8
    out_specs = (shards, shards, P(), P(), P())
    return jax.shard_map(local, mesh=mesh, in_specs=in_specs, out_specs=out_specs, check_vma=False)
```

```python
import math

import jax
import jax.numpy as jnp
from jax import lax
from jax.experimental import pallas as pl
from jax.experimental.pallas import tpu as pltpu
from jax.sharding import PartitionSpec as P

C = 128
HID = 512
TS = 96
CELLS = TS * TS
NODE = 4
WIDE = 32
PITCH = 112
PADROWS = TS + 6
STRIP = 3 * TS
BAND = 3 * PITCH
BLOCK = 2304
CHUNK = 256
EPS = 1e-06
GELU_COEF = 0.7978845608028654
CUBIC = 0.044715
GRAD_SCALE = 1.0 / math.sqrt(NODE * WIDE * CELLS)
MESH = pl.DeviceIdType.MESH
F32 = jnp.float32
BF16 = jnp.bfloat16
VMEM_LIMIT = 60 * 2**20


def border_peers(n, w):
    out = []
    for k in range(1, 4):
        out.append((k - 1, k - 1, (lax.rem(n + k, 4), w)))
    sides = ((3, 3, lax.rem(w + 31, 32)), (7, 4, lax.rem(w + 1, 32)), (11, 5, 31 - w))
    for base, source, column in sides:
        for k in range(4):
            out.append((base + k, source, (lax.rem(n + k, 4), column)))
    return out


def broadcast_taps(k49, kb):
    for t in range(49):
        kb[t] = jnp.broadcast_to(k49[t : t + 1, :], (8, C))


def taps_columns(src, kb, out, flip, low, high):
    def passes(columns):
        def body(it, carry):
            b0 = low + columns * (it // 12)
            i0 = lax.rem(it, 12) * 8
            taps = [
                [kb[48 - 7 * a - b0 - e] if flip else kb[7 * a + b0 + e] for a in range(7)]
                for e in range(columns)
            ]
            for jb in range(12):
                base = i0 * PITCH + 8 * jb + 5 + b0
                totals = [None] * 8
                for e in range(columns):
                    v = [src[pl.ds(base + e + r * PITCH, 8), :] for r in range(14)]
                    for d in range(8):
                        for a in range(7):
                            p = taps[e][a] * v[d + a]
                            totals[d] = p if totals[d] is None else totals[d] + p
                for d in range(8):
                    o = pl.ds(pl.multiple_of((i0 + d) * TS + 8 * jb, 8), 8)
                    out[o, :] = out[o, :] + totals[d]
            return carry

        return body

    if (high - low) % 2:
        lax.fori_loop(0, 12, passes(1), 0)
        low += 1
    if high > low:
        lax.fori_loop(0, (high - low) // 2 * 12, passes(2), 0)


def clear_rows(out):
    zero = jnp.zeros((TS, C), F32)

    def body(i, carry):
        out[pl.ds(pl.multiple_of(i * TS, 8), TS), :] = zero
        return carry

    lax.fori_loop(0, TS, body, 0)


def clear_margins(pad):
    zero8 = jnp.zeros((8, C), F32)
    zero_row = jnp.zeros((PITCH, C), F32)
    for r in (0, 1, 2, 99, 100, 101):
        pad[r * PITCH : (r + 1) * PITCH, :] = zero_row

    def body(i, carry):
        o = pl.multiple_of((i + 3) * PITCH, 8)
        pad[pl.ds(o, 8), :] = zero8
        pad[pl.ds(o + 104, 8), :] = zero8
        return carry

    lax.fori_loop(0, TS, body, 0)


def cosine(x):
    x2 = x * x
    total = jnp.full_like(x, 1.0 / math.factorial(16))
    for k in range(7, -1, -1):
        total = total * x2 + (-1.0) ** k / math.factorial(2 * k)
    return total


def nt(a, b):
    return lax.dot_general(a, b, (((1,), (1,)), ((), ())), preferred_element_type=F32)


def mm(a, b):
    return jnp.dot(a, b, preferred_element_type=F32)


def tree(parts):
    while len(parts) > 1:
        pairs = [parts[k] + parts[k + 1] for k in range(0, len(parts) - 1, 2)]
        parts = pairs + parts[len(pairs) * 2 :]
    return parts[0]


def wide2(column):
    return jnp.concatenate([column, column], axis=1)


def find_neighbours(n, w, slot_tile, neighbours):
    tile = slot_tile[n * WIDE + w]
    known = jnp.maximum(tile, 0)
    columns = {0: w, 3: lax.rem(w + 1, 32), 7: lax.rem(w + 31, 32), 11: 31 - w}
    held = {key: [slot_tile[k * WIDE + col] for k in range(4)] for key, col in columns.items()}
    bases = (0, 0, 7, 3, 7, 3, 7, 3)
    slots, present, targets = [], [], []

    def find(base, target):
        slot = jnp.int32(0)
        for k in range(4):
            away = lax.rem(n + 4 - k, 4)
            here = jnp.maximum(away - 1, 0) if base == 0 else base + away
            slot = jnp.where(held[base][k] == target, here, slot)
        return slot

    for d in range(8):
        near = jnp.where(tile >= 0, neighbours[d, known], -1)
        present.append(near >= 0)
        targets.append(jnp.maximum(near, 0) >> 1)
        slots.append(find(bases[d], targets[d]))
        if d == 0:
            flip = near & 1
    mirror = find(11, targets[0])
    north_of = []
    for k in range(1, 4):
        other = slot_tile[lax.rem(n + k, 4) * WIDE + w]
        north_of.append(present[1] & (other == targets[1]))
    return known, slots, present, mirror, present[0] & (flip == 1), north_of


def block_kernel(
    feat_hbm, cot_hbm, wet, k49, slot_tile, neighbours, gain_row, w_in, bias_row, w_out, scale_row,
    updated_hbm, grad_hbm, g_in, g_out, ksum,
    feat, cot, updated, grad, wc, rmet, pad, gp, cells, kb, strips, got, hw, he, hs, hn, strip,
    gain, scale, ones, w_in_t, w_out_t, w_out_half, gwi, gwo, frame, fw, fe, back_strips, back_got, cw, ce,
    wmine, part8, mine4, part4, nodes, all4, wall, kx, kmine, kz, kq, kn,
    in_sem, up_sem, gr_sem, fsend, frecv, bsend, brecv, s1, r1, s2, r2, s3, r3, s4, r4, s5, r5,
    s6, r6, s7, r7, s8, r8,
):
    n = lax.axis_index("node")
    w = lax.axis_index("wide")
    x = w // 8
    z = lax.rem(w, 8)
    peers = border_peers(n, w)
    z_peers = [(k, lax.rem(z + k, 8)) for k in range(1, 8)]
    x_peers = [(k, lax.rem(x + k, 4)) for k in range(1, 4)]
    n_peers = [(k, lax.rem(n + k, 4)) for k in range(1, 4)]
    greet = [device for _, _, device in peers]
    greet += [(n, x * 8 + v) for _, v in z_peers] + [(n, v * 8 + z) for _, v in x_peers]
    barrier = pltpu.get_barrier_semaphore()
    for device in greet:
        pl.semaphore_signal(barrier, inc=1, device_id=device, device_id_type=MESH)
    fetch = [
        pltpu.make_async_copy(feat_hbm.at[0], feat, in_sem.at[0]),
        pltpu.make_async_copy(cot_hbm.at[0], cot, in_sem.at[1]),
    ]
    for copy in fetch:
        copy.start()

    def send(src, dst, send_sem, recv_sem, device):
        copy = pltpu.make_async_remote_copy(
            src_ref=src,
            dst_ref=dst,
            send_sem=send_sem,
            recv_sem=recv_sem,
            device_id=device,
            device_id_type=MESH,
        )
        copy.start()
        return copy

    known, slots, present, mirror, folded, north_of = find_neighbours(n, w, slot_tile, neighbours)
    broadcast_taps(k49, kb)
    clear_margins(pad)
    clear_margins(gp)
    clear_rows(cells)
    cell = lax.broadcasted_iota(jnp.int32, (1, 384), 1)
    sub_row = jnp.where(cell >= 96, 1.0, 0.0) + jnp.where(cell >= 192, 1.0, 0.0)
    sub_row = sub_row + jnp.where(cell >= 288, 1.0, 0.0)
    first_row = ((known >> 5) * TS).astype(F32) + 0.5
    fetch[0].wait()

    def prep(g, carry):
        here = pl.ds(pl.multiple_of(g * 384, 128), 384)
        latitude = -80.0 + 160.0 * (sub_row + ((g * 4).astype(F32) + first_row)) / float(8 * TS)
        metric = cosine(latitude * (math.pi / 180.0))
        weight = wet[:, here] * metric
        wc[:, here] = weight
        rmet[:, here] = 1.0 / metric
        t = (feat[:, here].astype(F32) * weight).astype(BF16).astype(F32).T
        for r in range(4):
            row = pl.multiple_of((g * 4 + r + 3) * PITCH + 8, 8)
            pad[pl.ds(row, TS), :] = t[r * TS : (r + 1) * TS]
        return carry

    def prep_pair(g, carry):
        prep(2 * g - 1, carry)
        return prep(2 * g, carry)

    prep(jnp.int32(0), 0)
    prep(jnp.int32(23), 0)
    for q in range(3):
        here = pl.ds(q * TS, TS)
        south = pad[pl.ds((3 + q) * PITCH + 8, TS), :]
        north = pad[pl.ds((96 + q) * PITCH + 8, TS), :]
        strips[5, here, :] = north.astype(BF16)
        for k in range(3):
            strips[k, here, :] = jnp.where(north_of[k], south, north).astype(BF16)
    pl.semaphore_wait(barrier, len(greet))
    copies = []

    def send_strips(sources):
        for slot, source, device in peers:
            if source in sources:
                copies.append(
                    send(strips.at[source], got.at[slot], fsend.at[slot], frecv.at[slot], device)
                )

    send_strips((0, 1, 2, 5))
    lax.fori_loop(1, 12, prep_pair, 0)
    for q in range(3):
        here = pl.ds(q * TS, TS)
        strips[3, here, :] = pad[pl.ds(3 * PITCH + 8 + q, TS, stride=PITCH), :].astype(BF16)
        strips[4, here, :] = pad[pl.ds(3 * PITCH + 101 + q, TS, stride=PITCH), :].astype(BF16)
    send_strips((3, 4))

    taps_columns(pad, kb, cells, False, 0, 7)
    ones[...] = jnp.ones((C, CHUNK), BF16)
    column = lax.broadcasted_iota(jnp.int32, (C, C), 1)
    gain[...] = jnp.broadcast_to(gain_row[...], (C, C)).T
    scale[...] = jnp.broadcast_to(scale_row[...], (C, C)).T
    for k in range(4):
        here = slice(k * C, (k + 1) * C)
        w_in_t[here, 0:C] = (0.5 * w_in[:, here].astype(F32).T).astype(BF16)
        w_out_half[here, :] = (0.5 * w_out[here, :].astype(F32)).astype(BF16)
        rest = 0.5 * jnp.broadcast_to(bias_row[:, here], (C, C)).T
        parts = jnp.zeros((C, C), F32)
        for part in range(3):
            now = rest.astype(BF16).astype(F32)
            parts = jnp.where(column == part, now, parts)
            rest = rest - now
        w_in_t[here, C : 2 * C] = parts.astype(BF16)
        w_out_t[:, here] = w_out[here, :].astype(F32).T.astype(BF16)
    gwi[...] = jnp.zeros_like(gwi)
    gwo[...] = jnp.zeros_like(gwo)
    hw[...] = jnp.zeros_like(hw)
    he[...] = jnp.zeros_like(he)
    i0 = lax.broadcasted_iota(jnp.int32, (TS, TS), 0)
    i1 = lax.broadcasted_iota(jnp.int32, (TS, TS), 1)
    turn = (i0 + i1 == TS - 1).astype(BF16)
    for copy in copies:
        copy.wait()

    def chosen(direction, q):
        v = got[slots[direction], pl.ds(q * TS, TS), :].astype(F32)
        return jnp.where(present[direction], v, 0.0)

    for side, (mid, top, low), col in ((hw, (2, 4, 6), 5), (he, (3, 5, 7), 8)):
        for q in range(3):
            strip[0:TS, :] = chosen(low, q)
            strip[0:3, :] = strip[TS - 3 : TS, :]
            strip[3 : TS + 3, :] = chosen(mid, q)
            strip[112 : 112 + TS, :] = chosen(top, q)
            strip[TS + 3 : TS + 6, :] = strip[112:115, :]
            side[pl.ds(col + q, PADROWS, stride=16), :] = strip[0:PADROWS, :]
    for q in range(3):
        o = q * PITCH
        hs[o + 8 : o + 104, :] = chosen(1, q)
        hs[o : o + 8, :] = hw[q * 16 : q * 16 + 8, :]
        hs[o + 104 : o + 112, :] = he[q * 16 + 8 : q * 16 + 16, :]
        flipped = mm(turn, got[mirror, pl.ds((2 - q) * TS, TS), :])
        north = jnp.where(folded, flipped, chosen(0, q))
        hn[o + 8 : o + 104, :] = jnp.where(present[0], north, 0.0)
        r = (TS + 3 + q) * 16
        hn[o : o + 8, :] = hw[r : r + 8, :]
        hn[o + 104 : o + 112, :] = he[r + 8 : r + 16, :]
    pad[0:BAND, :] = hs[...]
    pad[99 * PITCH :, :] = hn[...]

    def rim(rows, pairs):
        def body(jb, carry):
            j0 = pl.multiple_of(jb * 8, 8)
            for d, terms in pairs:
                o = pl.ds(pl.multiple_of(d * TS + j0, 8), 8)
                total = cells[o, :]
                for a, r in terms:
                    part = None
                    for b in range(7):
                        v = kb[7 * a + b] * rows[pl.ds(r * PITCH + j0 + 5 + b, 8), :]
                        part = v if part is None else part + v
                    total = total + part
                cells[o, :] = total
            return carry

        lax.fori_loop(0, 12, body, 0)

    rim(hs, [(i, [(a, i + a) for a in range(3 - i)]) for i in range(3)])
    rim(hn, [(93 + i, [(a, i + a - 6) for a in range(6 - i, 7)]) for i in range(3)])

    def sides(g, carry):
        for e in range(4):
            i = g * 4 + e
            p = pl.multiple_of((i + 3) * PITCH, 8)
            r = pl.multiple_of((i + 3) * 16, 8)
            pad[pl.ds(p, 8), :] = hw[pl.ds(r, 8), :]
            pad[pl.ds(p + 104, 8), :] = he[pl.ds(r + 8, 8), :]
            for side, taps, shift, col in ((hw, (0, 1, 2), 5, 0), (he, (4, 5, 6), -3, 88)):
                parts = []
                for a in range(7):
                    row = i + a
                    inside = jnp.logical_and(row >= 3, row < TS + 3).astype(F32)
                    v = [
                        kb[7 * a + b] * side[pl.ds(row * 16 + b + shift, 8), :] for b in taps
                    ]
                    parts.append(((v[0] + v[1]) + v[2]) * inside)
                o = pl.ds(pl.multiple_of(i * TS + col, 8), 8)
                cells[o, :] = cells[o, :] + tree(parts)
        return carry

    lax.fori_loop(0, TS // 4, sides, 0)
    fetch[1].wait()

    def first_half(here):
        rm = rmet[:, here]
        conv = cells[here, :].T * rm
        centred = conv - jnp.mean(conv, axis=0, keepdims=True)
        inv_std = lax.rsqrt(jnp.mean(centred * centred, axis=0, keepdims=True) + EPS)
        normed = centred * inv_std
        normed_bf = (normed * wide2(gain[...])).astype(BF16)
        ms = wet[:, here] * wide2(scale[...])
        gm = (ms * cot[:, here].astype(F32)).astype(BF16)
        half = mm(w_in_t[...], jnp.concatenate([normed_bf, ones[...]], axis=0))
        half_grad = mm(w_out_half[...], gm)
        return rm, inv_std, normed, normed_bf, ms, gm, half, half_grad

    def second_half(here, rm, inv_std, normed, normed_bf, ms, gm, half, half_grad):
        sq = half * half
        t = jnp.tanh(half * (2.0 * GELU_COEF + (8.0 * GELU_COEF * CUBIC) * sq))
        one_more = 1.0 + t
        active = half * one_more
        slope = (2.0 * GELU_COEF) + (24.0 * GELU_COEF * CUBIC) * sq
        slope = one_more + active * (1.0 - t) * slope
        active_bf = active.astype(BF16)
        gh = (half_grad * slope).astype(BF16)
        mixed = mm(w_out_t[...], active_bf)
        updated[:, here] = (feat[:, here].astype(F32) + ms * mixed).astype(BF16)
        gn = mm(w_in[...], gh) * wide2(gain[...])
        gc = (inv_std * rm) * (
            gn
            - jnp.mean(gn, axis=0, keepdims=True)
            - normed * jnp.mean(gn * normed, axis=0, keepdims=True)
        )
        gwo[...] += nt(gm, active_bf)
        gwi[...] += nt(normed_bf, gh)
        return gc.T.astype(BF16).astype(F32)

    def mlp_block(step, carry):
        at = [
            pl.ds(pl.multiple_of(step * BLOCK + c * CHUNK, CHUNK), CHUNK)
            for c in range(BLOCK // CHUNK)
        ]
        ahead = first_half(at[0])
        for c in range(BLOCK // CHUNK):
            now = ahead
            if c + 1 < BLOCK // CHUNK:
                ahead = first_half(at[c + 1])
            gs = second_half(at[c], *now)
            for r in range(BLOCK // TS):
                low, high = max(c * CHUNK, r * TS), min((c + 1) * CHUNK, (r + 1) * TS)
                if low < high:
                    row = step * (BLOCK // TS) + r + 3
                    o = pl.multiple_of(row * PITCH + 8 + low - r * TS, 8)
                    gp[pl.ds(o, high - low), :] = gs[low - c * CHUNK : high - c * CHUNK]
        return carry

    lax.fori_loop(0, CELLS // BLOCK, mlp_block, 0)
    out_updated = pltpu.make_async_copy(updated, updated_hbm.at[0], up_sem)
    out_updated.start()

    for k in range(4):
        here = slice(k * C, (k + 1) * C)
        wmine[here, :] = (gwi[:, here] * GRAD_SCALE).astype(BF16)
        wmine[HID + k * C : HID + (k + 1) * C, :] = (gwo[:, here] * GRAD_SCALE).astype(BF16)
    stage1 = []
    for k, v in z_peers:
        src = wmine.at[pl.ds(pl.multiple_of(v * C, C), C)]
        stage1.append(send(src, part8.at[k], s1.at[k], r1.at[k], (n, x * 8 + v)))

    def frame_rows(jb, carry):
        j0 = pl.multiple_of(jb * 8, 8)
        for f, p in enumerate((0, 1, 2, 99, 100, 101)):
            parts = []
            for a in range(7):
                if 0 <= p - a < TS:
                    parts += [
                        kb[7 * a + b] * gp[pl.ds((p - a + 3) * PITCH + j0 + 8 - b, 8), :]
                        for b in range(7)
                    ]
            frame[f, pl.ds(j0, 8), :] = tree(parts)
        return carry

    lax.fori_loop(0, 13, frame_rows, 0)

    def frame_cols(g, carry):
        for e in range(4):
            p = g * 4 + e + 3
            for side, taps, q0 in ((fw, (0, 1, 2), 0), (fe, (4, 5, 6), 96)):
                parts = [
                    kb[7 * a + b] * gp[pl.ds((p - a + 3) * PITCH + q0 + 8 - b, 8), :]
                    for a in range(7)
                    for b in taps
                ]
                side[pl.ds(pl.multiple_of(p * 8, 8), 8), :] = tree(parts)
        return carry

    lax.fori_loop(0, TS // 4, frame_cols, 0)
    for f, p in enumerate((0, 1, 2, 99, 100, 101)):
        fw[p * 8 : p * 8 + 8, :] = frame[f, 0:8, :]
        fe[p * 8 : p * 8 + 8, :] = frame[f, 96:104, :]
    fw[PADROWS * 8 :, :] = jnp.zeros((80, C), F32)
    fe[PADROWS * 8 :, :] = jnp.zeros((80, C), F32)
    for q in range(3):
        here = pl.ds(q * PITCH, PITCH)
        back_strips[3, here, :] = fw[pl.ds(q, PITCH, stride=8), :].astype(BF16)
        back_strips[4, here, :] = fe[pl.ds(3 + q, PITCH, stride=8), :].astype(BF16)
        here = pl.ds(q * TS, TS)
        south = frame[q, 3 : 3 + TS, :]
        north = frame[3 + q, 3 : 3 + TS, :]
        back_strips[5, here, :] = north.astype(BF16)
        for k in range(3):
            back_strips[k, here, :] = jnp.where(north_of[k], south, north).astype(BF16)
    borders = []
    for slot, source, device in peers:
        size = BAND if source in (3, 4) else STRIP
        borders.append(
            send(
                back_strips.at[source, pl.ds(0, size)],
                back_got.at[slot, pl.ds(0, size)],
                bsend.at[slot],
                brecv.at[slot],
                device,
            )
        )

    kx[...] = jnp.zeros_like(kx)
    zero = jnp.zeros((8, C), F32)

    def tap_column(b, carry):
        def taps(it, acc):
            i0 = it * 4
            acc = list(acc)
            for jb in range(12):
                g = [gp[pl.ds((i0 + d + 3) * PITCH + 8 + 8 * jb, 8), :] for d in range(4)]
                v = [pad[pl.ds((i0 + r) * PITCH + 8 * jb + 5 + b, 8), :] for r in range(10)]
                for a in range(7):
                    near = (g[0] * v[a] + g[1] * v[a + 1]) + (g[2] * v[a + 2] + g[3] * v[a + 3])
                    acc[a] = acc[a] + near
            return tuple(acc)

        acc = lax.fori_loop(0, 24, taps, (zero,) * 7)
        for a in range(7):
            t = 7 * a + b
            kx[pl.ds(t, 1), :] = jnp.sum(acc[a], axis=0, keepdims=True)
        return carry

    lax.fori_loop(0, 7, tap_column, 0)

    kmine[...] = (kx[...] * GRAD_SCALE).astype(BF16)
    kz[z] = kmine[...]
    kstage = []
    for k, v in z_peers:
        kstage.append(send(kmine, kz.at[z], s6.at[k], r6.at[k], (n, x * 8 + v)))
    for copy in stage1:
        copy.wait()
    total = wmine[pl.ds(pl.multiple_of(z * C, C), C), :].astype(F32)
    for k in range(1, 8):
        total = total + part8[k].astype(F32)
    mine4[...] = total
    stage2 = []
    for k, v in x_peers:
        src = mine4.at[pl.ds(pl.multiple_of(v * 32, 32), 32)]
        stage2.append(send(src, part4.at[k], s2.at[k], r2.at[k], (n, v * 8 + z)))
    clear_rows(cells)
    taps_columns(gp, kb, cells, True, 0, 2)
    for copy in stage2 + kstage:
        copy.wait()
    total = mine4[pl.ds(pl.multiple_of(x * 32, 32), 32), :]
    for k in range(1, 4):
        total = total + part4[k]
    nodes[n] = total
    stage3 = []
    for k, v in n_peers:
        stage3.append(send(nodes.at[n], nodes.at[n], s3.at[k], r3.at[k], (v, w)))
    total = kz[0].astype(F32)
    for v in range(1, 8):
        total = total + kz[v].astype(F32)
    kq[x] = total
    kstage = []
    for k, v in x_peers:
        kstage.append(send(kq.at[x], kq.at[x], s7.at[k], r7.at[k], (n, v * 8 + z)))
    taps_columns(gp, kb, cells, True, 2, 4)
    for copy in stage3 + kstage:
        copy.wait()
    all4[x] = ((nodes[0] + nodes[1]) + (nodes[2] + nodes[3])).astype(BF16)
    stage4 = []
    for k, v in x_peers:
        stage4.append(send(all4.at[x], all4.at[x], s4.at[k], r4.at[k], (n, v * 8 + z)))
    kn[n] = (kq[0] + kq[1]) + (kq[2] + kq[3])
    kstage = []
    for k, v in n_peers:
        kstage.append(send(kn.at[n], kn.at[n], s8.at[k], r8.at[k], (v, w)))
    taps_columns(gp, kb, cells, True, 4, 6)
    for copy in stage4:
        copy.wait()
    for v in range(4):
        wall[z, v * 32 : (v + 1) * 32, :] = all4[v]
    stage5 = []
    for k, v in z_peers:
        stage5.append(send(wall.at[z], wall.at[z], s5.at[k], r5.at[k], (n, x * 8 + v)))
    taps_columns(gp, kb, cells, True, 6, 7)
    for copy in borders:
        copy.wait()

    cw[...] = jnp.zeros_like(cw)
    ce[...] = jnp.zeros_like(ce)

    def received(direction, start, size):
        v = back_got[slots[direction], pl.ds(start, size), :].astype(F32)
        return jnp.where(present[direction], v, 0.0)

    for side, (mid, north, south), col in ((cw, (2, 4, 6), 0), (ce, (3, 5, 7), 5)):
        for q in range(3):
            strip[0:PITCH, :] = received(mid, q * PITCH, PITCH)
            strip[PITCH : 2 * PITCH, :] = received(north, q * PITCH, PITCH)
            strip[2 * PITCH :, :] = received(south, q * PITCH, PITCH)
            strip[TS : TS + 3, :] += strip[PITCH : PITCH + 3, :]
            strip[3:6, :] += strip[2 * PITCH + TS + 3 : 2 * PITCH + TS + 6, :]
            side[pl.ds(col + q, TS, stride=8), :] = strip[3 : TS + 3, :]
    for q in range(3):
        cells[q * TS : (q + 1) * TS, :] += received(1, q * TS, TS)
        flipped = mm(turn, back_got[mirror, pl.ds((2 - q) * TS, TS), :])
        north = jnp.where(folded, flipped, received(0, q * TS, TS))
        cells[(93 + q) * TS : (94 + q) * TS, :] += jnp.where(present[0], north, 0.0)

    def finish(step, carry):
        for r in range(BLOCK // TS):
            i = step * (BLOCK // TS) + r
            o = pl.multiple_of(i * TS, 8)
            row = pl.multiple_of(i * 8, 8)
            cells[pl.ds(o, 8), :] += cw[pl.ds(row, 8), :]
            cells[pl.ds(o + 88, 8), :] += ce[pl.ds(row, 8), :]
        here = pl.ds(pl.multiple_of(step * BLOCK, BLOCK), BLOCK)
        whole = cot[:, here].astype(F32) + wc[:, here] * cells[here, :].T
        grad[:, here] = whole.astype(BF16)
        return carry

    lax.fori_loop(0, CELLS // BLOCK, finish, 0)
    out_grad = pltpu.make_async_copy(grad, grad_hbm.at[0], gr_sem)
    out_grad.start()
    for copy in kstage:
        copy.wait()
    ksum[...] = ((kn[0] + kn[1]) + (kn[2] + kn[3]))[0:49, :]
    for copy in stage5:
        copy.wait()
    for k in range(4):
        here = slice(k * C, (k + 1) * C)
        g_in[:, here] = wall[k].astype(F32)
        g_out[here, :] = wall[4 + k].astype(F32).T
    out_updated.wait()
    out_grad.wait()


def block_call(*args):
    vmem = pl.BlockSpec(memory_space=pltpu.VMEM)
    smem = pl.BlockSpec(memory_space=pltpu.SMEM)
    hbm = pl.BlockSpec(memory_space=pl.ANY)
    dma = pltpu.SemaphoreType.DMA
    shapes = [
        ((C, CELLS), BF16), ((C, CELLS), BF16), ((C, CELLS), BF16), ((C, CELLS), BF16),
        ((1, CELLS), F32), ((1, CELLS), F32),
        ((PADROWS * PITCH, C), F32), ((PADROWS * PITCH, C), F32), ((CELLS, C), F32),
        ((49, 8, C), F32), ((6, STRIP, C), BF16), ((15, STRIP, C), BF16),
        ((PADROWS * 16, C), F32), ((PADROWS * 16, C), F32), ((BAND, C), F32), ((BAND, C), F32),
        ((3 * PITCH, C), F32),
        ((C, C), F32), ((C, C), F32), ((C, CHUNK), BF16), ((HID, 2 * C), BF16), ((C, HID), BF16),
        ((HID, C), BF16),
        ((C, HID), F32), ((C, HID), F32),
        ((6, 104, C), F32), ((PITCH * 8, C), F32), ((PITCH * 8, C), F32),
        ((6, BAND, C), BF16), ((15, BAND, C), BF16), ((TS * 8, C), F32), ((TS * 8, C), F32),
        ((8 * C, C), BF16), ((8, C, C), BF16), ((C, C), F32), ((4, 32, C), F32),
        ((4, 32, C), F32), ((4, 32, C), BF16), ((8, C, C), BF16),
        ((64, C), F32), ((64, C), BF16), ((8, 64, C), BF16), ((4, 64, C), F32), ((4, 64, C), F32),
    ]
    sems = [dma((2,)), dma, dma, dma((15,)), dma((15,)), dma((15,)), dma((15,))]
    sems += [dma((8,)), dma((8,))] + [dma((4,))] * 6 + [dma((8,))] * 4 + [dma((4,))] * 4
    return pl.pallas_call(
        block_kernel,
        out_shape=(
            jax.ShapeDtypeStruct((1, C, CELLS), BF16),
            jax.ShapeDtypeStruct((1, C, CELLS), BF16),
            jax.ShapeDtypeStruct((C, HID), F32),
            jax.ShapeDtypeStruct((HID, C), F32),
            jax.ShapeDtypeStruct((49, C), F32),
        ),
        in_specs=[hbm, hbm, vmem, vmem, smem, smem] + [vmem] * 5,
        out_specs=(hbm, hbm, vmem, vmem, vmem),
        scratch_shapes=[pltpu.VMEM(shape, dtype) for shape, dtype in shapes] + sems,
        compiler_params=pltpu.CompilerParams(
            collective_id=0, has_side_effects=True, vmem_limit_bytes=VMEM_LIMIT
        ),
        name="block",
    )(*args)


def hand_over_kernel(*refs):
    sources, results, held = refs[:5], refs[5:10], refs[10:15]
    in_sem, out_sem = refs[15:]
    pieces = []
    for source, result, stage in zip(sources[:2], results[:2], held[:2]):
        for k in range(4):
            here = pl.ds(k * 32, 32)
            pieces.append((source.at[0, here], stage.at[here], result.at[0, here]))
    pieces += [(a, b, c) for a, b, c in zip(sources[2:], held[2:], results[2:])]
    loads = [pltpu.make_async_copy(a, b, in_sem.at[k]) for k, (a, b, _) in enumerate(pieces)]
    stores = [pltpu.make_async_copy(b, c, out_sem.at[k]) for k, (_, b, c) in enumerate(pieces)]
    for copy in loads:
        copy.start()
    for load, store in zip(loads, stores):
        load.wait()
        store.start()
    for copy in stores:
        copy.wait()


def hand_over(*arrays):
    hbm = pl.BlockSpec(memory_space=pl.ANY)
    held = [pltpu.VMEM((C, CELLS), BF16)] * 2
    held += [pltpu.VMEM(a.shape, a.dtype) for a in arrays[2:]]
    return pl.pallas_call(
        hand_over_kernel,
        out_shape=tuple(jax.ShapeDtypeStruct(a.shape, a.dtype) for a in arrays),
        in_specs=[hbm] * 5,
        out_specs=(hbm,) * 5,
        scratch_shapes=held + [pltpu.SemaphoreType.DMA((11,))] * 2,
        compiler_params=pltpu.CompilerParams(vmem_limit_bytes=VMEM_LIMIT),
        name="hand_over",
    )(*arrays)


def local(
    features,
    cotangent,
    wet_fraction,
    slot_tile,
    neighbours,
    kernel,
    norm_gain,
    weight_in,
    bias_in,
    weight_out,
    layer_scale,
):
    results = block_call(
        features,
        cotangent,
        wet_fraction,
        kernel,
        slot_tile,
        neighbours.T,
        norm_gain[None, :],
        weight_in,
        bias_in[None, :],
        weight_out,
        layer_scale[None, :],
    )
    return hand_over(*results)


def solution(mesh):
    shards = P(("node", "wide"), None, None)
    in_specs = (shards, shards, P(("node", "wide"), None)) + (P(),) * 8
    out_specs = (shards, shards, P(), P(), P())
    return jax.shard_map(local, mesh=mesh, in_specs=in_specs, out_specs=out_specs, check_vma=False)
```

```python
import math

import jax
import jax.numpy as jnp
from jax import lax
from jax.experimental import pallas as pl
from jax.experimental.pallas import tpu as pltpu
from jax.sharding import PartitionSpec as P

C = 128
HID = 512
TS = 96
CELLS = TS * TS
NODE = 4
WIDE = 32
PITCH = 112
PADROWS = TS + 6
STRIP = 3 * TS
BAND = 3 * PITCH
BLOCK = 2304
CHUNK = 256
EPS = 1e-06
GELU_COEF = 0.7978845608028654
CUBIC = 0.044715
GRAD_SCALE = 1.0 / math.sqrt(NODE * WIDE * CELLS)
MESH = pl.DeviceIdType.MESH
F32 = jnp.float32
BF16 = jnp.bfloat16
VMEM_LIMIT = 60 * 2**20


def border_peers(n, w):
    out = []
    for k in range(1, 4):
        out.append((k - 1, k - 1, (lax.rem(n + k, 4), w)))
    sides = ((3, 3, lax.rem(w + 31, 32)), (7, 4, lax.rem(w + 1, 32)), (11, 5, 31 - w))
    for base, source, column in sides:
        for k in range(4):
            out.append((base + k, source, (lax.rem(n + k, 4), column)))
    return out


def broadcast_taps(k49, kb):
    for t in range(49):
        kb[t] = jnp.broadcast_to(k49[t : t + 1, :], (8, C))


def taps_columns(src, kb, out, flip, low, high):
    def passes(columns):
        def body(it, carry):
            b0 = low + columns * (it // 12)
            i0 = lax.rem(it, 12) * 8
            taps = [
                [kb[48 - 7 * a - b0 - e] if flip else kb[7 * a + b0 + e] for a in range(7)]
                for e in range(columns)
            ]
            for jb in range(12):
                base = i0 * PITCH + 8 * jb + 5 + b0
                totals = [None] * 8
                for e in range(columns):
                    v = [src[pl.ds(base + e + r * PITCH, 8), :] for r in range(14)]
                    for d in range(8):
                        for a in range(7):
                            p = taps[e][a] * v[d + a]
                            totals[d] = p if totals[d] is None else totals[d] + p
                for d in range(8):
                    o = pl.ds(pl.multiple_of((i0 + d) * TS + 8 * jb, 8), 8)
                    out[o, :] = out[o, :] + totals[d]
            return carry

        return body

    if (high - low) % 2:
        lax.fori_loop(0, 12, passes(1), 0)
        low += 1
    if high > low:
        lax.fori_loop(0, (high - low) // 2 * 12, passes(2), 0)


def clear_rows(out):
    zero = jnp.zeros((TS, C), F32)

    def body(i, carry):
        out[pl.ds(pl.multiple_of(i * TS, 8), TS), :] = zero
        return carry

    lax.fori_loop(0, TS, body, 0)


def clear_margins(pad):
    zero8 = jnp.zeros((8, C), F32)
    zero_row = jnp.zeros((PITCH, C), F32)
    for r in (0, 1, 2, 99, 100, 101):
        pad[r * PITCH : (r + 1) * PITCH, :] = zero_row

    def body(i, carry):
        o = pl.multiple_of((i + 3) * PITCH, 8)
        pad[pl.ds(o, 8), :] = zero8
        pad[pl.ds(o + 104, 8), :] = zero8
        return carry

    lax.fori_loop(0, TS, body, 0)


def cosine(x):
    x2 = x * x
    total = jnp.full_like(x, 1.0 / math.factorial(16))
    for k in range(7, -1, -1):
        total = total * x2 + (-1.0) ** k / math.factorial(2 * k)
    return total


def nt(a, b):
    return lax.dot_general(a, b, (((1,), (1,)), ((), ())), preferred_element_type=F32)


def mm(a, b):
    return jnp.dot(a, b, preferred_element_type=F32)


def tree(parts):
    while len(parts) > 1:
        pairs = [parts[k] + parts[k + 1] for k in range(0, len(parts) - 1, 2)]
        parts = pairs + parts[len(pairs) * 2 :]
    return parts[0]


def wide2(column):
    return jnp.concatenate([column, column], axis=1)


def find_neighbours(n, w, slot_tile, neighbours):
    tile = slot_tile[n * WIDE + w]
    known = jnp.maximum(tile, 0)
    columns = {0: w, 3: lax.rem(w + 1, 32), 7: lax.rem(w + 31, 32), 11: 31 - w}
    held = {key: [slot_tile[k * WIDE + col] for k in range(4)] for key, col in columns.items()}
    bases = (0, 0, 7, 3, 7, 3, 7, 3)
    slots, present, targets = [], [], []

    def find(base, target):
        slot = jnp.int32(0)
        for k in range(4):
            away = lax.rem(n + 4 - k, 4)
            here = jnp.maximum(away - 1, 0) if base == 0 else base + away
            slot = jnp.where(held[base][k] == target, here, slot)
        return slot

    for d in range(8):
        near = jnp.where(tile >= 0, neighbours[d, known], -1)
        present.append(near >= 0)
        targets.append(jnp.maximum(near, 0) >> 1)
        slots.append(find(bases[d], targets[d]))
        if d == 0:
            flip = near & 1
    mirror = find(11, targets[0])
    north_of = []
    for k in range(1, 4):
        other = slot_tile[lax.rem(n + k, 4) * WIDE + w]
        north_of.append(present[1] & (other == targets[1]))
    return known, slots, present, mirror, present[0] & (flip == 1), north_of


def block_kernel(
    feat_hbm, cot_hbm, wet, k49, slot_tile, neighbours, gain_row, w_in, bias_row, w_out, scale_row,
    updated_hbm, grad_hbm, g_in, g_out, ksum,
    feat, cot, updated, grad, wc, rmet, pad, gp, cells, kb, strips, got, hw, he, hs, hn, strip,
    gain, scale, ones, w_in_t, w_out_t, w_out_half, gwi, gwo, frame, fw, fe, back_strips, back_got, cw, ce,
    wmine, part8, mine4, part4, nodes, all4, wall, kx, kmine, kz, kq, kn,
    in_sem, up_sem, gr_sem, fsend, frecv, bsend, brecv, s1, r1, s2, r2, s3, r3, s4, r4, s5, r5,
    s6, r6, s7, r7, s8, r8,
):
    n = lax.axis_index("node")
    w = lax.axis_index("wide")
    x = w // 8
    z = lax.rem(w, 8)
    peers = border_peers(n, w)
    z_peers = [(k, lax.rem(z + k, 8)) for k in range(1, 8)]
    x_peers = [(k, lax.rem(x + k, 4)) for k in range(1, 4)]
    n_peers = [(k, lax.rem(n + k, 4)) for k in range(1, 4)]
    greet = [device for _, _, device in peers]
    greet += [(n, x * 8 + v) for _, v in z_peers] + [(n, v * 8 + z) for _, v in x_peers]
    barrier = pltpu.get_barrier_semaphore()
    for device in greet:
        pl.semaphore_signal(barrier, inc=1, device_id=device, device_id_type=MESH)
    fetch = [
        pltpu.make_async_copy(feat_hbm.at[0], feat, in_sem.at[0]),
        pltpu.make_async_copy(cot_hbm.at[0], cot, in_sem.at[1]),
    ]
    for copy in fetch:
        copy.start()

    def send(src, dst, send_sem, recv_sem, device):
        copy = pltpu.make_async_remote_copy(
            src_ref=src,
            dst_ref=dst,
            send_sem=send_sem,
            recv_sem=recv_sem,
            device_id=device,
            device_id_type=MESH,
        )
        copy.start()
        return copy

    known, slots, present, mirror, folded, north_of = find_neighbours(n, w, slot_tile, neighbours)
    broadcast_taps(k49, kb)
    clear_margins(pad)
    clear_margins(gp)
    clear_rows(cells)
    cell = lax.broadcasted_iota(jnp.int32, (1, 384), 1)
    sub_row = jnp.where(cell >= 96, 1.0, 0.0) + jnp.where(cell >= 192, 1.0, 0.0)
    sub_row = sub_row + jnp.where(cell >= 288, 1.0, 0.0)
    first_row = ((known >> 5) * TS).astype(F32) + 0.5
    fetch[0].wait()

    def prep(g, carry):
        here = pl.ds(pl.multiple_of(g * 384, 128), 384)
        latitude = -80.0 + 160.0 * (sub_row + ((g * 4).astype(F32) + first_row)) / float(8 * TS)
        metric = cosine(latitude * (math.pi / 180.0))
        weight = wet[:, here] * metric
        wc[:, here] = weight
        rmet[:, here] = 1.0 / metric
        t = (feat[:, here].astype(F32) * weight).astype(BF16).astype(F32).T
        for r in range(4):
            row = pl.multiple_of((g * 4 + r + 3) * PITCH + 8, 8)
            pad[pl.ds(row, TS), :] = t[r * TS : (r + 1) * TS]
        return carry

    def prep_pair(g, carry):
        prep(2 * g - 1, carry)
        return prep(2 * g, carry)

    prep(jnp.int32(0), 0)
    prep(jnp.int32(23), 0)
    for q in range(3):
        here = pl.ds(q * TS, TS)
        south = pad[pl.ds((3 + q) * PITCH + 8, TS), :]
        north = pad[pl.ds((96 + q) * PITCH + 8, TS), :]
        strips[5, here, :] = north.astype(BF16)
        for k in range(3):
            strips[k, here, :] = jnp.where(north_of[k], south, north).astype(BF16)
    pl.semaphore_wait(barrier, len(greet))
    copies = []

    def send_strips(sources):
        for slot, source, device in peers:
            if source in sources:
                copies.append(
                    send(strips.at[source], got.at[slot], fsend.at[slot], frecv.at[slot], device)
                )

    send_strips((0, 1, 2, 5))
    lax.fori_loop(1, 12, prep_pair, 0)
    for q in range(3):
        here = pl.ds(q * TS, TS)
        strips[3, here, :] = pad[pl.ds(3 * PITCH + 8 + q, TS, stride=PITCH), :].astype(BF16)
        strips[4, here, :] = pad[pl.ds(3 * PITCH + 101 + q, TS, stride=PITCH), :].astype(BF16)
    send_strips((3, 4))

    taps_columns(pad, kb, cells, False, 0, 7)
    ones[...] = jnp.ones((C, CHUNK), BF16)
    column = lax.broadcasted_iota(jnp.int32, (C, C), 1)
    gain[...] = jnp.broadcast_to(gain_row[...], (C, C)).T
    scale[...] = jnp.broadcast_to(scale_row[...], (C, C)).T
    for k in range(4):
        here = slice(k * C, (k + 1) * C)
        w_in_t[here, 0:C] = (0.5 * w_in[:, here].astype(F32).T).astype(BF16)
        w_out_half[here, :] = (0.5 * w_out[here, :].astype(F32)).astype(BF16)
        rest = 0.5 * jnp.broadcast_to(bias_row[:, here], (C, C)).T
        parts = jnp.zeros((C, C), F32)
        for part in range(3):
            now = rest.astype(BF16).astype(F32)
            parts = jnp.where(column == part, now, parts)
            rest = rest - now
        w_in_t[here, C : 2 * C] = parts.astype(BF16)
        w_out_t[:, here] = w_out[here, :].astype(F32).T.astype(BF16)
    gwi[...] = jnp.zeros_like(gwi)
    gwo[...] = jnp.zeros_like(gwo)
    hw[...] = jnp.zeros_like(hw)
    he[...] = jnp.zeros_like(he)
    i0 = lax.broadcasted_iota(jnp.int32, (TS, TS), 0)
    i1 = lax.broadcasted_iota(jnp.int32, (TS, TS), 1)
    turn = (i0 + i1 == TS - 1).astype(BF16)
    for copy in copies:
        copy.wait()

    def chosen(direction, q):
        v = got[slots[direction], pl.ds(q * TS, TS), :].astype(F32)
        return jnp.where(present[direction], v, 0.0)

    for side, (mid, top, low), col in ((hw, (2, 4, 6), 5), (he, (3, 5, 7), 8)):
        for q in range(3):
            strip[0:TS, :] = chosen(low, q)
            strip[0:3, :] = strip[TS - 3 : TS, :]
            strip[3 : TS + 3, :] = chosen(mid, q)
            strip[112 : 112 + TS, :] = chosen(top, q)
            strip[TS + 3 : TS + 6, :] = strip[112:115, :]
            side[pl.ds(col + q, PADROWS, stride=16), :] = strip[0:PADROWS, :]
    for q in range(3):
        o = q * PITCH
        hs[o + 8 : o + 104, :] = chosen(1, q)
        hs[o : o + 8, :] = hw[q * 16 : q * 16 + 8, :]
        hs[o + 104 : o + 112, :] = he[q * 16 + 8 : q * 16 + 16, :]
        flipped = mm(turn, got[mirror, pl.ds((2 - q) * TS, TS), :])
        north = jnp.where(folded, flipped, chosen(0, q))
        hn[o + 8 : o + 104, :] = jnp.where(present[0], north, 0.0)
        r = (TS + 3 + q) * 16
        hn[o : o + 8, :] = hw[r : r + 8, :]
        hn[o + 104 : o + 112, :] = he[r + 8 : r + 16, :]
    pad[0:BAND, :] = hs[...]
    pad[99 * PITCH :, :] = hn[...]

    def rim(rows, pairs):
        def body(jb, carry):
            j0 = pl.multiple_of(jb * 8, 8)
            for d, terms in pairs:
                o = pl.ds(pl.multiple_of(d * TS + j0, 8), 8)
                total = cells[o, :]
                for a, r in terms:
                    part = None
                    for b in range(7):
                        v = kb[7 * a + b] * rows[pl.ds(r * PITCH + j0 + 5 + b, 8), :]
                        part = v if part is None else part + v
                    total = total + part
                cells[o, :] = total
            return carry

        lax.fori_loop(0, 12, body, 0)

    rim(hs, [(i, [(a, i + a) for a in range(3 - i)]) for i in range(3)])
    rim(hn, [(93 + i, [(a, i + a - 6) for a in range(6 - i, 7)]) for i in range(3)])

    def sides(g, carry):
        for e in range(4):
            i = g * 4 + e
            p = pl.multiple_of((i + 3) * PITCH, 8)
            r = pl.multiple_of((i + 3) * 16, 8)
            pad[pl.ds(p, 8), :] = hw[pl.ds(r, 8), :]
            pad[pl.ds(p + 104, 8), :] = he[pl.ds(r + 8, 8), :]
            for side, taps, shift, col in ((hw, (0, 1, 2), 5, 0), (he, (4, 5, 6), -3, 88)):
                parts = []
                for a in range(7):
                    row = i + a
                    inside = jnp.logical_and(row >= 3, row < TS + 3).astype(F32)
                    v = [
                        kb[7 * a + b] * side[pl.ds(row * 16 + b + shift, 8), :] for b in taps
                    ]
                    parts.append(((v[0] + v[1]) + v[2]) * inside)
                o = pl.ds(pl.multiple_of(i * TS + col, 8), 8)
                cells[o, :] = cells[o, :] + tree(parts)
        return carry

    lax.fori_loop(0, TS // 4, sides, 0)
    fetch[1].wait()

    def first_half(here):
        rm = rmet[:, here]
        conv = cells[here, :].T * rm
        centred = conv - jnp.mean(conv, axis=0, keepdims=True)
        inv_std = lax.rsqrt(jnp.mean(centred * centred, axis=0, keepdims=True) + EPS)
        normed = centred * inv_std
        normed_bf = (normed * wide2(gain[...])).astype(BF16)
        ms = wet[:, here] * wide2(scale[...])
        gm = (ms * cot[:, here].astype(F32)).astype(BF16)
        half = mm(w_in_t[...], jnp.concatenate([normed_bf, ones[...]], axis=0))
        half_grad = mm(w_out_half[...], gm)
        return rm, inv_std, normed, normed_bf, ms, gm, half, half_grad

    def second_half(here, rm, inv_std, normed, normed_bf, ms, gm, half, half_grad):
        sq = half * half
        t = jnp.tanh(half * (2.0 * GELU_COEF + (8.0 * GELU_COEF * CUBIC) * sq))
        one_more = 1.0 + t
        active = half * one_more
        slope = (2.0 * GELU_COEF) + (24.0 * GELU_COEF * CUBIC) * sq
        slope = one_more + active * (1.0 - t) * slope
        active_bf = active.astype(BF16)
        gh = (half_grad * slope).astype(BF16)
        mixed = mm(w_out_t[...], active_bf)
        updated[:, here] = (feat[:, here].astype(F32) + ms * mixed).astype(BF16)
        gn = mm(w_in[...], gh) * wide2(gain[...])
        gc = (inv_std * rm) * (
            gn
            - jnp.mean(gn, axis=0, keepdims=True)
            - normed * jnp.mean(gn * normed, axis=0, keepdims=True)
        )
        gwo[...] += nt(gm, active_bf)
        gwi[...] += nt(normed_bf, gh)
        return gc.T.astype(BF16).astype(F32)

    def mlp_block(step, carry):
        at = [
            pl.ds(pl.multiple_of(step * BLOCK + c * CHUNK, CHUNK), CHUNK)
            for c in range(BLOCK // CHUNK)
        ]
        ahead = first_half(at[0])
        for c in range(BLOCK // CHUNK):
            now = ahead
            if c + 1 < BLOCK // CHUNK:
                ahead = first_half(at[c + 1])
            gs = second_half(at[c], *now)
            for r in range(BLOCK // TS):
                low, high = max(c * CHUNK, r * TS), min((c + 1) * CHUNK, (r + 1) * TS)
                if low < high:
                    row = step * (BLOCK // TS) + r + 3
                    o = pl.multiple_of(row * PITCH + 8 + low - r * TS, 8)
                    gp[pl.ds(o, high - low), :] = gs[low - c * CHUNK : high - c * CHUNK]
        return carry

    lax.fori_loop(0, CELLS // BLOCK, mlp_block, 0)
    out_updated = pltpu.make_async_copy(updated, updated_hbm.at[0], up_sem)
    out_updated.start()

    for k in range(4):
        here = slice(k * C, (k + 1) * C)
        wmine[here, :] = (gwi[:, here] * GRAD_SCALE).astype(BF16)
        wmine[HID + k * C : HID + (k + 1) * C, :] = (gwo[:, here] * GRAD_SCALE).astype(BF16)
    stage1 = []
    for k, v in z_peers:
        src = wmine.at[pl.ds(pl.multiple_of(v * C, C), C)]
        stage1.append(send(src, part8.at[k], s1.at[k], r1.at[k], (n, x * 8 + v)))

    def frame_rows(jb, carry):
        j0 = pl.multiple_of(jb * 8, 8)
        for f, p in enumerate((0, 1, 2, 99, 100, 101)):
            parts = []
            for a in range(7):
                if 0 <= p - a < TS:
                    parts += [
                        kb[7 * a + b] * gp[pl.ds((p - a + 3) * PITCH + j0 + 8 - b, 8), :]
                        for b in range(7)
                    ]
            frame[f, pl.ds(j0, 8), :] = tree(parts)
        return carry

    lax.fori_loop(0, 13, frame_rows, 0)

    def frame_cols(g, carry):
        for e in range(4):
            p = g * 4 + e + 3
            for side, taps, q0 in ((fw, (0, 1, 2), 0), (fe, (4, 5, 6), 96)):
                parts = [
                    kb[7 * a + b] * gp[pl.ds((p - a + 3) * PITCH + q0 + 8 - b, 8), :]
                    for a in range(7)
                    for b in taps
                ]
                side[pl.ds(pl.multiple_of(p * 8, 8), 8), :] = tree(parts)
        return carry

    lax.fori_loop(0, TS // 4, frame_cols, 0)
    for f, p in enumerate((0, 1, 2, 99, 100, 101)):
        fw[p * 8 : p * 8 + 8, :] = frame[f, 0:8, :]
        fe[p * 8 : p * 8 + 8, :] = frame[f, 96:104, :]
    fw[PADROWS * 8 :, :] = jnp.zeros((80, C), F32)
    fe[PADROWS * 8 :, :] = jnp.zeros((80, C), F32)
    for q in range(3):
        here = pl.ds(q * PITCH, PITCH)
        back_strips[3, here, :] = fw[pl.ds(q, PITCH, stride=8), :].astype(BF16)
        back_strips[4, here, :] = fe[pl.ds(3 + q, PITCH, stride=8), :].astype(BF16)
        here = pl.ds(q * TS, TS)
        south = frame[q, 3 : 3 + TS, :]
        north = frame[3 + q, 3 : 3 + TS, :]
        back_strips[5, here, :] = north.astype(BF16)
        for k in range(3):
            back_strips[k, here, :] = jnp.where(north_of[k], south, north).astype(BF16)
    borders = []
    for slot, source, device in peers:
        size = BAND if source in (3, 4) else STRIP
        borders.append(
            send(
                back_strips.at[source, pl.ds(0, size)],
                back_got.at[slot, pl.ds(0, size)],
                bsend.at[slot],
                brecv.at[slot],
                device,
            )
        )

    kx[...] = jnp.zeros_like(kx)
    zero = jnp.zeros((8, C), F32)

    def tap_column(b, carry):
        def taps(it, acc):
            i0 = it * 4
            acc = list(acc)
            for jb in range(12):
                g = [gp[pl.ds((i0 + d + 3) * PITCH + 8 + 8 * jb, 8), :] for d in range(4)]
                v = [pad[pl.ds((i0 + r) * PITCH + 8 * jb + 5 + b, 8), :] for r in range(10)]
                for a in range(7):
                    near = (g[0] * v[a] + g[1] * v[a + 1]) + (g[2] * v[a + 2] + g[3] * v[a + 3])
                    acc[a] = acc[a] + near
            return tuple(acc)

        acc = lax.fori_loop(0, 24, taps, (zero,) * 7)
        for a in range(7):
            t = 7 * a + b
            kx[pl.ds(t, 1), :] = jnp.sum(acc[a], axis=0, keepdims=True)
        return carry

    lax.fori_loop(0, 7, tap_column, 0)

    kmine[...] = (kx[...] * GRAD_SCALE).astype(BF16)
    kz[z] = kmine[...]
    kstage = []
    for k, v in z_peers:
        kstage.append(send(kmine, kz.at[z], s6.at[k], r6.at[k], (n, x * 8 + v)))
    for copy in stage1:
        copy.wait()
    total = wmine[pl.ds(pl.multiple_of(z * C, C), C), :].astype(F32)
    for k in range(1, 8):
        total = total + part8[k].astype(F32)
    mine4[...] = total
    stage2 = []
    for k, v in x_peers:
        src = mine4.at[pl.ds(pl.multiple_of(v * 32, 32), 32)]
        stage2.append(send(src, part4.at[k], s2.at[k], r2.at[k], (n, v * 8 + z)))
    clear_rows(cells)
    taps_columns(gp, kb, cells, True, 0, 2)
    for copy in stage2 + kstage:
        copy.wait()
    total = mine4[pl.ds(pl.multiple_of(x * 32, 32), 32), :]
    for k in range(1, 4):
        total = total + part4[k]
    nodes[n] = total
    stage3 = []
    for k, v in n_peers:
        stage3.append(send(nodes.at[n], nodes.at[n], s3.at[k], r3.at[k], (v, w)))
    total = kz[0].astype(F32)
    for v in range(1, 8):
        total = total + kz[v].astype(F32)
    kq[x] = total
    kstage = []
    for k, v in x_peers:
        kstage.append(send(kq.at[x], kq.at[x], s7.at[k], r7.at[k], (n, v * 8 + z)))
    taps_columns(gp, kb, cells, True, 2, 4)
    for copy in stage3 + kstage:
        copy.wait()
    all4[x] = ((nodes[0] + nodes[1]) + (nodes[2] + nodes[3])).astype(BF16)
    stage4 = []
    for k, v in x_peers:
        stage4.append(send(all4.at[x], all4.at[x], s4.at[k], r4.at[k], (n, v * 8 + z)))
    kn[n] = (kq[0] + kq[1]) + (kq[2] + kq[3])
    kstage = []
    for k, v in n_peers:
        kstage.append(send(kn.at[n], kn.at[n], s8.at[k], r8.at[k], (v, w)))
    taps_columns(gp, kb, cells, True, 4, 6)
    for copy in stage4:
        copy.wait()
    for v in range(4):
        wall[z, v * 32 : (v + 1) * 32, :] = all4[v]
    stage5 = []
    for k, v in z_peers:
        stage5.append(send(wall.at[z], wall.at[z], s5.at[k], r5.at[k], (n, x * 8 + v)))
    taps_columns(gp, kb, cells, True, 6, 7)
    for copy in borders:
        copy.wait()

    cw[...] = jnp.zeros_like(cw)
    ce[...] = jnp.zeros_like(ce)

    def received(direction, start, size):
        v = back_got[slots[direction], pl.ds(start, size), :].astype(F32)
        return jnp.where(present[direction], v, 0.0)

    for side, (mid, north, south), col in ((cw, (2, 4, 6), 0), (ce, (3, 5, 7), 5)):
        for q in range(3):
            strip[0:PITCH, :] = received(mid, q * PITCH, PITCH)
            strip[PITCH : 2 * PITCH, :] = received(north, q * PITCH, PITCH)
            strip[2 * PITCH :, :] = received(south, q * PITCH, PITCH)
            strip[TS : TS + 3, :] += strip[PITCH : PITCH + 3, :]
            strip[3:6, :] += strip[2 * PITCH + TS + 3 : 2 * PITCH + TS + 6, :]
            side[pl.ds(col + q, TS, stride=8), :] = strip[3 : TS + 3, :]
    for q in range(3):
        cells[q * TS : (q + 1) * TS, :] += received(1, q * TS, TS)
        flipped = mm(turn, back_got[mirror, pl.ds((2 - q) * TS, TS), :])
        north = jnp.where(folded, flipped, received(0, q * TS, TS))
        cells[(93 + q) * TS : (94 + q) * TS, :] += jnp.where(present[0], north, 0.0)

    def finish(step, carry):
        for r in range(BLOCK // TS):
            i = step * (BLOCK // TS) + r
            o = pl.multiple_of(i * TS, 8)
            row = pl.multiple_of(i * 8, 8)
            cells[pl.ds(o, 8), :] += cw[pl.ds(row, 8), :]
            cells[pl.ds(o + 88, 8), :] += ce[pl.ds(row, 8), :]
        here = pl.ds(pl.multiple_of(step * BLOCK, BLOCK), BLOCK)
        whole = cot[:, here].astype(F32) + wc[:, here] * cells[here, :].T
        grad[:, here] = whole.astype(BF16)
        return carry

    lax.fori_loop(0, CELLS // BLOCK, finish, 0)
    out_grad = pltpu.make_async_copy(grad, grad_hbm.at[0], gr_sem)
    out_grad.start()
    for copy in kstage:
        copy.wait()
    ksum[...] = ((kn[0] + kn[1]) + (kn[2] + kn[3]))[0:56, :]
    for copy in stage5:
        copy.wait()
    for k in range(4):
        here = slice(k * C, (k + 1) * C)
        g_in[:, here] = wall[k].astype(F32)
        g_out[here, :] = wall[4 + k].astype(F32).T
    out_updated.wait()
    out_grad.wait()


def block_call(*args):
    vmem = pl.BlockSpec(memory_space=pltpu.VMEM)
    smem = pl.BlockSpec(memory_space=pltpu.SMEM)
    hbm = pl.BlockSpec(memory_space=pl.ANY)
    dma = pltpu.SemaphoreType.DMA
    shapes = [
        ((C, CELLS), BF16), ((C, CELLS), BF16), ((C, CELLS), BF16), ((C, CELLS), BF16),
        ((1, CELLS), F32), ((1, CELLS), F32),
        ((PADROWS * PITCH, C), F32), ((PADROWS * PITCH, C), F32), ((CELLS, C), F32),
        ((49, 8, C), F32), ((6, STRIP, C), BF16), ((15, STRIP, C), BF16),
        ((1680, C), F32), ((1680, C), F32), ((BAND, C), F32), ((BAND, C), F32),
        ((3 * PITCH, C), F32),
        ((C, C), F32), ((C, C), F32), ((C, CHUNK), BF16), ((HID, 2 * C), BF16), ((C, HID), BF16),
        ((HID, C), BF16),
        ((C, HID), F32), ((C, HID), F32),
        ((6, 104, C), F32), ((PITCH * 8, C), F32), ((PITCH * 8, C), F32),
        ((6, BAND, C), BF16), ((15, BAND, C), BF16), ((TS * 8, C), F32), ((TS * 8, C), F32),
        ((8 * C, C), BF16), ((8, C, C), BF16), ((C, C), F32), ((4, 32, C), F32),
        ((4, 32, C), F32), ((4, 32, C), BF16), ((8, C, C), BF16),
        ((64, C), F32), ((64, C), BF16), ((8, 64, C), BF16), ((4, 64, C), F32), ((4, 64, C), F32),
    ]
    sems = [dma((2,)), dma, dma, dma((15,)), dma((15,)), dma((15,)), dma((15,))]
    sems += [dma((8,)), dma((8,))] + [dma((4,))] * 6 + [dma((8,))] * 4 + [dma((4,))] * 4
    return pl.pallas_call(
        block_kernel,
        out_shape=(
            jax.ShapeDtypeStruct((1, C, CELLS), BF16),
            jax.ShapeDtypeStruct((1, C, CELLS), BF16),
            jax.ShapeDtypeStruct((C, HID), F32),
            jax.ShapeDtypeStruct((HID, C), F32),
            jax.ShapeDtypeStruct((56, C), F32),
        ),
        in_specs=[hbm, hbm, vmem, vmem, smem, smem] + [vmem] * 5,
        out_specs=(hbm, hbm, vmem, vmem, vmem),
        scratch_shapes=[pltpu.VMEM(shape, dtype) for shape, dtype in shapes] + sems,
        compiler_params=pltpu.CompilerParams(
            collective_id=0, has_side_effects=True, vmem_limit_bytes=VMEM_LIMIT
        ),
        name="block",
    )(*args)


def hand_over_kernel(*refs):
    sources, results, held = refs[:5], refs[5:10], refs[10:15]
    in_sem, out_sem = refs[15:]
    pieces = []
    for source, result, stage in zip(sources[:2], results[:2], held[:2]):
        for k in range(4):
            here = pl.ds(k * 32, 32)
            pieces.append((source.at[0, here], stage.at[here], result.at[0, here]))
    pieces += [(a, b, c) for a, b, c in zip(sources[2:], held[2:], results[2:])]
    loads = [pltpu.make_async_copy(a, b, in_sem.at[k]) for k, (a, b, _) in enumerate(pieces)]
    stores = [pltpu.make_async_copy(b, c, out_sem.at[k]) for k, (_, b, c) in enumerate(pieces)]
    for copy in loads:
        copy.start()
    for load, store in zip(loads, stores):
        load.wait()
        store.start()
    for copy in stores:
        copy.wait()


def hand_over(*arrays):
    hbm = pl.BlockSpec(memory_space=pl.ANY)
    held = [pltpu.VMEM((C, CELLS), BF16)] * 2
    held += [pltpu.VMEM(a.shape, a.dtype) for a in arrays[2:]]
    return pl.pallas_call(
        hand_over_kernel,
        out_shape=tuple(jax.ShapeDtypeStruct(a.shape, a.dtype) for a in arrays),
        in_specs=[hbm] * 5,
        out_specs=(hbm,) * 5,
        scratch_shapes=held + [pltpu.SemaphoreType.DMA((11,))] * 2,
        compiler_params=pltpu.CompilerParams(vmem_limit_bytes=VMEM_LIMIT),
        name="hand_over",
    )(*arrays)


def local(
    features,
    cotangent,
    wet_fraction,
    slot_tile,
    neighbours,
    kernel,
    norm_gain,
    weight_in,
    bias_in,
    weight_out,
    layer_scale,
):
    results = block_call(
        features,
        cotangent,
        wet_fraction,
        kernel,
        slot_tile,
        neighbours.T,
        norm_gain[None, :],
        weight_in,
        bias_in[None, :],
        weight_out,
        layer_scale[None, :],
    )
    results = hand_over(*results)
    return (*results[:4], results[4][:49])


def solution(mesh):
    shards = P(("node", "wide"), None, None)
    in_specs = (shards, shards, P(("node", "wide"), None)) + (P(),) * 8
    out_specs = (shards, shards, P(), P(), P())
    return jax.shard_map(local, mesh=mesh, in_specs=in_specs, out_specs=out_specs, check_vma=False)
```
